32 devices in a mesh: tensor: 4 (over z), dp: 4 (over x, core), pipe: 2 (over y).
Axes of the slice: x: 2, y: 2, z: 4, core: 2. Of those that a mesh axis runs over, the one named last changes fastest.
Arguments:
- mix: bfloat16 [2, 2, 4, 64, 4096], P('pipe', None, 'dp', None, 'tensor'), may hold values from -6 to 6
- hidden_in: bfloat16 [2, 4, 64, 8192], P(None, 'dp', 'tensor'), may hold values from -40 to 40
- cotangent: bfloat16 [2, 4, 64, 8192], P(None, 'dp', 'tensor'), may hold values from -6 to 6
- frozen_weight: bfloat16 [2, 4096, 8192], P('pipe', 'tensor', 'dp'), may hold values from -0.09375 to 0.09375
- right_factor: bfloat16 [2, 4, 1024, 128], P('pipe', 'tensor'), may hold values from -0.1875 to 0.1875
- left_factor: bfloat16 [2, 4, 128, 2048], P('pipe', 'tensor'), may hold values from -0.5 to 0.5
- norm_gain: bfloat16 [8192], replicated, may hold values from 0.25 to 1.75
Outputs:
- section_out: bfloat16 [2, 2, 4, 64, 8192], P('pipe', None, 'dp', 'tensor')
- grad_mix: bfloat16 [2, 2, 4, 64, 4096], P('pipe', None, 'dp', None, 'tensor')
- grad_right: float32 [2, 4, 1024, 128], P('pipe', 'tensor')
- grad_left: float32 [2, 4, 128, 2048], P('pipe', 'tensor')
The draws below stay inside these ranges and needn't reach their ends.
All inputs are finite; a program needn't handle non-finite values.
Results may differ from the reference program's by a relative error of at most 0.0054.
Values may be sent and summed in bfloat16 or wider, within the bound.
No kernel may reach another device: no remote copies, remote signals or barrier semaphores. Data moves between devices by JAX's collectives and lax.ppermute only.
A program may use at most 128 MiB of HBM per device.

```python
import jax
import jax.numpy as jnp
from jax import lax

D = 8192
SUB = 32
MB = 2
MTOK = 64
A = 4096
NB = 4
RB = 128
GROUPS = 4
SECTIONS = 2


def draw_hidden_in(key, part):
    key = jax.random.fold_in(key, 11)
    keys = jax.random.split(key, 3)
    shape = (MB, GROUPS, MTOK, D)
    base = jax.random.truncated_normal(keys[0], -4.0, 4.0, shape, jnp.float32)
    column_scale = jnp.exp(jax.random.uniform(keys[1], (D,), jnp.float32, -1.15, 1.15))
    row_scale = jnp.exp(jax.random.uniform(keys[2], (MB, GROUPS, MTOK, 1), jnp.float32, -1.15, 1.15))
    return (base * column_scale * row_scale).astype(jnp.bfloat16)


def block_levels(key, shape, shards, least, top_value):
    level, own = 1.0, jax.random.fold_in(key, 6)
    for dim, shards_of in shards:
        draws = jnp.exp(jax.random.uniform(jax.random.fold_in(own, dim), (shards_of,), jnp.float32, least / len(shards), top_value / len(shards)))
        level = level * jnp.repeat(draws, shape[dim] // shards_of).reshape([-1 if axis == dim else 1 for axis in range(len(shape))])
    return level


def scatter_about(rng, extent, spread, bound, cuts=(), held_as=jnp.bfloat16):
    level = block_levels(rng, extent, cuts, -0.22, 0.18) if cuts else 1.0
    values = jax.random.normal(rng, extent, jnp.float32) * spread * level
    return jnp.minimum(jnp.maximum(values, -bound), bound).astype(held_as)


def setup_inputs(seed: int = 0) -> dict:
    streams_of = jax.random.split(jax.random.key(seed), 8)
    return {
        "mix": scatter_about(streams_of[0], (SECTIONS, MB, GROUPS, MTOK, A), 1.0, 6.0, ((0, 2), (2, 4), (4, 4))),
        "hidden_in": draw_hidden_in(jax.random.fold_in(streams_of[7], 71), 0),
        "cotangent": scatter_about(streams_of[2], (MB, GROUPS, MTOK, D), 1.0, 6.0, ((1, 4), (2, 4))),
        "frozen_weight": scatter_about(streams_of[3], (SECTIONS, A, D), A ** -0.5, 0.09375, ((0, 2), (1, 4), (2, 4))),
        "right_factor": scatter_about(streams_of[4], (SECTIONS, NB, A // NB, RB), (A // NB) ** -0.5, 0.1875, ((0, 2), (1, 4))),
        "left_factor": scatter_about(streams_of[5], (SECTIONS, NB, RB, D // NB), RB ** -0.5, 0.5, ((0, 2), (1, 4))),
        "norm_gain": jnp.clip(1.0 + 0.15 * jax.random.normal(streams_of[6], (D,), jnp.float32), 0.25, 1.75).astype(jnp.bfloat16),
    }


def forward_section(hidden, mix_rows, weight, right, left):
    rows = mix_rows.shape[0]
    blocks = mix_rows.reshape(rows, NB, A // NB).astype(jnp.float32)
    inner = jnp.einsum('tip,ipr->tir', blocks, right.astype(jnp.float32)).astype(jnp.bfloat16)
    permuted = inner.reshape(rows, NB, NB, SUB).transpose(0, 2, 1, 3).reshape(rows, NB, RB)
    adapter = jnp.einsum('tkr,krd->tkd', permuted.astype(jnp.float32), left.astype(jnp.float32)).reshape(rows, D)
    frozen = jnp.dot(mix_rows, weight, preferred_element_type=jnp.float32)
    result = (hidden.astype(jnp.float32) + frozen + adapter).astype(jnp.bfloat16)
    return (permuted, result)

def reference(mix, hidden_in, cotangent, frozen_weight, right_factor, left_factor, norm_gain):
    rows = MB * GROUPS * MTOK
    hidden = hidden_in.reshape(rows, D)
    outputs = []
    saved = []
    for section in range(SECTIONS):
        permuted, hidden = forward_section(hidden, mix[section].reshape(rows, A), frozen_weight[section], right_factor[section], left_factor[section])
        outputs.append(hidden)
        saved.append(permuted)
    final = hidden.astype(jnp.float32)
    scale = jax.lax.rsqrt(lax.optimization_barrier(jnp.mean(final * final, axis=-1, keepdims=True)) + 1e-05)
    normed = final * scale
    upstream = cotangent.reshape(rows, D).astype(jnp.float32) * norm_gain.astype(jnp.float32)
    grad_top = (scale * (upstream - normed * lax.optimization_barrier(jnp.mean(upstream * normed, axis=-1, keepdims=True)))).astype(jnp.bfloat16)
    top_blocks = grad_top.reshape(rows, NB, D // NB).astype(jnp.float32)
    mix_grads = []
    right_grads = []
    left_grads = []
    for section in range(SECTIONS):
        left = left_factor[section].astype(jnp.float32)
        right = right_factor[section].astype(jnp.float32)
        grad_permuted = jnp.einsum('tkd,krd->tkr', top_blocks, left).astype(jnp.bfloat16)
        grad_inner = grad_permuted.reshape(rows, NB, NB, SUB).transpose(0, 2, 1, 3).reshape(rows, NB, RB).astype(jnp.float32)
        back = jnp.dot(grad_top, frozen_weight[section].T, preferred_element_type=jnp.float32)
        back = back + jnp.einsum('tir,ipr->tip', grad_inner, right).reshape(rows, A)
        mix_grads.append(back.astype(jnp.bfloat16).reshape(MB, GROUPS, MTOK, A))
        blocks = mix[section].reshape(rows, NB, A // NB).astype(jnp.float32)
        right_grads.append(jnp.einsum('tip,tir->ipr', blocks, grad_inner))
        left_grads.append(jnp.einsum('tkr,tkd->krd', saved[section].astype(jnp.float32), top_blocks))
    section_out = jnp.stack(outputs).reshape(SECTIONS, MB, GROUPS, MTOK, D)
    return (section_out, jnp.stack(mix_grads), jnp.stack(right_grads), jnp.stack(left_grads))
```

```python
import jax
import jax.numpy as jnp
from jax import lax
from jax.sharding import PartitionSpec as P

F32 = jnp.float32
BF16 = jnp.bfloat16


def dot(left_side, right_side, left_dim, right_dim):
    return lax.dot_general(
        left_side,
        right_side,
        (((left_dim,), (right_dim,)), ((), ())),
        preferred_element_type=F32,
    )


def pick(value, index):
    return lax.dynamic_index_in_dim(value, index, 0, keepdims=False)


def columns(value, start, size):
    return lax.dynamic_slice_in_dim(value, start, size, value.ndim - 1)


def on_device(mix, hidden_in, cotangent, frozen_weight, right_factor, left_factor, norm_gain):
    blocks = lax.axis_size("tensor")
    parts = lax.axis_size("dp")
    sections = lax.axis_size("pipe")
    t = lax.axis_index("tensor")
    d = lax.axis_index("dp")
    section = lax.axis_index("pipe")
    outers = parts // 2
    outer = d // 2
    core = d % 2

    def to_core(value):
        return lax.ppermute(value, "dp", [(i, i ^ 1) for i in range(parts)])

    def to_outer(value, step):
        pairs = [(i, (i + 2 * step) % parts) for i in range(parts)]
        return lax.ppermute(value, "dp", pairs)

    mixes = mix[0, :, 0]
    micro, tokens, head_cols = mixes.shape
    own_rows = tokens // blocks
    weight = frozen_weight[0]
    right = right_factor[0, 0]
    left = left_factor[0, 0]
    rank, block_cols = left.shape
    sub = rank // blocks
    width = weight.shape[1]
    features = width * parts
    rows = outers * own_rows
    all_rows = blocks * rows
    per_block = parts // blocks
    slots = (d, d ^ 1)

    def block_of(part):
        return part // per_block

    own = mixes.reshape(micro, blocks, 1, own_rows, head_cols)
    taken = [
        jnp.concatenate(
            [own[m]] + [to_outer(own[m], step) for step in range(1, outers)], axis=1
        ).reshape(all_rows, head_cols)
        for m in range(micro)
    ]
    weights = (weight, to_core(weight))
    pieces = lax.all_to_all(
        left.reshape(blocks, sub, block_cols), "tensor", split_axis=0, concat_axis=0, tiled=True
    )
    left_slots = [
        columns(pick(pieces, block_of(part)), (part % per_block) * width, width) for part in slots
    ]

    def by_column(step):
        target = (outer + step) % outers
        cuts = [2 * target + core, 2 * target + (1 - core)]
        return jnp.stack(
            [
                jnp.stack([columns(value[:, 0], part * width, width) for part in cuts])
                for value in (hidden_in, cotangent)
            ]
        )

    entering = jnp.concatenate(
        [by_column(0)] + [to_outer(by_column(step), step) for step in range(1, outers)], axis=3
    )
    gains = jnp.stack([columns(norm_gain, part * width, width) for part in slots]).astype(F32)

    inners = [dot(taken[m], right, 1, 0).astype(BF16) for m in range(micro)]
    inner_cols = [
        [columns(inners[m], block_of(part) * sub, sub) for part in slots] for m in range(micro)
    ]
    partial = [
        jnp.stack(
            [
                (
                    dot(taken[m], weights[slot], 1, 0)
                    + dot(inner_cols[m][slot], left_slots[slot], 1, 0)
                ).astype(BF16)
                for slot in range(2)
            ]
        ).reshape(2, blocks, rows, width)
        for m in range(micro)
    ]

    def shard(m, index):
        return lax.dynamic_index_in_dim(
            partial[m], jnp.clip(index, 0, blocks - 1), 1, keepdims=False
        ).astype(F32)

    zero = jnp.zeros((2, rows, width), BF16)
    going_up = [zero] * micro
    going_down = [zero] * micro
    for step in range(1, blocks):
        up = [(i, i + 1) for i in range(min(step, blocks - 1))]
        down = [(blocks - 1 - i, blocks - 2 - i) for i in range(min(step, blocks - 1))]
        for m in range(micro):
            send_up = (shard(m, blocks - step + t) + going_up[m].astype(F32)).astype(BF16)
            send_down = (shard(m, t + step - blocks) + going_down[m].astype(F32)).astype(BF16)
            going_up[m] = lax.ppermute(send_up, "tensor", up)
            going_down[m] = lax.ppermute(send_down, "tensor", down)

    grads = []
    leaving = []
    for m in range(micro):
        update = shard(m, t) + going_up[m].astype(F32) + going_down[m].astype(F32)
        sent = update.astype(BF16)
        updates = [update] + [
            lax.ppermute(
                sent, "pipe", [(i, (i + step) % sections) for i in range(sections)]
            ).astype(F32)
            for step in range(1, sections)
        ]
        state = entering[0, :, m]
        kept = state
        for s in range(sections):
            add = updates[0]
            for step in range(1, sections):
                add = jnp.where((section - step) % sections == s, updates[step], add)
            state = (state.astype(F32) + add).astype(BF16)
            kept = jnp.where(section == s, state, kept)
        leaving.append(kept)
        final = state.astype(F32)
        upstream = entering[1, :, m].astype(F32) * gains[:, None, :]
        sums = jnp.stack(
            [jnp.sum(final * final, axis=(0, 2)), jnp.sum(upstream * final, axis=(0, 2))]
        ).reshape(2, outers, own_rows)
        total = sums
        for step in range(1, outers):
            total = total + jnp.roll(to_outer(sums, step), step, axis=1)
        total = total.reshape(2, rows) / features
        scale = lax.rsqrt(total[0] + 1e-05)
        shrink = scale * scale * total[1]
        grads.append(
            (scale[None, :, None] * (upstream - final * shrink[None, :, None])).astype(BF16)
        )

    outs = []
    for m in range(micro):
        pieces_out = [leaving[m].reshape(2, outers, own_rows, width)[:, 0]]
        source = [outer]
        for step in range(1, outers):
            pieces_out.append(
                to_outer(leaving[m].reshape(2, outers, own_rows, width)[:, step], outers - step)
            )
            source.append((outer + step) % outers)
        row = jnp.zeros((own_rows, features), BF16)
        for piece, at in zip(pieces_out, source):
            row = lax.dynamic_update_slice_in_dim(row, piece[0], (2 * at + core) * width, 1)
            row = lax.dynamic_update_slice_in_dim(row, piece[1], (2 * at + 1 - core) * width, 1)
        outs.append(row)
    section_out = jnp.stack(outs).reshape(1, micro, 1, own_rows, features)

    full = []
    for m in range(micro):
        buffer = jnp.zeros((2, blocks, rows, width), BF16)
        buffer = lax.dynamic_update_slice_in_dim(buffer, grads[m][:, None], t, 1)
        ups, downs = [grads[m]], [grads[m]]
        for step in range(1, blocks):
            ups.append(
                lax.ppermute(ups[-1], "tensor", [(i, i + 1) for i in range(step - 1, blocks - 1)])
            )
            downs.append(
                lax.ppermute(
                    downs[-1], "tensor", [(i + 1, i) for i in range(0, blocks - step)]
                )
            )
        for step in range(1, blocks):
            value = jnp.where(t >= step, ups[step], downs[blocks - step])
            buffer = lax.dynamic_update_slice_in_dim(
                buffer, value[:, None], (t - step) % blocks, 1
            )
        full.append(buffer.reshape(2, all_rows, width))

    inner_stack = jnp.concatenate(inners, axis=0)
    permuted = lax.all_to_all(
        inner_stack.T.reshape(blocks, sub, micro * all_rows),
        "tensor",
        split_axis=0,
        concat_axis=0,
        tiled=True,
    ).reshape(rank, micro * all_rows)

    holder = (t * per_block) // 2
    mix_grads = []
    grad_right = jnp.zeros((head_cols, rank), F32)
    left_sum = jnp.zeros((rank, block_cols), F32)
    for m in range(micro):
        inner_grads = [dot(full[m][slot], left_slots[slot], 1, 1) for slot in range(2)]
        if per_block == 1:
            mine = jnp.where(
                core == 0,
                jnp.concatenate(inner_grads, axis=1),
                jnp.concatenate(inner_grads[::-1], axis=1),
            ).astype(BF16)
        else:
            mine = (inner_grads[0] + inner_grads[1]).astype(BF16)
        per_outer = mine.shape[1]
        partial_mix = (
            dot(full[m][0], weights[0], 1, 1)
            + dot(full[m][1], weights[1], 1, 1)
            + dot(mine, columns(right, outer * per_outer, per_outer), 1, 1)
        ).reshape(blocks, outers, own_rows, head_cols)
        summed = partial_mix[:, 0]
        for step in range(1, outers):
            summed = summed + to_outer(
                partial_mix[:, step].astype(BF16), outers - step
            ).astype(F32)
        mix_grads.append(summed.astype(BF16).reshape(tokens, head_cols))

        inner_full = jnp.zeros((blocks, outers, own_rows, rank), BF16)
        mine_rows = mine.reshape(blocks, outers, own_rows, per_outer)
        for step in range(outers):
            arrived = to_outer(mine_rows, step) if step else mine_rows
            ordered = jnp.zeros_like(arrived)
            for s in range(outers):
                ordered = lax.dynamic_update_slice_in_dim(
                    ordered, arrived[:, s : s + 1], (outer - step - s) % outers, 1
                )
            inner_full = lax.dynamic_update_slice_in_dim(
                inner_full, ordered, ((outer - step) % outers) * per_outer, 3
            )
        mix_rows = taken[m].reshape(blocks, outers, own_rows, head_cols)
        ordered_mix = jnp.zeros_like(mix_rows)
        for s in range(outers):
            ordered_mix = lax.dynamic_update_slice_in_dim(
                ordered_mix, mix_rows[:, s : s + 1], (outer - s) % outers, 1
            )
        grad_right = grad_right + dot(
            ordered_mix.reshape(all_rows, head_cols), inner_full.reshape(all_rows, rank), 0, 0
        )

        if per_block == 1:
            cols = pick(full[m], jnp.where(t % 2 == core, 0, 1))
        else:
            cols = jnp.where(
                core == 0,
                jnp.concatenate([full[m][0], full[m][1]], axis=1),
                jnp.concatenate([full[m][1], full[m][0]], axis=1),
            )
        left_sum = left_sum + dot(
            permuted[:, m * all_rows : (m + 1) * all_rows], cols, 1, 0
        )

    grad_right = grad_right + to_core(grad_right)

    half = block_cols // 2
    mine = columns(left_sum, core * half, half)
    other = to_core(columns(left_sum, (1 - core) * half, half))
    half_sum = (mine + other).astype(BF16)
    best = half_sum
    for step in range(1, outers):
        pairs = []
        for i in range(blocks):
            for c in range(2):
                at = (i * per_block) // 2
                pairs.append(
                    (i * parts + 2 * at + c, i * parts + 2 * ((at + step) % outers) + c)
                )
        arrived = lax.ppermute(half_sum, ("tensor", "dp"), pairs)
        best = jnp.where((outer - holder) % outers == step, arrived, best)
    there = to_core(best)
    grad_left = jnp.where(
        core == 0,
        jnp.concatenate([best, there], axis=1),
        jnp.concatenate([there, best], axis=1),
    ).astype(F32)

    grad_mix = jnp.stack(mix_grads).reshape(1, micro, 1, tokens, head_cols)
    return (
        section_out,
        grad_mix,
        grad_right.reshape(1, 1, head_cols, rank),
        grad_left.reshape(1, 1, rank, block_cols),
    )


def solution(mesh):
    return jax.shard_map(
        on_device,
        mesh=mesh,
        in_specs=(
            P("pipe", None, "dp", None, "tensor"),
            P(None, "dp", "tensor", None),
            P(None, "dp", "tensor", None),
            P("pipe", "tensor", "dp"),
            P("pipe", "tensor", None, None),
            P("pipe", "tensor", None, None),
            P(),
        ),
        out_specs=(
            P("pipe", None, "dp", "tensor", None),
            P("pipe", None, "dp", None, "tensor"),
            P("pipe", "tensor", None, None),
            P("pipe", "tensor", None, None),
        ),
        check_vma=False,
    )
```

```python
import jax
import jax.numpy as jnp
from jax import lax
from jax.sharding import PartitionSpec as P

F32 = jnp.float32
BF16 = jnp.bfloat16


def dot(left_side, right_side, left_dim, right_dim):
    return lax.dot_general(
        left_side,
        right_side,
        (((left_dim,), (right_dim,)), ((), ())),
        preferred_element_type=F32,
    )


def pick(value, index, dim=0):
    return lax.dynamic_index_in_dim(value, index, dim, keepdims=False)


def columns(value, start, size):
    return lax.dynamic_slice_in_dim(value, start, size, value.ndim - 1)


def after(value, *others):
    return lax.optimization_barrier((value, *others))[0]


def on_device(mix, hidden_in, cotangent, frozen_weight, right_factor, left_factor, norm_gain):
    blocks = lax.axis_size("tensor")
    parts = lax.axis_size("dp")
    sections = lax.axis_size("pipe")
    t = lax.axis_index("tensor")
    d = lax.axis_index("dp")
    section = lax.axis_index("pipe")
    outers = parts // 2
    outer = d // 2
    core = d % 2

    def to_core(value):
        return lax.ppermute(value, "dp", [(i, i ^ 1) for i in range(parts)])

    def to_outer(value, step):
        return lax.ppermute(value, "dp", [(i, (i + 2 * step) % parts) for i in range(parts)])

    def to_block(value, step):
        return lax.ppermute(value, "tensor", [(i, (i + step) % blocks) for i in range(blocks)])

    def of_cores(value):
        return jnp.where(core == 0, value, value[::-1])

    mixes = mix[0, :, 0]
    micro, tokens, head_cols = mixes.shape
    own_rows = tokens // blocks
    weight = frozen_weight[0]
    right = right_factor[0, 0]
    left = left_factor[0, 0]
    rank, block_cols = left.shape
    sub = rank // blocks
    width = weight.shape[1]
    features = width * parts
    rows = outers * own_rows
    all_rows = blocks * rows
    per_block = parts // blocks
    slots = (d, d ^ 1)

    def block_of(part):
        return part // per_block

    weights = (weight, to_core(weight))
    own = mixes.reshape(micro, blocks, 1, own_rows, head_cols)
    taken = [
        jnp.concatenate(
            [own[m]] + [to_outer(own[m], step) for step in range(1, outers)], axis=1
        ).reshape(all_rows, head_cols)
        for m in range(micro)
    ]
    own_inner = dot(right, mixes.reshape(micro * tokens, head_cols), 0, 1).astype(BF16)
    pieces = lax.all_to_all(
        jnp.concatenate(
            [
                left.reshape(blocks, sub, block_cols),
                own_inner.reshape(blocks, sub, micro * tokens),
            ],
            axis=2,
        ),
        "tensor",
        split_axis=0,
        concat_axis=0,
        tiled=True,
    )
    left_slots = [
        columns(pick(pieces, block_of(part)), (part % per_block) * width, width) for part in slots
    ]
    right_slots = [columns(right, block_of(part) * sub, sub) for part in slots]
    own_permuted = pieces[:, :, block_cols:].reshape(rank, micro * tokens)
    own_permuted = after(own_permuted, *taken)
    permuted = [own_permuted] + [to_outer(own_permuted, step) for step in range(1, outers)]

    inners = [dot(taken[m], right, 1, 0).astype(BF16) for m in range(micro)]
    partial = [
        jnp.stack(
            [
                (
                    dot(taken[m], weights[slot], 1, 0)
                    + dot(
                        columns(inners[m], block_of(part) * sub, sub), left_slots[slot], 1, 0
                    )
                ).astype(BF16)
                for slot, part in enumerate(slots)
            ]
        ).reshape(2, blocks, rows, width)
        for m in range(micro)
    ]

    def shard(m, index):
        return pick(partial[m], index, 1)

    updates_here = []
    arrived_last = None
    for m in range(micro):
        total = shard(m, t).astype(F32)
        if blocks != 4:
            for step in range(1, blocks):
                total = total + to_block(shard(m, (t + step) % blocks), step).astype(F32)
            updates_here.append(total)
            continue
        far = shard(m, jnp.where(t < 2, 3, 0))
        if arrived_last is not None:
            far = after(far, arrived_last)
        passed = lax.ppermute(far, "tensor", [(0, 1), (3, 2)])
        mid = lax.ppermute(
            after(shard(m, jnp.where(t < 2, 2, 1)), far), "tensor", [(1, 2), (2, 1)]
        )
        beside = lax.ppermute(after(shard(m, t ^ 1), far), "tensor", [(i, i ^ 1) for i in range(4)])
        middle = (t == 1) | (t == 2)
        two_away = jnp.where(
            middle, (far.astype(F32) + passed.astype(F32)).astype(BF16), shard(m, t ^ 2)
        )
        arrived_last = two_away
        crossed = to_block(two_away, 2)
        updates_here.append(
            total + beside.astype(F32) + mid.astype(F32) + crossed.astype(F32)
        )

    hidden_late = after(hidden_in, *taken)

    def by_column(step):
        target = (outer + step) % outers
        cuts = [2 * target + core, 2 * target + (1 - core)]
        return jnp.stack(
            [
                jnp.stack([columns(value[:, 0], part * width, width) for part in cuts])
                for value in (hidden_late, cotangent)
            ]
        )

    entering = jnp.concatenate(
        [by_column(0)] + [to_outer(by_column(step), step) for step in range(1, outers)], axis=3
    )
    gains = jnp.stack([columns(norm_gain, part * width, width) for part in slots]).astype(F32)

    grads = []
    leaving = []
    for m in range(micro):
        sent = updates_here[m].astype(BF16)
        updates = [updates_here[m]] + [
            lax.ppermute(
                sent, "pipe", [(i, (i + step) % sections) for i in range(sections)]
            ).astype(F32)
            for step in range(1, sections)
        ]
        state = entering[0, :, m]
        kept = state
        for s in range(sections):
            add = updates[0]
            for step in range(1, sections):
                add = jnp.where((section - step) % sections == s, updates[step], add)
            state = (state.astype(F32) + add).astype(BF16)
            kept = jnp.where(section == s, state, kept)
        leaving.append(kept)
        final = state.astype(F32)
        upstream = entering[1, :, m].astype(F32) * gains[:, None, :]
        sums = jnp.stack(
            [jnp.sum(final * final, axis=(0, 2)), jnp.sum(upstream * final, axis=(0, 2))]
        ).reshape(2, outers, own_rows)
        total = sums
        for step in range(1, outers):
            total = total + jnp.roll(to_outer(sums, step), step, axis=1)
        total = total.reshape(2, rows) / features
        scale = lax.rsqrt(total[0] + 1e-05)
        shrink = scale * scale * total[1]
        grads.append(
            (scale[None, :, None] * (upstream - final * shrink[None, :, None])).astype(BF16)
        )

    full = []
    order = []
    earlier = None
    for m in range(micro):
        if blocks != 4:
            pieces_m = [grads[m]] + [to_block(grads[m], step) for step in range(1, blocks)]
            full.append(jnp.concatenate(pieces_m, axis=1))
            order.append([(t - step) % blocks for step in range(blocks)])
            continue
        opposite = to_block(grads[m], 2)
        beside = lax.ppermute(grads[m], "tensor", [(i, i ^ 1) for i in range(4)])
        mid = lax.ppermute(grads[m], "tensor", [(1, 2), (2, 1)])
        relay = after(opposite, beside, mid)
        farthest = lax.ppermute(relay, "tensor", [(1, 0), (2, 3)])
        last = jnp.where((t == 1) | (t == 2), mid, farthest)
        if earlier is not None:
            full[-1] = after(full[-1], relay)
        full.append(jnp.concatenate([grads[m], beside, opposite, last], axis=1))
        order.append([t, t ^ 1, t ^ 2, t ^ 3])
        earlier = relay

    outs = []
    for m in range(micro):
        by_group = after(leaving[m], grads[m]).reshape(2, outers, own_rows, width)
        row = jnp.zeros((own_rows, features), BF16)
        for step in range(outers):
            at = (outer + step) % outers
            piece = by_group[:, step]
            if step:
                piece = after(to_outer(piece, outers - step), full[-1])
            for slot in range(2):
                place = (2 * at + (core if slot == 0 else 1 - core)) * width
                row = lax.dynamic_update_slice_in_dim(row, piece[slot], place, 1)
        outs.append(row)
    section_out = jnp.stack(outs).reshape(1, micro, 1, own_rows, features)

    mix_rows = [
        jnp.concatenate(
            [pick(taken[m].reshape(blocks, rows, head_cols), at) for at in order[m]], axis=0
        )
        for m in range(micro)
    ]
    permuted_rows = [
        jnp.concatenate(
            [
                columns(half, m * tokens + at * own_rows, own_rows)
                for at in order[m]
                for half in permuted
            ],
            axis=1,
        )
        for m in range(micro)
    ]

    holder = (t * per_block) // 2
    mix_grads = []
    right_sum = 0.0
    left_sum = 0.0
    for m in range(micro):
        if per_block == 1:
            cols = pick(full[m], jnp.where(t % 2 == core, 0, 1))
        else:
            cols = jnp.concatenate(list(of_cores(full[m])), axis=1)
        left_sum = left_sum + dot(permuted_rows[m], cols, 1, 0)

        inner_grads = [
            dot(full[m][slot], left_slots[slot], 1, 1).astype(BF16) for slot in range(2)
        ]
        if per_block == 1:
            mine = jnp.concatenate(inner_grads, axis=1)
            right_here = jnp.concatenate(right_slots, axis=1)
        else:
            mine = (inner_grads[0].astype(F32) + inner_grads[1].astype(F32)).astype(BF16)
            right_here = right_slots[0]
        right_sum = right_sum + dot(mine, mix_rows[m], 0, 0)

        partial_mix = (
            dot(full[m][0], weights[0], 1, 1)
            + dot(full[m][1], weights[1], 1, 1)
            + dot(mine, right_here, 1, 1)
        ).reshape(blocks, outers, own_rows, head_cols)
        whole = partial_mix[:, 0]
        for step in range(1, outers):
            whole = whole + to_outer(partial_mix[:, step].astype(BF16), outers - step).astype(F32)
        whole = whole.astype(BF16)
        back = [t ^ i for i in range(blocks)] if blocks == 4 else order[m]
        mix_grads.append(
            jnp.concatenate([pick(whole, at) for at in back], axis=0)
        )
    grad_mix = jnp.stack(mix_grads).reshape(1, micro, 1, tokens, head_cols)

    half = block_cols // 2
    half_sum = (
        columns(left_sum, core * half, half) + to_core(columns(left_sum, (1 - core) * half, half))
    ).astype(BF16)
    best = half_sum
    for step in range(1, outers):
        pairs = []
        for i in range(blocks):
            at = (i * per_block) // 2
            for c in range(2):
                pairs.append(
                    (i * parts + 2 * at + c, i * parts + 2 * ((at + step) % outers) + c)
                )
        arrived = lax.ppermute(half_sum, ("tensor", "dp"), pairs)
        best = jnp.where((outer - holder) % outers == step, arrived, best)
    there = to_core(best)
    grad_left = jnp.concatenate(list(of_cores(jnp.stack([best, there]))), axis=1).astype(F32)

    if per_block == 1:
        right_sum = of_cores(right_sum.reshape(2, sub, head_cols)).reshape(2 * sub, head_cols)
    right_sum = (right_sum + to_core(right_sum)).astype(BF16)
    wide = jnp.zeros((rank, head_cols), BF16)
    count = right_sum.shape[0]
    for step in range(outers):
        arrived = to_outer(right_sum, step) if step else right_sum
        wide = lax.dynamic_update_slice_in_dim(
            wide, arrived, ((outer - step) % outers) * count, 0
        )
    grad_right = wide.T.astype(F32)

    return (
        section_out,
        grad_mix,
        grad_right.reshape(1, 1, head_cols, rank),
        grad_left.reshape(1, 1, rank, block_cols),
    )


def solution(mesh):
    return jax.shard_map(
        on_device,
        mesh=mesh,
        in_specs=(
            P("pipe", None, "dp", None, "tensor"),
            P(None, "dp", "tensor", None),
            P(None, "dp", "tensor", None),
            P("pipe", "tensor", "dp"),
            P("pipe", "tensor", None, None),
            P("pipe", "tensor", None, None),
            P(),
        ),
        out_specs=(
            P("pipe", None, "dp", "tensor", None),
            P("pipe", None, "dp", None, "tensor"),
            P("pipe", "tensor", None, None),
            P("pipe", "tensor", None, None),
        ),
        check_vma=False,
    )
```

```python
import functools

import jax
import jax.numpy as jnp
from jax import lax
from jax.experimental import pallas as pl
from jax.experimental.pallas import tpu as pltpu
from jax.sharding import PartitionSpec as P

F32 = jnp.float32
BF16 = jnp.bfloat16
VMEM = 24 * 2**20


def dot(left_side, right_side, left_dim, right_dim):
    return lax.dot_general(
        left_side,
        right_side,
        (((left_dim,), (right_dim,)), ((), ())),
        preferred_element_type=F32,
    )


def pick(value, index, dim=0):
    return lax.dynamic_index_in_dim(value, index, dim, keepdims=False)


def columns(value, start, size):
    return lax.dynamic_slice_in_dim(value, start, size, value.ndim - 1)


def after(value, *others):
    return lax.optimization_barrier((value, *others))[0]


def piece_kernel(place, mixes, right, left, *refs):
    pieces, turned = refs[:-1], refs[-1]
    t, core = place[0], place[2]
    sub = pieces[0].shape[0]
    half = left.shape[1] // 2
    turned[...] = jnp.dot(mixes[...], right[...], preferred_element_type=F32).T
    for o, piece in enumerate(pieces):
        at = pl.ds(pl.multiple_of((t ^ o) * sub, sub), sub)
        piece[:, :half] = left[at, pl.ds(pl.multiple_of(core * half, half), half)]
        piece[:, half:] = turned[at, :].astype(BF16)


def cut_pieces(place, mixes, right, left):
    rows = mixes.shape[0]
    rank, width = left.shape
    vmem = pl.BlockSpec(memory_space=pltpu.VMEM)
    return pl.pallas_call(
        piece_kernel,
        in_specs=[pl.BlockSpec(memory_space=pltpu.SMEM)] + [vmem] * 3,
        out_specs=[vmem] * 4,
        out_shape=[jax.ShapeDtypeStruct((rank // 4, width // 2 + rows), BF16)] * 4,
        scratch_shapes=[pltpu.VMEM((rank, rows), F32)],
        compiler_params=pltpu.CompilerParams(vmem_limit_bytes=VMEM),
    )(place, mixes, right, left)


def project_kernel(place, own_mix, other_mix, w00, w01, w10, w11, right, own_half, other_half, *refs):
    sums, (mix_rows, left_rows, inner) = refs[:-3], refs[-3:]
    cuts = ((w00, w01), (w10, w11))
    t, outer, core = place[0], place[1], place[2]
    micro, shards = mix_rows.shape[0], 4
    sub, half = own_half.shape[1:]
    step = pl.program_id(0)
    rows = sums[0].shape[1]
    own_rows = rows // 2
    size = shards * rows
    depth, tile = w00.shape

    @pl.when(step == 0)
    def _():
        for m in range(micro):
            for r in range(shards):
                at = pl.ds(pl.multiple_of((t ^ r) * own_rows, own_rows), own_rows)
                for group, source in enumerate((own_mix, other_mix)):
                    mix_rows[m, pl.ds(r * rows + group * own_rows, own_rows), :] = source[m, at, :]
            inner[pl.ds(m * size, size), :] = jnp.dot(
                mix_rows[m], right[...], preferred_element_type=F32
            ).astype(BF16)
        left_rows[...] = jnp.zeros_like(left_rows)
        for slot in range(2):
            part = core ^ slot
            at = pl.ds(pl.multiple_of((2 * outer + part) * sub, sub), sub)
            left_rows[slot, at, pl.ds(pl.multiple_of(core * half, half), half)] = own_half[part]
            left_rows[slot, at, pl.ds(pl.multiple_of((1 - core) * half, half), half)] = other_half[part]

    at = pl.ds(pl.multiple_of(step * tile, tile), tile)
    lines = mix_rows[...].reshape(micro * size, -1)
    for slot in range(2):
        product = jnp.dot(inner[...], left_rows[slot, :, at], preferred_element_type=F32)
        for i, weight in enumerate(cuts[slot]):
            product += jnp.dot(
                lines[:, i * depth : (i + 1) * depth], weight[...], preferred_element_type=F32
            )
        for i in range(micro * shards):
            sums[i][slot] = product[i * rows : (i + 1) * rows].astype(BF16)


def doubled(weights):
    return [weights[0], weights[0], weights[1], weights[1]]


def weight_specs(head_cols, tile):
    return [
        pl.BlockSpec((head_cols // 2, tile), lambda i: (0, i)),
        pl.BlockSpec((head_cols // 2, tile), lambda i: (1, i)),
    ] * 2


def whole(*shape):
    return pl.BlockSpec(shape, lambda i: (0,) * len(shape))


def project(place, own_mix, other_mix, weights, right, own_half, other_half):
    micro, tokens, head_cols = own_mix.shape
    width = weights[0].shape[1]
    rank = right.shape[1]
    tile = 512
    tiles = width // tile
    rows = tokens // 2
    size = 4 * rows
    return pl.pallas_call(
        project_kernel,
        grid=(tiles,),
        in_specs=[
            pl.BlockSpec(memory_space=pltpu.SMEM),
            whole(*own_mix.shape),
            whole(*own_mix.shape),
            *weight_specs(head_cols, tile),
            whole(*right.shape),
            whole(*own_half.shape),
            whole(*own_half.shape),
        ],
        out_specs=[pl.BlockSpec((2, rows, tile), lambda i: (0, 0, i))] * (4 * micro)
        + [whole(micro, size, head_cols), whole(2, rank, width)],
        out_shape=[jax.ShapeDtypeStruct((2, rows, width), BF16)] * (4 * micro)
        + [
            jax.ShapeDtypeStruct((micro, size, head_cols), BF16),
            jax.ShapeDtypeStruct((2, rank, width), BF16),
        ],
        scratch_shapes=[pltpu.VMEM((micro * size, rank), BF16)],
        compiler_params=pltpu.CompilerParams(vmem_limit_bytes=VMEM),
        cost_estimate=pl.CostEstimate(
            flops=4 * micro * size * head_cols * width,
            bytes_accessed=4 * head_cols * width,
            transcendentals=0,
        ),
    )(place, own_mix, other_mix, *doubled(weights), right, own_half, other_half)


def back_kernel(m, place, *refs):
    pieces, refs = refs[:5], refs[5:]
    cuts, refs = (refs[0:2], refs[2:4]), refs[4:]
    left_rows, right, mix_rows, own_permuted, other_permuted = refs[:5]
    earlier, refs = (refs[5:7], refs[7:]) if m else (None, refs[5:])
    mix_here, mix_sent, left_sum, right_sum, total, inner_grad, turned, permuted, right_all = refs
    t, outer, core = place[0], place[1], place[2]
    step = pl.program_id(0)
    steps = pl.num_programs(0)
    rows = pieces[0].shape[1]
    own_rows = rows // 2
    tokens = 4 * own_rows
    depth, tile = cuts[0][0].shape
    half = left_sum.shape[2]

    @pl.when(step == 0)
    def _():
        total[...] = jnp.zeros_like(total)
        inner_grad[...] = jnp.zeros_like(inner_grad)
        for group, source in enumerate((own_permuted, other_permuted)):
            turned[group] = source[...].astype(F32).T
        for r in range(4):
            at = pl.ds(pl.multiple_of(m * tokens + (t ^ r) * own_rows, own_rows), own_rows)
            for group in range(2):
                permuted[pl.ds(r * rows + group * own_rows, own_rows), :] = turned[group, at, :]
        permuted[...] = permuted[...].T

    own, beside, opposite, mid, farthest = pieces
    grads = [
        jnp.concatenate(
            [own[slot], beside[slot], opposite[slot], mid[slot] + farthest[slot]], axis=0
        )
        for slot in range(2)
    ]
    over = (((1,), (1,)), ((), ()))
    for i in range(2):
        total[pl.ds(i * depth, depth), :] += lax.dot_general(
            cuts[0][i][...], grads[0], over, preferred_element_type=F32
        ) + lax.dot_general(cuts[1][i][...], grads[1], over, preferred_element_type=F32)
    inner_grad[...] += lax.dot_general(
        grads[0], left_rows[0], over, preferred_element_type=F32
    ) + lax.dot_general(grads[1], left_rows[1], over, preferred_element_type=F32)

    at = step * tile
    which = (at // half) ^ core
    cut = pl.ds(pl.multiple_of(at % half, tile), tile)
    block = jnp.where(((t & 1) ^ core) == 0, grads[0], grads[1])
    product = jnp.dot(permuted[...].astype(BF16), block, preferred_element_type=F32)
    if m:
        product += earlier[0][which, :, cut]
    left_sum[which, :, cut] = product

    @pl.when(step == steps - 1)
    def _():
        mine = inner_grad[...].astype(BF16)
        everything = total[...].T + lax.dot_general(
            mine, right[...], (((1,), (1,)), ((), ())), preferred_element_type=F32
        )
        for r in range(4):
            at = pl.ds(pl.multiple_of((t ^ r) * own_rows, own_rows), own_rows)
            mix_here[at, :] = everything[r * rows : r * rows + own_rows]
            mix_sent[at, :] = everything[r * rows + own_rows : (r + 1) * rows].astype(BF16)
        right_all[...] = lax.dot_general(
            mine, mix_rows[0], (((0,), (0,)), ((), ())), preferred_element_type=F32
        )
        count = right_sum.shape[0]
        product = right_all[pl.ds(pl.multiple_of(outer * count, count), count), :]
        if m:
            product += earlier[1][...]
        right_sum[...] = product


def back(m, place, pieces, weights, left_rows, right, mix_rows, permuted, earlier):
    _, rows, width = pieces[0].shape
    head_cols, rank = right.shape
    size = 4 * rows
    tokens = size // 2
    half = width // 2
    tile = 512
    tiles = width // tile
    piece = pl.BlockSpec((2, rows, tile), lambda i: (0, 0, i))
    shapes = [
        jax.ShapeDtypeStruct((tokens, head_cols), F32),
        jax.ShapeDtypeStruct((tokens, head_cols), BF16),
        jax.ShapeDtypeStruct((2, rank, half), F32),
        jax.ShapeDtypeStruct((rank // 2, head_cols), F32),
    ]
    return pl.pallas_call(
        functools.partial(back_kernel, m),
        grid=(tiles,),
        in_specs=[pl.BlockSpec(memory_space=pltpu.SMEM)]
        + [piece] * 5
        + weight_specs(head_cols, tile)
        + [
            pl.BlockSpec((2, rank, tile), lambda i: (0, 0, i)),
            whole(*right.shape),
            pl.BlockSpec((1, size, head_cols), lambda i: (m, 0, 0)),
            whole(*permuted[0].shape),
            whole(*permuted[0].shape),
        ]
        + [whole(*value.shape) for value in earlier],
        out_specs=[whole(*shape.shape) for shape in shapes],
        out_shape=shapes,
        scratch_shapes=[
            pltpu.VMEM((head_cols, size), F32),
            pltpu.VMEM((size, rank), F32),
            pltpu.VMEM((2, *permuted[0].shape[::-1]), F32),
            pltpu.VMEM((size, rank), F32),
            pltpu.VMEM((rank, head_cols), F32),
        ],
        compiler_params=pltpu.CompilerParams(vmem_limit_bytes=VMEM),
        cost_estimate=pl.CostEstimate(
            flops=4 * size * head_cols * width,
            bytes_accessed=4 * head_cols * width,
            transcendentals=0,
        ),
    )(place, *pieces, *doubled(weights), left_rows, right, mix_rows, *permuted, *earlier)


def finish_kernel(place, own_left, other_left, own_right, other_right, grad_left, grad_right, wide):
    outer, core = place[1], place[2]
    half = own_left.shape[1]
    count = own_right.shape[0]
    grad_left[:, pl.ds(pl.multiple_of(core * half, half), half)] = own_left[...].astype(F32)
    grad_left[:, pl.ds(pl.multiple_of((1 - core) * half, half), half)] = other_left[...].astype(F32)
    wide[pl.ds(pl.multiple_of(outer * count, count), count), :] = own_right[...].astype(F32)
    wide[pl.ds(pl.multiple_of((1 - outer) * count, count), count), :] = other_right[...].astype(F32)
    grad_right[...] = wide[...].T


def finish(place, own_left, other_left, own_right, other_right):
    rank, half = own_left.shape
    head_cols = own_right.shape[1]
    vmem = pl.BlockSpec(memory_space=pltpu.VMEM)
    return pl.pallas_call(
        finish_kernel,
        in_specs=[pl.BlockSpec(memory_space=pltpu.SMEM)] + [vmem] * 4,
        out_specs=[vmem] * 2,
        out_shape=[
            jax.ShapeDtypeStruct((rank, 2 * half), F32),
            jax.ShapeDtypeStruct((head_cols, rank), F32),
        ],
        scratch_shapes=[pltpu.VMEM((rank, head_cols), F32)],
        compiler_params=pltpu.CompilerParams(vmem_limit_bytes=VMEM),
    )(place, own_left, other_left, own_right, other_right)


def on_device(mix, hidden_in, cotangent, frozen_weight, right_factor, left_factor, norm_gain):
    t = lax.axis_index("tensor")
    d = lax.axis_index("dp")
    section = lax.axis_index("pipe")
    outer = d // 2
    core = d % 2
    place = jnp.stack([t, outer, core]).astype(jnp.int32)

    def to_core(value):
        return lax.ppermute(value, "dp", [(i, i ^ 1) for i in range(4)])

    def to_outer(value):
        return lax.ppermute(value, "dp", [(i, i ^ 2) for i in range(4)])

    def along(value, *pairs):
        return lax.ppermute(value, "tensor", pairs)

    mixes = mix[0, :, 0]
    micro, tokens, head_cols = mixes.shape
    own_rows = tokens // 4
    rows = 2 * own_rows
    weight = frozen_weight[0]
    right = right_factor[0, 0]
    left = left_factor[0, 0]
    rank, width = left.shape
    sub = rank // 4
    half = width // 2
    features = 4 * width
    slots = (d, d ^ 1)

    other_mixes = to_outer(mixes)
    weights = (weight, to_core(weight))
    cut = cut_pieces(place, mixes.reshape(micro * tokens, head_cols), right, left)
    met = [cut[0]] + [along(cut[o], *[(i, i ^ o) for i in range(4)]) for o in range(1, 4)]

    def of_block(block, start, stop):
        return lax.select_n(t ^ block, *[piece[:, start:stop] for piece in met])

    own_half = jnp.stack([of_block(2 * outer + i, 0, half) for i in range(2)])
    other_half = to_core(own_half)
    own_permuted = jnp.concatenate(
        [of_block(i, half, half + micro * tokens) for i in range(4)], axis=0
    )

    *partial, mix_rows, left_rows = project(
        place, mixes, other_mixes, weights, right, own_half, other_half
    )

    totals = []
    ahead = None
    for m in range(micro):
        own, next_one, two_away, last = partial[4 * m : 4 * m + 4]
        if ahead is not None:
            next_one = after(next_one, ahead)
            last = after(last, ahead)
        passed = along(last, (0, 1), (3, 2))
        beside = along(next_one, *[(i, i ^ 1) for i in range(4)])
        mid = along(last, (1, 2), (2, 1))
        ahead = (two_away.astype(F32) + passed.astype(F32)).astype(BF16)
        if m == 0:
            ahead = after(ahead, beside, mid)
        crossed = along(ahead, *[(i, i ^ 2) for i in range(4)])
        totals.append((own, beside, mid, crossed))

    hidden_late = after(hidden_in, partial[0])

    def by_column(target):
        cuts = [2 * target + core, 2 * target + (1 - core)]
        return jnp.stack(
            [
                jnp.stack([columns(value[:, 0], part * width, width) for part in cuts])
                for value in (hidden_late, cotangent)
            ]
        )

    entering = jnp.concatenate([by_column(outer), to_outer(by_column(1 - outer))], axis=3)
    gains = jnp.stack([columns(norm_gain, part * width, width) for part in slots]).astype(F32)
    own_permuted = after(own_permuted, partial[0])
    permuted = (own_permuted, to_outer(own_permuted))

    grads = []
    leaving = []
    for m in range(micro):
        own, beside, mid, crossed = totals[m]
        if m:
            crossed = after(crossed, grads[m - 1])
        update = (
            own.astype(F32) + beside.astype(F32) + mid.astype(F32) + crossed.astype(F32)
        )
        sent = update.astype(BF16)
        other = lax.ppermute(sent, "pipe", [(0, 1), (1, 0)])
        if m == 0:
            other = after(other, ahead)
        other = other.astype(F32)
        first = entering[0, :, m].astype(F32) + jnp.where(section == 0, update, other)
        first = first.astype(BF16)
        second = (first.astype(F32) + jnp.where(section == 0, other, update)).astype(BF16)
        leaving.append(jnp.where(section == 0, first, second))
        final = second.astype(F32)
        upstream = entering[1, :, m].astype(F32) * gains[:, None, :]
        sums = jnp.stack(
            [jnp.sum(final * final, axis=(0, 2)), jnp.sum(upstream * final, axis=(0, 2))]
        ).reshape(2, 2, own_rows)
        total = (sums + to_outer(sums)[:, ::-1]).reshape(2, rows) / features
        scale = lax.rsqrt(total[0] + 1e-05)
        shrink = scale * scale * total[1]
        grads.append(
            (scale[None, :, None] * (upstream - final * shrink[None, :, None])).astype(BF16)
        )

    sums = ()
    mix_grads = []
    relays = []
    for m in range(micro):
        opposite = along(grads[m], *[(i, i ^ 2) for i in range(4)])
        beside = along(grads[m], *[(i, i ^ 1) for i in range(4)])
        mid = along(grads[m], (1, 2), (2, 1))
        relay = after(opposite, beside, mid, *sums)
        farthest = along(relay, (1, 0), (2, 3))
        relays.append(relay)
        pieces = [after(grads[m], grads[-1]), beside, relay, mid, farthest]
        mix_here, mix_sent, *sums = back(
            m, place, pieces, weights, left_rows, right, mix_rows, permuted, sums
        )
        mix_grads.append((mix_here + to_outer(mix_sent).astype(F32)).astype(BF16))
    grad_mix = jnp.stack(mix_grads).reshape(1, micro, 1, tokens, head_cols)

    outs = []
    for m in range(micro):
        by_group = leaving[m].reshape(2, 2, own_rows, width)
        arrived = to_outer(after(by_group[:, 1], grads[m]))
        arrived = after(arrived, relays[-1])
        row = jnp.zeros((own_rows, features), BF16)
        for at, piece in ((outer, by_group[:, 0]), (1 - outer, arrived)):
            for slot in range(2):
                place_at = (2 * at + (core if slot == 0 else 1 - core)) * width
                row = lax.dynamic_update_slice_in_dim(row, piece[slot], place_at, 1)
        outs.append(row)
    section_out = jnp.stack(outs).reshape(1, micro, 1, own_rows, features)

    left_sum, right_sum = sums
    half_sum = (left_sum[0] + to_core(left_sum[1])).astype(BF16)
    pairs = [
        (4 * i + 2 * (i // 2) + c, 4 * i + 2 * (1 - i // 2) + c) for i in range(4) for c in range(2)
    ]
    arrived = lax.ppermute(half_sum, ("tensor", "dp"), pairs)
    best = jnp.where(outer == t // 2, half_sum, arrived)
    own_right = (right_sum + to_core(right_sum)).astype(BF16)
    grad_left, grad_right = finish(place, best, to_core(best), own_right, to_outer(own_right))

    return (
        section_out,
        grad_mix,
        grad_right.reshape(1, 1, head_cols, rank),
        grad_left.reshape(1, 1, rank, width),
    )


def on_device_general(mix, hidden_in, cotangent, frozen_weight, right_factor, left_factor, norm_gain):
    blocks = lax.axis_size("tensor")
    parts = lax.axis_size("dp")
    sections = lax.axis_size("pipe")
    t = lax.axis_index("tensor")
    d = lax.axis_index("dp")
    section = lax.axis_index("pipe")
    outers = parts // 2
    outer = d // 2
    core = d % 2

    def to_core(value):
        return lax.ppermute(value, "dp", [(i, i ^ 1) for i in range(parts)])

    def to_outer(value, step):
        return lax.ppermute(value, "dp", [(i, (i + 2 * step) % parts) for i in range(parts)])

    def to_block(value, step):
        return lax.ppermute(value, "tensor", [(i, (i + step) % blocks) for i in range(blocks)])

    def of_cores(value):
        return jnp.where(core == 0, value, value[::-1])

    mixes = mix[0, :, 0]
    micro, tokens, head_cols = mixes.shape
    own_rows = tokens // blocks
    weight = frozen_weight[0]
    right = right_factor[0, 0]
    left = left_factor[0, 0]
    rank, block_cols = left.shape
    sub = rank // blocks
    width = weight.shape[1]
    features = width * parts
    rows = outers * own_rows
    all_rows = blocks * rows
    per_block = parts // blocks
    slots = (d, d ^ 1)

    def block_of(part):
        return part // per_block

    weights = (weight, to_core(weight))
    own = mixes.reshape(micro, blocks, 1, own_rows, head_cols)
    taken = [
        jnp.concatenate(
            [own[m]] + [to_outer(own[m], step) for step in range(1, outers)], axis=1
        ).reshape(all_rows, head_cols)
        for m in range(micro)
    ]
    own_inner = dot(right, mixes.reshape(micro * tokens, head_cols), 0, 1).astype(BF16)
    pieces = lax.all_to_all(
        jnp.concatenate(
            [
                left.reshape(blocks, sub, block_cols),
                own_inner.reshape(blocks, sub, micro * tokens),
            ],
            axis=2,
        ),
        "tensor",
        split_axis=0,
        concat_axis=0,
        tiled=True,
    )
    left_slots = [
        columns(pick(pieces, block_of(part)), (part % per_block) * width, width) for part in slots
    ]
    right_slots = [columns(right, block_of(part) * sub, sub) for part in slots]
    own_permuted = pieces[:, :, block_cols:].reshape(rank, micro * tokens)
    own_permuted = after(own_permuted, *taken)
    permuted = [own_permuted] + [to_outer(own_permuted, step) for step in range(1, outers)]

    inners = [dot(taken[m], right, 1, 0).astype(BF16) for m in range(micro)]
    partial = [
        jnp.stack(
            [
                (
                    dot(taken[m], weights[slot], 1, 0)
                    + dot(
                        columns(inners[m], block_of(part) * sub, sub), left_slots[slot], 1, 0
                    )
                ).astype(BF16)
                for slot, part in enumerate(slots)
            ]
        ).reshape(2, blocks, rows, width)
        for m in range(micro)
    ]

    def shard(m, index):
        return pick(partial[m], index, 1)

    updates_here = []
    for m in range(micro):
        total = shard(m, t).astype(F32)
        for step in range(1, blocks):
            total = total + to_block(shard(m, (t + step) % blocks), step).astype(F32)
        updates_here.append(total)

    hidden_late = after(hidden_in, *taken)

    def by_column(step):
        target = (outer + step) % outers
        cuts = [2 * target + core, 2 * target + (1 - core)]
        return jnp.stack(
            [
                jnp.stack([columns(value[:, 0], part * width, width) for part in cuts])
                for value in (hidden_late, cotangent)
            ]
        )

    entering = jnp.concatenate(
        [by_column(0)] + [to_outer(by_column(step), step) for step in range(1, outers)], axis=3
    )
    gains = jnp.stack([columns(norm_gain, part * width, width) for part in slots]).astype(F32)

    grads = []
    leaving = []
    for m in range(micro):
        sent = updates_here[m].astype(BF16)
        updates = [updates_here[m]] + [
            lax.ppermute(
                sent, "pipe", [(i, (i + step) % sections) for i in range(sections)]
            ).astype(F32)
            for step in range(1, sections)
        ]
        state = entering[0, :, m]
        kept = state
        for s in range(sections):
            add = updates[0]
            for step in range(1, sections):
                add = jnp.where((section - step) % sections == s, updates[step], add)
            state = (state.astype(F32) + add).astype(BF16)
            kept = jnp.where(section == s, state, kept)
        leaving.append(kept)
        final = state.astype(F32)
        upstream = entering[1, :, m].astype(F32) * gains[:, None, :]
        sums = jnp.stack(
            [jnp.sum(final * final, axis=(0, 2)), jnp.sum(upstream * final, axis=(0, 2))]
        ).reshape(2, outers, own_rows)
        total = sums
        for step in range(1, outers):
            total = total + jnp.roll(to_outer(sums, step), step, axis=1)
        total = total.reshape(2, rows) / features
        scale = lax.rsqrt(total[0] + 1e-05)
        shrink = scale * scale * total[1]
        grads.append(
            (scale[None, :, None] * (upstream - final * shrink[None, :, None])).astype(BF16)
        )

    full = [
        jnp.concatenate(
            [grads[m]] + [to_block(grads[m], step) for step in range(1, blocks)], axis=1
        )
        for m in range(micro)
    ]
    order = [[(t - step) % blocks for step in range(blocks)]] * micro

    outs = []
    for m in range(micro):
        by_group = after(leaving[m], grads[m]).reshape(2, outers, own_rows, width)
        row = jnp.zeros((own_rows, features), BF16)
        for step in range(outers):
            at = (outer + step) % outers
            piece = by_group[:, step]
            if step:
                piece = after(to_outer(piece, outers - step), full[-1])
            for slot in range(2):
                place = (2 * at + (core if slot == 0 else 1 - core)) * width
                row = lax.dynamic_update_slice_in_dim(row, piece[slot], place, 1)
        outs.append(row)
    section_out = jnp.stack(outs).reshape(1, micro, 1, own_rows, features)

    mix_rows = [
        jnp.concatenate(
            [pick(taken[m].reshape(blocks, rows, head_cols), at) for at in order[m]], axis=0
        )
        for m in range(micro)
    ]
    permuted_rows = [
        jnp.concatenate(
            [
                columns(half, m * tokens + at * own_rows, own_rows)
                for at in order[m]
                for half in permuted
            ],
            axis=1,
        )
        for m in range(micro)
    ]

    holder = (t * per_block) // 2
    mix_grads = []
    right_sum = 0.0
    left_sum = 0.0
    for m in range(micro):
        if per_block == 1:
            cols = pick(full[m], jnp.where(t % 2 == core, 0, 1))
        else:
            cols = jnp.concatenate(list(of_cores(full[m])), axis=1)
        left_sum = left_sum + dot(permuted_rows[m], cols, 1, 0)

        inner_grads = [
            dot(full[m][slot], left_slots[slot], 1, 1).astype(BF16) for slot in range(2)
        ]
        if per_block == 1:
            mine = jnp.concatenate(inner_grads, axis=1)
            right_here = jnp.concatenate(right_slots, axis=1)
        else:
            mine = (inner_grads[0].astype(F32) + inner_grads[1].astype(F32)).astype(BF16)
            right_here = right_slots[0]
        right_sum = right_sum + dot(mine, mix_rows[m], 0, 0)

        partial_mix = (
            dot(full[m][0], weights[0], 1, 1)
            + dot(full[m][1], weights[1], 1, 1)
            + dot(mine, right_here, 1, 1)
        ).reshape(blocks, outers, own_rows, head_cols)
        whole = partial_mix[:, 0]
        for step in range(1, outers):
            whole = whole + to_outer(partial_mix[:, step].astype(BF16), outers - step).astype(F32)
        whole = whole.astype(BF16)
        back = order[m]
        mix_grads.append(
            jnp.concatenate([pick(whole, at) for at in back], axis=0)
        )
    grad_mix = jnp.stack(mix_grads).reshape(1, micro, 1, tokens, head_cols)

    half = block_cols // 2
    half_sum = (
        columns(left_sum, core * half, half) + to_core(columns(left_sum, (1 - core) * half, half))
    ).astype(BF16)
    best = half_sum
    for step in range(1, outers):
        pairs = []
        for i in range(blocks):
            at = (i * per_block) // 2
            for c in range(2):
                pairs.append(
                    (i * parts + 2 * at + c, i * parts + 2 * ((at + step) % outers) + c)
                )
        arrived = lax.ppermute(half_sum, ("tensor", "dp"), pairs)
        best = jnp.where((outer - holder) % outers == step, arrived, best)
    there = to_core(best)
    grad_left = jnp.concatenate(list(of_cores(jnp.stack([best, there]))), axis=1).astype(F32)

    if per_block == 1:
        right_sum = of_cores(right_sum.reshape(2, sub, head_cols)).reshape(2 * sub, head_cols)
    right_sum = (right_sum + to_core(right_sum)).astype(BF16)
    wide = jnp.zeros((rank, head_cols), BF16)
    count = right_sum.shape[0]
    for step in range(outers):
        arrived = to_outer(right_sum, step) if step else right_sum
        wide = lax.dynamic_update_slice_in_dim(
            wide, arrived, ((outer - step) % outers) * count, 0
        )
    grad_right = wide.T.astype(F32)

    return (
        section_out,
        grad_mix,
        grad_right.reshape(1, 1, head_cols, rank),
        grad_left.reshape(1, 1, rank, block_cols),
    )


def solution(mesh):
    sizes = (mesh.shape["tensor"], mesh.shape["dp"], mesh.shape["pipe"])
    return jax.shard_map(
        on_device if sizes == (4, 4, 2) else on_device_general,
        mesh=mesh,
        in_specs=(
            P("pipe", None, "dp", None, "tensor"),
            P(None, "dp", "tensor", None),
            P(None, "dp", "tensor", None),
            P("pipe", "tensor", "dp"),
            P("pipe", "tensor", None, None),
            P("pipe", "tensor", None, None),
            P(),
        ),
        out_specs=(
            P("pipe", None, "dp", "tensor", None),
            P("pipe", None, "dp", None, "tensor"),
            P("pipe", "tensor", None, None),
            P("pipe", "tensor", None, None),
        ),
        check_vma=False,
    )
```

```python
import functools

import jax
import jax.numpy as jnp
from jax import lax
from jax.experimental import pallas as pl
from jax.experimental.pallas import tpu as pltpu
from jax.sharding import PartitionSpec as P

F32 = jnp.float32
BF16 = jnp.bfloat16
VMEM = 24 * 2**20
VMEM_ALL = 48 * 2**20
VMEM_SMALL = 10 * 2**20


def dot(left_side, right_side, left_dim, right_dim):
    return lax.dot_general(
        left_side,
        right_side,
        (((left_dim,), (right_dim,)), ((), ())),
        preferred_element_type=F32,
    )


def pick(value, index, dim=0):
    return lax.dynamic_index_in_dim(value, index, dim, keepdims=False)


def columns(value, start, size):
    return lax.dynamic_slice_in_dim(value, start, size, value.ndim - 1)


def after(value, *others):
    return lax.optimization_barrier((value, *others))[0]


NO_COST = pl.CostEstimate(flops=0, bytes_accessed=0, transcendentals=0)


def small(kernel, outs, scratch, place, *values):
    vmem = pl.BlockSpec(memory_space=pltpu.VMEM)
    return pl.pallas_call(
        kernel,
        in_specs=[pl.BlockSpec(memory_space=pltpu.SMEM)] + [vmem] * len(values),
        out_specs=[vmem] * len(outs),
        out_shape=[jax.ShapeDtypeStruct(shape, dtype) for shape, dtype in outs],
        scratch_shapes=scratch,
        compiler_params=pltpu.CompilerParams(vmem_limit_bytes=VMEM_SMALL),
        cost_estimate=NO_COST,
    )(place, *values)


def at_multiple(index, size):
    return pl.ds(pl.multiple_of(index * size, size), size)


def cut_kernel(place, hidden, cotangent, here, there):
    outer, core = place[1], place[2]
    width = here.shape[4]
    for out, target in ((here, outer), (there, 1 - outer)):
        for which, source in enumerate((hidden, cotangent)):
            for m in range(source.shape[0]):
                for slot in range(2):
                    out[which, m, slot] = source[m, :, at_multiple(2 * target + (core ^ slot), width)]


def ahead_kernel(place, two_away, passed, ahead):
    carried = ahead.shape[2] - two_away.shape[2]
    width = two_away.shape[2] - carried
    ahead[:, :, :width] = (
        two_away[:, :, :width].astype(F32) + passed[:, :, :width].astype(F32)
    ).astype(BF16)
    if carried:
        ahead[:, :, width : width + carried] = two_away[:, :, width:]
        ahead[:, :, width + carried :] = passed[:, :, width:]


def update_kernel(place, own, beside, *refs):
    micro, _, _, width = own.shape
    mids, crossings, (update, kept, sent) = refs[:micro], refs[micro : 2 * micro], refs[2 * micro :]
    for m in range(micro):
        total = (own[m].astype(F32) + beside[m, :, :, :width].astype(F32)) + (
            mids[m][:, :, :width].astype(F32) + crossings[m][:, :, :width].astype(F32)
        )
        update[m] = total
        (sent if m else kept)[...] = total.astype(BF16)


def state_kernel(place, here, arrived, gain, update, other, leaving, final, sums):
    outer, core, section = place[1], place[2], place[3]
    own_rows, width = here.shape[3:]
    for group, source in enumerate((here, arrived)):
        at = pl.ds(group * own_rows, own_rows)
        squares = jnp.zeros((own_rows, 1), F32)
        products = jnp.zeros((own_rows, 1), F32)
        for slot in range(2):
            mine = update[0, slot, at, :]
            others = other[slot, at, :].astype(F32)
            first_add = jnp.where(section == 0, mine, others)
            second_add = jnp.where(section == 0, others, mine)
            first = (source[0, section, slot].astype(F32) + first_add).astype(BF16)
            second = (first.astype(F32) + second_add).astype(BF16)
            leaving[slot, at, :] = jnp.where(section == 0, first, second)
            final[slot, at, :] = second
            value = second.astype(F32)
            upstream = source[1, section, slot].astype(F32) * gain[:, at_multiple(2 * outer + (core ^ slot), width)]
            squares += jnp.sum(value * value, axis=1, keepdims=True)
            products += jnp.sum(value * upstream, axis=1, keepdims=True)
        lane = lax.broadcasted_iota(jnp.int32, (own_rows, sums.shape[1]), 1)
        sums[at, :] = jnp.where(lane < sums.shape[1] // 2, squares, products)


def later_kernel(place, here, arrived, update, before, leaving, own, sent):
    section = place[3]
    own_rows = here.shape[3]
    for group, (source, out) in enumerate(((here, own), (arrived, sent))):
        at = pl.ds(group * own_rows, own_rows)
        for slot in range(2):
            start = source[0, 1 - section, slot].astype(F32)
            entering = (start + before[slot, at, :].astype(F32)).astype(BF16).astype(F32)
            entering = jnp.where(section == 0, start, entering)
            out[0, slot] = leaving[slot, at, :]
            out[1, slot] = (entering + update[1, slot, at, :]).astype(BF16)


def norm_kernel(place, here, arrived, gain, final, sums, other_sums, grad):
    outer, core, section = place[1], place[2], place[3]
    own_rows, width = here.shape[3:]
    lanes = sums.shape[1]
    for group, source in enumerate((here, arrived)):
        at = pl.ds(group * own_rows, own_rows)
        total = sums[at, :] + other_sums[pl.ds((1 - group) * own_rows, own_rows), :]
        total = total * (1.0 / (4 * width))
        scale = lax.rsqrt(total[:, :1] + 1e-05)
        shrink = scale * scale * total[:, lanes // 2 : lanes // 2 + 1]
        for slot in range(2):
            upstream = source[1, section, slot].astype(F32) * gain[:, at_multiple(2 * outer + (core ^ slot), width)]
            value = final[slot, at, :].astype(F32)
            grad[slot, at, :] = (scale * (upstream - value * shrink)).astype(BF16)


def join_kernel(place, mid, farthest, last):
    last[...] = mid[...] + farthest[...]


def project_kernel(place, own_mix, other_mix, w00, w01, w10, w11, right, own_half, other_half, *refs):
    own, next_one, *sums, mix_rows, left_rows, piece, inner, turned = refs
    cuts = ((w00, w01), (w10, w11))
    t, outer, core, section = place[0], place[1], place[2], place[3]
    micro, shards = mix_rows.shape[0], 4
    sub, half = own_half.shape[1:]
    step = pl.program_id(0)
    rows = own.shape[2]
    own_rows = rows // 2
    size = shards * rows
    depth, tile = w00.shape

    @pl.when(step == 0)
    def _():
        for m in range(micro):
            for r in range(shards):
                at = pl.ds(pl.multiple_of((t ^ r) * own_rows, own_rows), own_rows)
                for group, source in enumerate((own_mix, other_mix)):
                    mix_rows[m, pl.ds(r * rows + group * own_rows, own_rows), :] = source[m ^ section, at, :]
        product = jnp.dot(
            mix_rows[...].reshape(micro * size, -1), right[...], preferred_element_type=F32
        )
        inner[...] = product.astype(BF16)
        width = left_rows.shape[2]
        for o in range(shards):
            lines = [
                product[m * size + (r ^ o) * rows :][:rows] for m in range(micro) for r in range(shards)
            ]
            turned[...] = jnp.concatenate(lines, axis=0).T
            cut = turned[at_multiple(t ^ o, sub), :].astype(BF16)
            for m in range(micro):
                beside = cut[:, m * size : (m + 1) * size]
                if o == 0:
                    piece[m] = beside
                elif o == 1:
                    next_one[0, m, :, pl.ds(width, size)] = beside
                    next_one[1, m, :, pl.ds(width, size)] = jnp.zeros_like(beside)
                else:
                    sums[(o - 2) * micro][m, :, pl.ds(width, size)] = beside
        left_rows[...] = jnp.zeros_like(left_rows)
        for slot in range(2):
            part = core ^ slot
            at = pl.ds(pl.multiple_of((2 * outer + part) * sub, sub), sub)
            left_rows[slot, at, pl.ds(pl.multiple_of(core * half, half), half)] = own_half[part]
            left_rows[slot, at, pl.ds(pl.multiple_of((1 - core) * half, half), half)] = other_half[part]

    at = pl.ds(pl.multiple_of(step * tile, tile), tile)
    lines = mix_rows[...].reshape(micro * size, -1)
    for slot in range(2):
        product = jnp.dot(inner[...], left_rows[slot, :, at], preferred_element_type=F32)
        for i, weight in enumerate(cuts[slot]):
            product += jnp.dot(
                lines[:, i * depth : (i + 1) * depth], weight[...], preferred_element_type=F32
            )
        for m in range(micro):
            for r in range(shards):
                at_row = m * size + r * rows
                value = product[at_row : at_row + rows].astype(BF16)
                if r == 0:
                    own[m, slot] = value
                elif r == 1:
                    next_one[m, slot, :, at] = value
                else:
                    sums[(r - 2) * micro + m][slot, :, at] = value


def doubled(weights):
    return [weights[0], weights[0], weights[1], weights[1]]


def weight_specs(head_cols, tile):
    return [
        pl.BlockSpec((head_cols // 2, tile), lambda i: (0, i)),
        pl.BlockSpec((head_cols // 2, tile), lambda i: (1, i)),
    ] * 2


def whole(*shape):
    return pl.BlockSpec(shape, lambda i: (0,) * len(shape))


def project(place, own_mix, other_mix, weights, right, own_half, other_half):
    micro, tokens, head_cols = own_mix.shape
    width = weights[0].shape[1]
    rank = right.shape[1]
    tile = 512
    tiles = width // tile
    rows = tokens // 2
    size = 4 * rows
    carrying = (2, rows, width + size)
    plain = (2, rows, width)
    shapes = [(micro, *carrying)] + [carrying, *[plain] * (micro - 1)] * 2
    shapes += [(micro, size, head_cols), (2, rank, width), (2, rank // 4, size)]
    return pl.pallas_call(
        project_kernel,
        grid=(tiles,),
        in_specs=[
            pl.BlockSpec(memory_space=pltpu.SMEM),
            whole(*own_mix.shape),
            whole(*own_mix.shape),
            *weight_specs(head_cols, tile),
            whole(*right.shape),
            whole(*own_half.shape),
            whole(*own_half.shape),
        ],
        out_specs=[pl.BlockSpec((micro, 2, rows, tile), lambda i: (0, 0, 0, i))]
        + [whole(*shape) for shape in shapes],
        out_shape=[jax.ShapeDtypeStruct((micro, 2, rows, width), BF16)]
        + [jax.ShapeDtypeStruct(shape, BF16) for shape in shapes],
        scratch_shapes=[
            pltpu.VMEM((micro * size, rank), BF16),
            pltpu.VMEM((rank, micro * size), F32),
        ],
        compiler_params=pltpu.CompilerParams(vmem_limit_bytes=VMEM_ALL),
        cost_estimate=NO_COST,
    )(place, own_mix, other_mix, *doubled(weights), right, own_half, other_half)


def back_kernel(micro, place, *refs):
    pieces, refs = refs[: 4 * micro], refs[4 * micro :]
    cuts, refs = (refs[0:2], refs[2:4]), refs[4:]
    left_rows, right, mix_rows = refs[:3]
    (own_piece, beside_piece, crossed_piece, relayed_piece, mid_piece), refs = refs[3:8], refs[8:]
    mix_here, mix_sent, *factors, total, inner_grad, permuted, right_all = refs
    rank = permuted.shape[0]
    t, outer, core, section = place[0], place[1], place[2], place[3]
    step = pl.program_id(0)
    rows = pieces[0].shape[1]
    own_rows = rows // 2
    depth, tile = cuts[0][0].shape
    half = factors[0].shape[1]

    @pl.when(step == 0)
    def _():
        total[...] = jnp.zeros_like(total)
        inner_grad[...] = jnp.zeros_like(inner_grad)
        _, sub, size = own_piece.shape
        for m in range(micro):
            cut = pl.ds(m * size, size)
            last = mid_piece[m] + relayed_piece[m]
            for o, value in enumerate((own_piece[m], beside_piece[0, m], crossed_piece[m], last)):
                permuted[at_multiple(t ^ o, sub), cut] = value

    grads = []
    for slot in range(2):
        parts = []
        for m in range(micro):
            parts += [piece[slot] for piece in pieces[4 * m : 4 * m + 4]]
        grads.append(jnp.concatenate(parts, axis=0))
    over = (((1,), (1,)), ((), ()))
    for i in range(2):
        total[pl.ds(i * depth, depth), :] += lax.dot_general(
            cuts[0][i][...], grads[0], over, preferred_element_type=F32
        ) + lax.dot_general(cuts[1][i][...], grads[1], over, preferred_element_type=F32)
    inner_grad[...] += lax.dot_general(
        grads[0], left_rows[0], over, preferred_element_type=F32
    ) + lax.dot_general(grads[1], left_rows[1], over, preferred_element_type=F32)

    at = step * tile
    cut = pl.ds(pl.multiple_of(at % half, tile), tile)
    block = jnp.where(((t & 1) ^ core) == 0, grads[0], grads[1])
    product = jnp.dot(permuted[...], block, preferred_element_type=F32)
    for i, factor in enumerate(factors):

        @pl.when((at // half) ^ core == i)
        def _():
            factor[:rank, cut] = product


    @pl.when(step == pl.num_programs(0) - 1)
    def _():
        mine = inner_grad[...].astype(BF16)
        everything = total[...].T + lax.dot_general(
            mine, right[...], over, preferred_element_type=F32
        )
        for m in range(micro):
            for r in range(4):
                at = at_multiple(t ^ r, own_rows)
                lines = everything[(4 * m + r) * rows :][:rows]
                mix_here[m ^ section, at, :] = lines[:own_rows]
                mix_sent[m ^ section, at, :] = lines[own_rows:].astype(BF16)
        right_all[...] = lax.dot_general(
            mine,
            mix_rows[...].reshape(mine.shape[0], -1),
            (((0,), (0,)), ((), ())),
            preferred_element_type=F32,
        )
        for i in range(2):
            factors[i][rank:, :] = right_all[at_multiple(outer, rank // 2), :]


def back(place, pieces, weights, left_rows, right, mix_rows, permuted):
    _, rows, width = pieces[0].shape
    head_cols, rank = right.shape
    micro, size, _ = mix_rows.shape
    half = width // 2
    tile = 512
    tiles = width // tile
    shapes = [
        jax.ShapeDtypeStruct((micro, size // 2, head_cols), F32),
        jax.ShapeDtypeStruct((micro, size // 2, head_cols), BF16),
        jax.ShapeDtypeStruct((rank + rank // 2, half), F32),
        jax.ShapeDtypeStruct((rank + rank // 2, half), F32),
    ]
    return pl.pallas_call(
        functools.partial(back_kernel, micro),
        grid=(tiles,),
        in_specs=[pl.BlockSpec(memory_space=pltpu.SMEM)]
        + [pl.BlockSpec((2, rows, tile), lambda i: (0, 0, i))] * (4 * micro)
        + weight_specs(head_cols, tile)
        + [
            pl.BlockSpec((2, rank, tile), lambda i: (0, 0, i)),
            whole(*right.shape),
            whole(*mix_rows.shape),
        ]
        + [
            whole(*permuted[0].shape),
            pl.BlockSpec((1, 2, rows, size), lambda i: (0, 0, 0, width // size)),
            pl.BlockSpec((2, rows, size), lambda i: (0, 0, width // size)),
            pl.BlockSpec((2, rows, size), lambda i: (0, 0, width // size + 1)),
            pl.BlockSpec((2, rows, size), lambda i: (0, 0, width // size)),
        ],
        out_specs=[whole(*shape.shape) for shape in shapes],
        out_shape=shapes,
        scratch_shapes=[
            pltpu.VMEM((head_cols, micro * size), F32),
            pltpu.VMEM((micro * size, rank), F32),
            pltpu.VMEM((rank, micro * size), BF16),
            pltpu.VMEM((rank, head_cols), F32),
        ],
        compiler_params=pltpu.CompilerParams(vmem_limit_bytes=VMEM_ALL),
        cost_estimate=NO_COST,
    )(place, *pieces, *doubled(weights), left_rows, right, mix_rows, *permuted)


def gather_kernel(place, here, arrived, out):
    outer, core, section = place[1], place[2], place[3]
    width = arrived.shape[3]
    for m in range(here.shape[0]):
        for slot in range(2):
            part = core ^ slot
            at = pl.ds(pl.multiple_of((2 * outer + part) * width, width), width)
            out[m ^ section, :, at] = here[m, slot]
            at = pl.ds(pl.multiple_of((2 * (1 - outer) + part) * width, width), width)
            out[m ^ section, :, at] = arrived[m, slot]


def left_kernel(place, own_left, other_left, grad_left):
    core = place[2]
    half = own_left.shape[1]
    grad_left[:, pl.ds(pl.multiple_of(core * half, half), half)] = own_left[...].astype(F32)
    grad_left[:, pl.ds(pl.multiple_of((1 - core) * half, half), half)] = other_left[...].astype(F32)


def right_kernel(place, own_right, other_right, grad_right, wide):
    outer = place[1]
    rank = wide.shape[0]
    wide[at_multiple(outer, rank // 2), :] = own_right[rank:, :].astype(F32)
    wide[at_multiple(1 - outer, rank // 2), :] = other_right[rank:, :].astype(F32)
    grad_right[...] = wide[...].T


def on_device(mix, hidden_in, cotangent, frozen_weight, right_factor, left_factor, norm_gain):
    t = lax.axis_index("tensor")
    d = lax.axis_index("dp")
    section = lax.axis_index("pipe")
    outer = d // 2
    core = d % 2
    place = jnp.stack([t, outer, core, section]).astype(jnp.int32)

    def to_core(value):
        return lax.ppermute(value, "dp", [(i, i ^ 1) for i in range(4)])

    def to_outer(value):
        return lax.ppermute(value, "dp", [(i, i ^ 2) for i in range(4)])

    def along(value, *pairs):
        return lax.ppermute(value, "tensor", pairs)

    mixes = mix[0, :, 0]
    micro, tokens, head_cols = mixes.shape
    own_rows = tokens // 4
    rows = 2 * own_rows
    weight = frozen_weight[0]
    right = right_factor[0, 0]
    left = left_factor[0, 0]
    rank, width = left.shape
    sub = rank // 4
    half = width // 2
    features = 4 * width
    slots = (d, d ^ 1)

    other_mixes = to_outer(mixes)
    weights = (weight, to_core(weight))

    def swapped(values):
        return [values[0]] + [along(values[o], *[(i, i ^ o) for i in range(4)]) for o in (1, 2, 3)]

    def of_block(values, block):
        return lax.select_n(t ^ block, *values)

    cut = [
        lax.dynamic_slice(left, ((t ^ o) * sub, core * half), (sub, half)) for o in range(4)
    ]
    met = swapped(cut)
    own_half = jnp.stack([of_block(met, 2 * outer + i) for i in range(2)])
    other_half = to_core(own_half)

    own, next_one, *partial, mix_rows, left_rows, own_piece = project(
        place, mixes, other_mixes, weights, right, own_half, other_half
    )

    swaps = [[(i, i ^ o) for i in range(4)] for o in range(4)]
    shape = (2, rows, width)
    passed, mids, crossings = [], [], []
    for m in range(micro):
        last = partial[micro + m]
        passed.append(along(last, (0, 1), (3, 2)))
        mids.append(along(last, (1, 2), (2, 1)))
    for m in range(micro):
        two_away = partial[m]
        carried = two_away.shape[2] - width
        (ahead,) = small(
            ahead_kernel,
            [((2, rows, width + 2 * carried), BF16)],
            [],
            place,
            two_away,
            after(passed[m], *mids, *passed),
        )
        crossings.append(along(ahead, *swaps[2]))
    beside = along(next_one, *swaps[1])
    permuted = (own_piece, beside, crossings[0], crossings[0], mids[0])

    layout = (2, micro, 2, own_rows, width)
    here, there = small(
        cut_kernel,
        [(layout, BF16)] * 2,
        [],
        place,
        after(hidden_in[:, 0], own),
        cotangent[:, 0],
    )
    arrived = to_outer(there)
    gain = norm_gain.astype(F32).reshape(1, features)

    update, kept, sent = small(
        update_kernel,
        [((micro, *shape), F32), (shape, BF16), (shape, BF16)],
        [],
        place,
        own,
        after(beside, arrived),
        *mids,
        *crossings,
    )

    def to_section(value):
        return lax.ppermute(value, "pipe", [(0, 1), (1, 0)])

    leaving, final, sums = small(
        state_kernel,
        [(shape, BF16)] * 2 + [((rows, 128), F32)],
        [],
        place,
        here,
        arrived,
        gain,
        update,
        to_section(sent),
    )
    (grad,) = small(
        norm_kernel, [(shape, BF16)], [], place, here, arrived, gain, final, sums, to_outer(sums)
    )

    opposite = along(grad, *swaps[2])
    beside = along(grad, *swaps[1])
    before = to_section(after(kept, final))
    own_there = to_section(after(grad, before))
    relay = after(opposite, own_there, beside)
    mid = along(after(grad, beside), (1, 2), (2, 1))
    farthest = along(relay, (1, 0), (2, 3))
    opposite_there = to_section(opposite)
    by_group, others = small(
        later_kernel,
        [((micro, 2, own_rows, width), BF16)] * 2,
        [],
        place,
        here,
        arrived,
        update,
        before,
        leaving,
    )
    others = to_outer(others)
    beside_there = to_section(after(beside, others))
    (section_out,) = small(
        gather_kernel, [((micro, own_rows, features), BF16)], [], place, by_group, others
    )
    (last,) = small(
        join_kernel, [(shape, BF16)], [], place, mid, after(farthest, beside_there)
    )
    pieces = [grad, beside, relay, last]
    pieces += [own_there, beside_there, opposite_there, to_section(after(last, opposite_there))]
    mix_here, mix_sent, kept_factors, sent_factors = back(
        place, pieces, weights, left_rows, right, mix_rows, permuted
    )
    joined = (kept_factors + to_core(sent_factors)).astype(BF16)
    other_joined = to_outer(joined)
    best = jnp.where(outer == t // 2, joined[:rank], other_joined[:rank])
    (grad_right,) = small(
        right_kernel,
        [((head_cols, rank), F32)],
        [pltpu.VMEM((rank, head_cols), F32)],
        place,
        joined,
        other_joined,
    )
    (grad_left,) = small(
        left_kernel, [((rank, width), F32)], [], place, best, after(to_core(best), grad_right)
    )
    grad_mix = (mix_here + after(to_outer(mix_sent), grad_left).astype(F32)).astype(BF16)
    grad_mix = grad_mix.reshape(1, micro, 1, tokens, head_cols)

    return (
        section_out.reshape(1, micro, 1, own_rows, features),
        grad_mix,
        grad_right.reshape(1, 1, head_cols, rank),
        grad_left.reshape(1, 1, rank, width),
    )


def on_device_general(mix, hidden_in, cotangent, frozen_weight, right_factor, left_factor, norm_gain):
    blocks = lax.axis_size("tensor")
    parts = lax.axis_size("dp")
    sections = lax.axis_size("pipe")
    t = lax.axis_index("tensor")
    d = lax.axis_index("dp")
    section = lax.axis_index("pipe")
    outers = parts // 2
    outer = d // 2
    core = d % 2

    def to_core(value):
        return lax.ppermute(value, "dp", [(i, i ^ 1) for i in range(parts)])

    def to_outer(value, step):
        return lax.ppermute(value, "dp", [(i, (i + 2 * step) % parts) for i in range(parts)])

    def to_block(value, step):
        return lax.ppermute(value, "tensor", [(i, (i + step) % blocks) for i in range(blocks)])

    def of_cores(value):
        return jnp.where(core == 0, value, value[::-1])

    mixes = mix[0, :, 0]
    micro, tokens, head_cols = mixes.shape
    own_rows = tokens // blocks
    weight = frozen_weight[0]
    right = right_factor[0, 0]
    left = left_factor[0, 0]
    rank, block_cols = left.shape
    sub = rank // blocks
    width = weight.shape[1]
    features = width * parts
    rows = outers * own_rows
    all_rows = blocks * rows
    per_block = parts // blocks
    slots = (d, d ^ 1)

    def block_of(part):
        return part // per_block

    weights = (weight, to_core(weight))
    own = mixes.reshape(micro, blocks, 1, own_rows, head_cols)
    taken = [
        jnp.concatenate(
            [own[m]] + [to_outer(own[m], step) for step in range(1, outers)], axis=1
        ).reshape(all_rows, head_cols)
        for m in range(micro)
    ]
    own_inner = dot(right, mixes.reshape(micro * tokens, head_cols), 0, 1).astype(BF16)
    pieces = lax.all_to_all(
        jnp.concatenate(
            [
                left.reshape(blocks, sub, block_cols),
                own_inner.reshape(blocks, sub, micro * tokens),
            ],
            axis=2,
        ),
        "tensor",
        split_axis=0,
        concat_axis=0,
        tiled=True,
    )
    left_slots = [
        columns(pick(pieces, block_of(part)), (part % per_block) * width, width) for part in slots
    ]
    right_slots = [columns(right, block_of(part) * sub, sub) for part in slots]
    own_permuted = pieces[:, :, block_cols:].reshape(rank, micro * tokens)
    own_permuted = after(own_permuted, *taken)
    permuted = [own_permuted] + [to_outer(own_permuted, step) for step in range(1, outers)]

    inners = [dot(taken[m], right, 1, 0).astype(BF16) for m in range(micro)]
    partial = [
        jnp.stack(
            [
                (
                    dot(taken[m], weights[slot], 1, 0)
                    + dot(
                        columns(inners[m], block_of(part) * sub, sub), left_slots[slot], 1, 0
                    )
                ).astype(BF16)
                for slot, part in enumerate(slots)
            ]
        ).reshape(2, blocks, rows, width)
        for m in range(micro)
    ]

    def shard(m, index):
        return pick(partial[m], index, 1)

    updates_here = []
    for m in range(micro):
        total = shard(m, t).astype(F32)
        for step in range(1, blocks):
            total = total + to_block(shard(m, (t + step) % blocks), step).astype(F32)
        updates_here.append(total)

    hidden_late = after(hidden_in, *taken)

    def by_column(step):
        target = (outer + step) % outers
        cuts = [2 * target + core, 2 * target + (1 - core)]
        return jnp.stack(
            [
                jnp.stack([columns(value[:, 0], part * width, width) for part in cuts])
                for value in (hidden_late, cotangent)
            ]
        )

    entering = jnp.concatenate(
        [by_column(0)] + [to_outer(by_column(step), step) for step in range(1, outers)], axis=3
    )
    gains = jnp.stack([columns(norm_gain, part * width, width) for part in slots]).astype(F32)

    grads = []
    leaving = []
    for m in range(micro):
        sent = updates_here[m].astype(BF16)
        updates = [updates_here[m]] + [
            lax.ppermute(
                sent, "pipe", [(i, (i + step) % sections) for i in range(sections)]
            ).astype(F32)
            for step in range(1, sections)
        ]
        state = entering[0, :, m]
        kept = state
        for s in range(sections):
            add = updates[0]
            for step in range(1, sections):
                add = jnp.where((section - step) % sections == s, updates[step], add)
            state = (state.astype(F32) + add).astype(BF16)
            kept = jnp.where(section == s, state, kept)
        leaving.append(kept)
        final = state.astype(F32)
        upstream = entering[1, :, m].astype(F32) * gains[:, None, :]
        sums = jnp.stack(
            [jnp.sum(final * final, axis=(0, 2)), jnp.sum(upstream * final, axis=(0, 2))]
        ).reshape(2, outers, own_rows)
        total = sums
        for step in range(1, outers):
            total = total + jnp.roll(to_outer(sums, step), step, axis=1)
        total = total.reshape(2, rows) / features
        scale = lax.rsqrt(total[0] + 1e-05)
        shrink = scale * scale * total[1]
        grads.append(
            (scale[None, :, None] * (upstream - final * shrink[None, :, None])).astype(BF16)
        )

    full = [
        jnp.concatenate(
            [grads[m]] + [to_block(grads[m], step) for step in range(1, blocks)], axis=1
        )
        for m in range(micro)
    ]
    order = [[(t - step) % blocks for step in range(blocks)]] * micro

    outs = []
    for m in range(micro):
        by_group = after(leaving[m], grads[m]).reshape(2, outers, own_rows, width)
        row = jnp.zeros((own_rows, features), BF16)
        for step in range(outers):
            at = (outer + step) % outers
            piece = by_group[:, step]
            if step:
                piece = after(to_outer(piece, outers - step), full[-1])
            for slot in range(2):
                place = (2 * at + (core if slot == 0 else 1 - core)) * width
                row = lax.dynamic_update_slice_in_dim(row, piece[slot], place, 1)
        outs.append(row)
    section_out = jnp.stack(outs).reshape(1, micro, 1, own_rows, features)

    mix_rows = [
        jnp.concatenate(
            [pick(taken[m].reshape(blocks, rows, head_cols), at) for at in order[m]], axis=0
        )
        for m in range(micro)
    ]
    permuted_rows = [
        jnp.concatenate(
            [
                columns(half, m * tokens + at * own_rows, own_rows)
                for at in order[m]
                for half in permuted
            ],
            axis=1,
        )
        for m in range(micro)
    ]

    holder = (t * per_block) // 2
    mix_grads = []
    right_sum = 0.0
    left_sum = 0.0
    for m in range(micro):
        if per_block == 1:
            cols = pick(full[m], jnp.where(t % 2 == core, 0, 1))
        else:
            cols = jnp.concatenate(list(of_cores(full[m])), axis=1)
        left_sum = left_sum + dot(permuted_rows[m], cols, 1, 0)

        inner_grads = [
            dot(full[m][slot], left_slots[slot], 1, 1).astype(BF16) for slot in range(2)
        ]
        if per_block == 1:
            mine = jnp.concatenate(inner_grads, axis=1)
            right_here = jnp.concatenate(right_slots, axis=1)
        else:
            mine = (inner_grads[0].astype(F32) + inner_grads[1].astype(F32)).astype(BF16)
            right_here = right_slots[0]
        right_sum = right_sum + dot(mine, mix_rows[m], 0, 0)

        partial_mix = (
            dot(full[m][0], weights[0], 1, 1)
            + dot(full[m][1], weights[1], 1, 1)
            + dot(mine, right_here, 1, 1)
        ).reshape(blocks, outers, own_rows, head_cols)
        whole = partial_mix[:, 0]
        for step in range(1, outers):
            whole = whole + to_outer(partial_mix[:, step].astype(BF16), outers - step).astype(F32)
        whole = whole.astype(BF16)
        back = order[m]
        mix_grads.append(
            jnp.concatenate([pick(whole, at) for at in back], axis=0)
        )
    grad_mix = jnp.stack(mix_grads).reshape(1, micro, 1, tokens, head_cols)

    half = block_cols // 2
    half_sum = (
        columns(left_sum, core * half, half) + to_core(columns(left_sum, (1 - core) * half, half))
    ).astype(BF16)
    best = half_sum
    for step in range(1, outers):
        pairs = []
        for i in range(blocks):
            at = (i * per_block) // 2
            for c in range(2):
                pairs.append(
                    (i * parts + 2 * at + c, i * parts + 2 * ((at + step) % outers) + c)
                )
        arrived = lax.ppermute(half_sum, ("tensor", "dp"), pairs)
        best = jnp.where((outer - holder) % outers == step, arrived, best)
    there = to_core(best)
    grad_left = jnp.concatenate(list(of_cores(jnp.stack([best, there]))), axis=1).astype(F32)

    if per_block == 1:
        right_sum = of_cores(right_sum.reshape(2, sub, head_cols)).reshape(2 * sub, head_cols)
    right_sum = (right_sum + to_core(right_sum)).astype(BF16)
    wide = jnp.zeros((rank, head_cols), BF16)
    count = right_sum.shape[0]
    for step in range(outers):
        arrived = to_outer(right_sum, step) if step else right_sum
        wide = lax.dynamic_update_slice_in_dim(
            wide, arrived, ((outer - step) % outers) * count, 0
        )
    grad_right = wide.T.astype(F32)

    return (
        section_out,
        grad_mix,
        grad_right.reshape(1, 1, head_cols, rank),
        grad_left.reshape(1, 1, rank, block_cols),
    )


def solution(mesh):
    sizes = (mesh.shape["tensor"], mesh.shape["dp"], mesh.shape["pipe"])
    return jax.shard_map(
        on_device if sizes == (4, 4, 2) else on_device_general,
        mesh=mesh,
        in_specs=(
            P("pipe", None, "dp", None, "tensor"),
            P(None, "dp", "tensor", None),
            P(None, "dp", "tensor", None),
            P("pipe", "tensor", "dp"),
            P("pipe", "tensor", None, None),
            P("pipe", "tensor", None, None),
            P(),
        ),
        out_specs=(
            P("pipe", None, "dp", "tensor", None),
            P("pipe", None, "dp", None, "tensor"),
            P("pipe", "tensor", None, None),
            P("pipe", "tensor", None, None),
        ),
        check_vma=False,
    )
```

```python
import functools

import jax
import jax.numpy as jnp
from jax import lax
from jax.experimental import pallas as pl
from jax.experimental.pallas import tpu as pltpu
from jax.sharding import PartitionSpec as P

F32 = jnp.float32
BF16 = jnp.bfloat16
VMEM = 24 * 2**20
VMEM_ALL = 48 * 2**20
VMEM_SMALL = 10 * 2**20


def dot(left_side, right_side, left_dim, right_dim):
    return lax.dot_general(
        left_side,
        right_side,
        (((left_dim,), (right_dim,)), ((), ())),
        preferred_element_type=F32,
    )


def pick(value, index, dim=0):
    return lax.dynamic_index_in_dim(value, index, dim, keepdims=False)


def columns(value, start, size):
    return lax.dynamic_slice_in_dim(value, start, size, value.ndim - 1)


def after(value, *others):
    return lax.optimization_barrier((value, *others))[0]


NO_COST = pl.CostEstimate(flops=0, bytes_accessed=0, transcendentals=0)


def small(kernel, outs, scratch, place, *values, cost=NO_COST):
    vmem = pl.BlockSpec(memory_space=pltpu.VMEM)
    return pl.pallas_call(
        kernel,
        in_specs=[pl.BlockSpec(memory_space=pltpu.SMEM)] + [vmem] * len(values),
        out_specs=[vmem] * len(outs),
        out_shape=[jax.ShapeDtypeStruct(shape, dtype) for shape, dtype in outs],
        scratch_shapes=scratch,
        compiler_params=pltpu.CompilerParams(vmem_limit_bytes=VMEM_SMALL),
        cost_estimate=cost,
    )(place, *values)


def at_multiple(index, size):
    return pl.ds(pl.multiple_of(index * size, size), size)


def cut_kernel(place, hidden, cotangent, here, there):
    outer, core = place[1], place[2]
    width = here.shape[4]
    for out, target in ((here, outer), (there, 1 - outer)):
        for which, source in enumerate((hidden, cotangent)):
            for m in range(source.shape[0]):
                for slot in range(2):
                    out[which, m, slot] = source[m, :, at_multiple(2 * target + (core ^ slot), width)]


def ahead_kernel(place, two_away, passed, ahead):
    carried = ahead.shape[2] - two_away.shape[2]
    width = two_away.shape[2] - carried
    ahead[:, :, :width] = (
        two_away[:, :, :width].astype(F32) + passed[:, :, :width].astype(F32)
    ).astype(BF16)
    if carried:
        ahead[:, :, width : width + carried] = two_away[:, :, width:]
        ahead[:, :, width + carried :] = passed[:, :, width:]


def update_kernel(place, own, beside, *refs):
    micro, _, _, width = own.shape
    mids, crossings, (update, kept, sent) = refs[:micro], refs[micro : 2 * micro], refs[2 * micro :]
    for m in range(micro):
        total = (own[m].astype(F32) + beside[m, :, :, :width].astype(F32)) + (
            mids[m][:, :, :width].astype(F32) + crossings[m][:, :, :width].astype(F32)
        )
        update[m] = total
        (sent if m else kept)[...] = total.astype(BF16)


def state_kernel(place, here, arrived, gain, update, other, leaving, final, sums):
    outer, core, section = place[1], place[2], place[3]
    own_rows, width = here.shape[3:]
    for group, source in enumerate((here, arrived)):
        at = pl.ds(group * own_rows, own_rows)
        squares = jnp.zeros((own_rows, 1), F32)
        products = jnp.zeros((own_rows, 1), F32)
        for slot in range(2):
            mine = update[0, slot, at, :]
            others = other[slot, at, :].astype(F32)
            first_add = jnp.where(section == 0, mine, others)
            second_add = jnp.where(section == 0, others, mine)
            first = (source[0, section, slot].astype(F32) + first_add).astype(BF16)
            second = (first.astype(F32) + second_add).astype(BF16)
            leaving[slot, at, :] = jnp.where(section == 0, first, second)
            final[slot, at, :] = second
            value = second.astype(F32)
            upstream = source[1, section, slot].astype(F32) * gain[:, at_multiple(2 * outer + (core ^ slot), width)]
            squares += jnp.sum(value * value, axis=1, keepdims=True)
            products += jnp.sum(value * upstream, axis=1, keepdims=True)
        lane = lax.broadcasted_iota(jnp.int32, (own_rows, sums.shape[1]), 1)
        sums[at, :] = jnp.where(lane < sums.shape[1] // 2, squares, products)


def later_kernel(place, here, arrived, update, before, leaving, own, sent):
    section = place[3]
    own_rows = here.shape[3]
    for group, (source, out) in enumerate(((here, own), (arrived, sent))):
        at = pl.ds(group * own_rows, own_rows)
        for slot in range(2):
            start = source[0, 1 - section, slot].astype(F32)
            entering = (start + before[slot, at, :].astype(F32)).astype(BF16).astype(F32)
            entering = jnp.where(section == 0, start, entering)
            out[0, slot] = leaving[slot, at, :]
            out[1, slot] = (entering + update[1, slot, at, :]).astype(BF16)


def norm_kernel(place, here, arrived, gain, final, sums, other_sums, grad):
    outer, core, section = place[1], place[2], place[3]
    own_rows, width = here.shape[3:]
    lanes = sums.shape[1]
    for group, source in enumerate((here, arrived)):
        at = pl.ds(group * own_rows, own_rows)
        total = sums[at, :] + other_sums[pl.ds((1 - group) * own_rows, own_rows), :]
        total = total * (1.0 / (4 * width))
        scale = lax.rsqrt(total[:, :1] + 1e-05)
        shrink = scale * scale * total[:, lanes // 2 : lanes // 2 + 1]
        for slot in range(2):
            upstream = source[1, section, slot].astype(F32) * gain[:, at_multiple(2 * outer + (core ^ slot), width)]
            value = final[slot, at, :].astype(F32)
            grad[slot, at, :] = (scale * (upstream - value * shrink)).astype(BF16)


def join_kernel(place, mid, farthest, last):
    last[...] = mid[...] + farthest[...]


def project_kernel(place, own_mix, other_mix, w00, w01, w10, w11, right, own_half, other_half, *refs):
    own, next_one, *sums, mix_rows, left_rows, piece, inner, turned = refs
    cuts = ((w00, w01), (w10, w11))
    t, outer, core, section = place[0], place[1], place[2], place[3]
    micro, shards = mix_rows.shape[0], 4
    sub, half = own_half.shape[1:]
    step = pl.program_id(0)
    rows = own.shape[2]
    own_rows = rows // 2
    size = shards * rows
    depth, tile = w00.shape

    @pl.when(step == 0)
    def _():
        for m in range(micro):
            for r in range(shards):
                at = pl.ds(pl.multiple_of((t ^ r) * own_rows, own_rows), own_rows)
                for group, source in enumerate((own_mix, other_mix)):
                    mix_rows[m, pl.ds(r * rows + group * own_rows, own_rows), :] = source[m ^ section, at, :]
        product = jnp.dot(
            mix_rows[...].reshape(micro * size, -1), right[...], preferred_element_type=F32
        )
        inner[...] = product.astype(BF16)
        width = left_rows.shape[2]
        for o in range(shards):
            lines = [
                product[m * size + (r ^ o) * rows :][:rows] for m in range(micro) for r in range(shards)
            ]
            turned[...] = jnp.concatenate(lines, axis=0).T
            cut = turned[at_multiple(t ^ o, sub), :].astype(BF16)
            for m in range(micro):
                beside = cut[:, m * size : (m + 1) * size]
                if o == 0:
                    piece[m] = beside
                elif o == 1:
                    next_one[0, m, :, pl.ds(width, size)] = beside
                    next_one[1, m, :, pl.ds(width, size)] = jnp.zeros_like(beside)
                else:
                    sums[(o - 2) * micro][m, :, pl.ds(width, size)] = beside
        left_rows[...] = jnp.zeros_like(left_rows)
        for slot in range(2):
            part = core ^ slot
            at = pl.ds(pl.multiple_of((2 * outer + part) * sub, sub), sub)
            left_rows[slot, at, pl.ds(pl.multiple_of(core * half, half), half)] = own_half[part]
            left_rows[slot, at, pl.ds(pl.multiple_of((1 - core) * half, half), half)] = other_half[part]

    at = pl.ds(pl.multiple_of(step * tile, tile), tile)
    lines = mix_rows[...].reshape(micro * size, -1)
    for slot in range(2):
        product = jnp.dot(inner[...], left_rows[slot, :, at], preferred_element_type=F32)
        for i, weight in enumerate(cuts[slot]):
            product += jnp.dot(
                lines[:, i * depth : (i + 1) * depth], weight[...], preferred_element_type=F32
            )
        for m in range(micro):
            for r in range(shards):
                at_row = m * size + r * rows
                value = product[at_row : at_row + rows].astype(BF16)
                if r == 0:
                    own[m, slot] = value
                elif r == 1:
                    next_one[m, slot, :, at] = value
                else:
                    sums[(r - 2) * micro + m][slot, :, at] = value


def doubled(weights):
    return [weights[0], weights[0], weights[1], weights[1]]


def weight_specs(head_cols, tile):
    return [
        pl.BlockSpec((head_cols // 2, tile), lambda i: (0, i)),
        pl.BlockSpec((head_cols // 2, tile), lambda i: (1, i)),
    ] * 2


def whole(*shape):
    return pl.BlockSpec(shape, lambda i: (0,) * len(shape))


def project(place, own_mix, other_mix, weights, right, own_half, other_half):
    micro, tokens, head_cols = own_mix.shape
    width = weights[0].shape[1]
    rank = right.shape[1]
    tile = 512
    tiles = width // tile
    rows = tokens // 2
    size = 4 * rows
    carrying = (2, rows, width + size)
    plain = (2, rows, width)
    shapes = [(micro, *carrying)] + [carrying, *[plain] * (micro - 1)] * 2
    shapes += [(micro, size, head_cols), (2, rank, width), (2, rank // 4, size)]
    return pl.pallas_call(
        project_kernel,
        grid=(tiles,),
        in_specs=[
            pl.BlockSpec(memory_space=pltpu.SMEM),
            whole(*own_mix.shape),
            whole(*own_mix.shape),
            *weight_specs(head_cols, tile),
            whole(*right.shape),
            whole(*own_half.shape),
            whole(*own_half.shape),
        ],
        out_specs=[pl.BlockSpec((micro, 2, rows, tile), lambda i: (0, 0, 0, i))]
        + [whole(*shape) for shape in shapes],
        out_shape=[jax.ShapeDtypeStruct((micro, 2, rows, width), BF16)]
        + [jax.ShapeDtypeStruct(shape, BF16) for shape in shapes],
        scratch_shapes=[
            pltpu.VMEM((micro * size, rank), BF16),
            pltpu.VMEM((rank, micro * size), F32),
        ],
        compiler_params=pltpu.CompilerParams(vmem_limit_bytes=VMEM_ALL),
        cost_estimate=NO_COST,
    )(place, own_mix, other_mix, *doubled(weights), right, own_half, other_half)


def back_kernel(micro, place, *refs):
    pieces, refs = refs[: 4 * micro], refs[4 * micro :]
    cuts, refs = (refs[0:2], refs[2:4]), refs[4:]
    left_rows, right, mix_rows = refs[:3]
    (own_piece, beside_piece, crossed_piece, relayed_piece, mid_piece), refs = refs[3:8], refs[8:]
    mix_here, mix_sent, *factors, total, inner_grad, permuted, right_all = refs
    rank = permuted.shape[0]
    t, outer, core, section = place[0], place[1], place[2], place[3]
    step = pl.program_id(0)
    rows = pieces[0].shape[1]
    own_rows = rows // 2
    depth, tile = cuts[0][0].shape
    half = factors[0].shape[1]

    @pl.when(step == 0)
    def _():
        total[...] = jnp.zeros_like(total)
        inner_grad[...] = jnp.zeros_like(inner_grad)
        _, sub, size = own_piece.shape
        for m in range(micro):
            cut = pl.ds(m * size, size)
            last = mid_piece[m] + relayed_piece[m]
            for o, value in enumerate((own_piece[m], beside_piece[0, m], crossed_piece[m], last)):
                permuted[at_multiple(t ^ o, sub), cut] = value

    grads = []
    for slot in range(2):
        parts = []
        for m in range(micro):
            parts += [piece[slot] for piece in pieces[4 * m : 4 * m + 4]]
        grads.append(jnp.concatenate(parts, axis=0))
    over = (((1,), (1,)), ((), ()))
    for i in range(2):
        total[pl.ds(i * depth, depth), :] += lax.dot_general(
            cuts[0][i][...], grads[0], over, preferred_element_type=F32
        ) + lax.dot_general(cuts[1][i][...], grads[1], over, preferred_element_type=F32)
    inner_grad[...] += lax.dot_general(
        grads[0], left_rows[0], over, preferred_element_type=F32
    ) + lax.dot_general(grads[1], left_rows[1], over, preferred_element_type=F32)

    at = step * tile
    cut = pl.ds(pl.multiple_of(at % half, tile), tile)
    block = jnp.where(((t & 1) ^ core) == 0, grads[0], grads[1])
    product = jnp.dot(permuted[...], block, preferred_element_type=F32)
    for i, factor in enumerate(factors):

        @pl.when((at // half) ^ core == i)
        def _():
            factor[:rank, cut] = product


    @pl.when(step == pl.num_programs(0) - 1)
    def _():
        mine = inner_grad[...].astype(BF16)
        everything = total[...].T + lax.dot_general(
            mine, right[...], over, preferred_element_type=F32
        )
        for m in range(micro):
            for r in range(4):
                at = at_multiple(t ^ r, own_rows)
                lines = everything[(4 * m + r) * rows :][:rows]
                mix_here[m ^ section, at, :] = lines[:own_rows]
                mix_sent[m ^ section, at, :] = lines[own_rows:].astype(BF16)
        right_all[...] = lax.dot_general(
            mine,
            mix_rows[...].reshape(mine.shape[0], -1),
            (((0,), (0,)), ((), ())),
            preferred_element_type=F32,
        )
        for i in range(2):
            factors[i][rank:, :] = right_all[at_multiple(outer, rank // 2), :]


def back(place, pieces, weights, left_rows, right, mix_rows, permuted):
    _, rows, width = pieces[0].shape
    head_cols, rank = right.shape
    micro, size, _ = mix_rows.shape
    half = width // 2
    tile = 512
    tiles = width // tile
    shapes = [
        jax.ShapeDtypeStruct((micro, size // 2, head_cols), F32),
        jax.ShapeDtypeStruct((micro, size // 2, head_cols), BF16),
        jax.ShapeDtypeStruct((rank + rank // 2, half), F32),
        jax.ShapeDtypeStruct((rank + rank // 2, half), F32),
    ]
    return pl.pallas_call(
        functools.partial(back_kernel, micro),
        grid=(tiles,),
        in_specs=[pl.BlockSpec(memory_space=pltpu.SMEM)]
        + [pl.BlockSpec((2, rows, tile), lambda i: (0, 0, i))] * (4 * micro)
        + weight_specs(head_cols, tile)
        + [
            pl.BlockSpec((2, rank, tile), lambda i: (0, 0, i)),
            whole(*right.shape),
            whole(*mix_rows.shape),
        ]
        + [
            whole(*permuted[0].shape),
            pl.BlockSpec((1, 2, rows, size), lambda i: (0, 0, 0, width // size)),
            pl.BlockSpec((2, rows, size), lambda i: (0, 0, width // size)),
            pl.BlockSpec((2, rows, size), lambda i: (0, 0, width // size + 1)),
            pl.BlockSpec((2, rows, size), lambda i: (0, 0, width // size)),
        ],
        out_specs=[whole(*shape.shape) for shape in shapes],
        out_shape=shapes,
        scratch_shapes=[
            pltpu.VMEM((head_cols, micro * size), F32),
            pltpu.VMEM((micro * size, rank), F32),
            pltpu.VMEM((rank, micro * size), BF16),
            pltpu.VMEM((rank, head_cols), F32),
        ],
        compiler_params=pltpu.CompilerParams(vmem_limit_bytes=VMEM),
        cost_estimate=NO_COST,
    )(place, *pieces, *doubled(weights), left_rows, right, mix_rows, *permuted)


def gather_kernel(place, here, arrived, out):
    outer, core, section = place[1], place[2], place[3]
    width = arrived.shape[3]
    for m in range(here.shape[0]):
        for slot in range(2):
            part = core ^ slot
            at = pl.ds(pl.multiple_of((2 * outer + part) * width, width), width)
            out[m ^ section, :, at] = here[m, slot]
            at = pl.ds(pl.multiple_of((2 * (1 - outer) + part) * width, width), width)
            out[m ^ section, :, at] = arrived[m, slot]


def add_kernel(place, here, arrived, total):
    total[...] = (here[...] + arrived[...].astype(F32)).astype(BF16)


def left_kernel(place, own_left, other_left, grad_left):
    core = place[2]
    half = own_left.shape[1]
    grad_left[:, pl.ds(pl.multiple_of(core * half, half), half)] = own_left[...].astype(F32)
    grad_left[:, pl.ds(pl.multiple_of((1 - core) * half, half), half)] = other_left[...].astype(F32)


def right_kernel(place, own_right, other_right, grad_right, wide):
    outer = place[1]
    rank = wide.shape[0]
    wide[at_multiple(outer, rank // 2), :] = own_right[rank:, :].astype(F32)
    wide[at_multiple(1 - outer, rank // 2), :] = other_right[rank:, :].astype(F32)
    grad_right[...] = wide[...].T


def on_device(mix, hidden_in, cotangent, frozen_weight, right_factor, left_factor, norm_gain):
    t = lax.axis_index("tensor")
    d = lax.axis_index("dp")
    section = lax.axis_index("pipe")
    outer = d // 2
    core = d % 2
    place = jnp.stack([t, outer, core, section]).astype(jnp.int32)

    def to_core(value):
        return lax.ppermute(value, "dp", [(i, i ^ 1) for i in range(4)])

    def to_outer(value):
        return lax.ppermute(value, "dp", [(i, i ^ 2) for i in range(4)])

    def along(value, *pairs):
        return lax.ppermute(value, "tensor", pairs)

    mixes = mix[0, :, 0]
    micro, tokens, head_cols = mixes.shape
    own_rows = tokens // 4
    rows = 2 * own_rows
    weight = frozen_weight[0]
    right = right_factor[0, 0]
    left = left_factor[0, 0]
    rank, width = left.shape
    sub = rank // 4
    half = width // 2
    features = 4 * width
    slots = (d, d ^ 1)

    other_mixes = to_outer(mixes)
    weights = (weight, to_core(weight))

    def swapped(values):
        return [values[0]] + [along(values[o], *[(i, i ^ o) for i in range(4)]) for o in (1, 2, 3)]

    def of_block(values, block):
        return lax.select_n(t ^ block, *values)

    cut = [
        lax.dynamic_slice(left, ((t ^ o) * sub, core * half), (sub, half)) for o in range(4)
    ]
    met = swapped(cut)
    own_half = jnp.stack([of_block(met, 2 * outer + i) for i in range(2)])
    other_half = to_core(own_half)

    own, next_one, *partial, mix_rows, left_rows, own_piece = project(
        place, mixes, other_mixes, weights, right, own_half, other_half
    )

    swaps = [[(i, i ^ o) for i in range(4)] for o in range(4)]
    shape = (2, rows, width)
    passed, mids, crossings = [], [], []
    for m in range(micro):
        last = partial[micro + m]
        passed.append(along(last, (0, 1), (3, 2)))
        mids.append(along(last, (1, 2), (2, 1)))
    for m in range(micro):
        two_away = partial[m]
        carried = two_away.shape[2] - width
        (ahead,) = small(
            ahead_kernel,
            [((2, rows, width + 2 * carried), BF16)],
            [],
            place,
            two_away,
            after(passed[m], *mids, *passed),
        )
        crossings.append(along(ahead, *swaps[2]))
    beside = along(next_one, *swaps[1])
    permuted = (own_piece, beside, crossings[0], crossings[0], mids[0])

    layout = (2, micro, 2, own_rows, width)
    here, there = small(
        cut_kernel,
        [(layout, BF16)] * 2,
        [],
        place,
        after(hidden_in[:, 0], own),
        cotangent[:, 0],
    )
    arrived = to_outer(there)
    gain = norm_gain.astype(F32).reshape(1, features)

    update, kept, sent = small(
        update_kernel,
        [((micro, *shape), F32), (shape, BF16), (shape, BF16)],
        [],
        place,
        own,
        after(beside, arrived),
        *mids,
        *crossings,
    )

    def to_section(value):
        return lax.ppermute(value, "pipe", [(0, 1), (1, 0)])

    leaving, final, sums = small(
        state_kernel,
        [(shape, BF16)] * 2 + [((rows, 128), F32)],
        [],
        place,
        here,
        arrived,
        gain,
        update,
        to_section(sent),
    )
    (grad,) = small(
        norm_kernel, [(shape, BF16)], [], place, here, arrived, gain, final, sums, to_outer(sums)
    )

    opposite = along(grad, *swaps[2])
    beside = along(grad, *swaps[1])
    before = to_section(after(kept, final))
    own_there = to_section(after(grad, before))
    relay = after(opposite, own_there, beside)
    mid = along(after(grad, beside), (1, 2), (2, 1))
    farthest = along(relay, (1, 0), (2, 3))
    opposite_there = to_section(opposite)
    by_group, others = small(
        later_kernel,
        [((micro, 2, own_rows, width), BF16)] * 2,
        [],
        place,
        here,
        arrived,
        update,
        before,
        leaving,
    )
    others = to_outer(others)
    beside_there = to_section(after(beside, others))
    (section_out,) = small(
        gather_kernel, [((micro, own_rows, features), BF16)], [], place, by_group, others
    )
    (last,) = small(
        join_kernel, [(shape, BF16)], [], place, mid, after(farthest, beside_there)
    )
    pieces = [grad, beside, relay, last]
    pieces += [own_there, beside_there, opposite_there, to_section(after(last, opposite_there))]
    mix_here, mix_sent, kept_factors, sent_factors = back(
        place, pieces, weights, left_rows, right, mix_rows, permuted
    )
    joined = (kept_factors + after(to_core(sent_factors), section_out)).astype(BF16)
    other_joined = to_outer(joined)
    best = jnp.where(outer == t // 2, joined[:rank], other_joined[:rank])
    (grad_right,) = small(
        right_kernel,
        [((head_cols, rank), F32)],
        [pltpu.VMEM((rank, head_cols), F32)],
        place,
        joined,
        other_joined,
    )
    (grad_left,) = small(
        left_kernel,
        [((rank, width), F32)],
        [],
        place,
        best,
        after(to_core(best), grad_right),
        cost=pl.CostEstimate(flops=8 * 10**9, bytes_accessed=0, transcendentals=0),
    )
    (grad_mix,) = small(
        add_kernel,
        [(mix_here.shape, BF16)],
        [],
        place,
        mix_here,
        after(to_outer(mix_sent), grad_right),
        cost=pl.CostEstimate(flops=5 * 10**9, bytes_accessed=0, transcendentals=0),
    )
    grad_mix = grad_mix.reshape(1, micro, 1, tokens, head_cols)

    return (
        section_out.reshape(1, micro, 1, own_rows, features),
        grad_mix,
        grad_right.reshape(1, 1, head_cols, rank),
        grad_left.reshape(1, 1, rank, width),
    )


def on_device_general(mix, hidden_in, cotangent, frozen_weight, right_factor, left_factor, norm_gain):
    blocks = lax.axis_size("tensor")
    parts = lax.axis_size("dp")
    sections = lax.axis_size("pipe")
    t = lax.axis_index("tensor")
    d = lax.axis_index("dp")
    section = lax.axis_index("pipe")
    outers = parts // 2
    outer = d // 2
    core = d % 2

    def to_core(value):
        return lax.ppermute(value, "dp", [(i, i ^ 1) for i in range(parts)])

    def to_outer(value, step):
        return lax.ppermute(value, "dp", [(i, (i + 2 * step) % parts) for i in range(parts)])

    def to_block(value, step):
        return lax.ppermute(value, "tensor", [(i, (i + step) % blocks) for i in range(blocks)])

    def of_cores(value):
        return jnp.where(core == 0, value, value[::-1])

    mixes = mix[0, :, 0]
    micro, tokens, head_cols = mixes.shape
    own_rows = tokens // blocks
    weight = frozen_weight[0]
    right = right_factor[0, 0]
    left = left_factor[0, 0]
    rank, block_cols = left.shape
    sub = rank // blocks
    width = weight.shape[1]
    features = width * parts
    rows = outers * own_rows
    all_rows = blocks * rows
    per_block = parts // blocks
    slots = (d, d ^ 1)

    def block_of(part):
        return part // per_block

    weights = (weight, to_core(weight))
    own = mixes.reshape(micro, blocks, 1, own_rows, head_cols)
    taken = [
        jnp.concatenate(
            [own[m]] + [to_outer(own[m], step) for step in range(1, outers)], axis=1
        ).reshape(all_rows, head_cols)
        for m in range(micro)
    ]
    own_inner = dot(right, mixes.reshape(micro * tokens, head_cols), 0, 1).astype(BF16)
    pieces = lax.all_to_all(
        jnp.concatenate(
            [
                left.reshape(blocks, sub, block_cols),
                own_inner.reshape(blocks, sub, micro * tokens),
            ],
            axis=2,
        ),
        "tensor",
        split_axis=0,
        concat_axis=0,
        tiled=True,
    )
    left_slots = [
        columns(pick(pieces, block_of(part)), (part % per_block) * width, width) for part in slots
    ]
    right_slots = [columns(right, block_of(part) * sub, sub) for part in slots]
    own_permuted = pieces[:, :, block_cols:].reshape(rank, micro * tokens)
    own_permuted = after(own_permuted, *taken)
    permuted = [own_permuted] + [to_outer(own_permuted, step) for step in range(1, outers)]

    inners = [dot(taken[m], right, 1, 0).astype(BF16) for m in range(micro)]
    partial = [
        jnp.stack(
            [
                (
                    dot(taken[m], weights[slot], 1, 0)
                    + dot(
                        columns(inners[m], block_of(part) * sub, sub), left_slots[slot], 1, 0
                    )
                ).astype(BF16)
                for slot, part in enumerate(slots)
            ]
        ).reshape(2, blocks, rows, width)
        for m in range(micro)
    ]

    def shard(m, index):
        return pick(partial[m], index, 1)

    updates_here = []
    for m in range(micro):
        total = shard(m, t).astype(F32)
        for step in range(1, blocks):
            total = total + to_block(shard(m, (t + step) % blocks), step).astype(F32)
        updates_here.append(total)

    hidden_late = after(hidden_in, *taken)

    def by_column(step):
        target = (outer + step) % outers
        cuts = [2 * target + core, 2 * target + (1 - core)]
        return jnp.stack(
            [
                jnp.stack([columns(value[:, 0], part * width, width) for part in cuts])
                for value in (hidden_late, cotangent)
            ]
        )

    entering = jnp.concatenate(
        [by_column(0)] + [to_outer(by_column(step), step) for step in range(1, outers)], axis=3
    )
    gains = jnp.stack([columns(norm_gain, part * width, width) for part in slots]).astype(F32)

    grads = []
    leaving = []
    for m in range(micro):
        sent = updates_here[m].astype(BF16)
        updates = [updates_here[m]] + [
            lax.ppermute(
                sent, "pipe", [(i, (i + step) % sections) for i in range(sections)]
            ).astype(F32)
            for step in range(1, sections)
        ]
        state = entering[0, :, m]
        kept = state
        for s in range(sections):
            add = updates[0]
            for step in range(1, sections):
                add = jnp.where((section - step) % sections == s, updates[step], add)
            state = (state.astype(F32) + add).astype(BF16)
            kept = jnp.where(section == s, state, kept)
        leaving.append(kept)
        final = state.astype(F32)
        upstream = entering[1, :, m].astype(F32) * gains[:, None, :]
        sums = jnp.stack(
            [jnp.sum(final * final, axis=(0, 2)), jnp.sum(upstream * final, axis=(0, 2))]
        ).reshape(2, outers, own_rows)
        total = sums
        for step in range(1, outers):
            total = total + jnp.roll(to_outer(sums, step), step, axis=1)
        total = total.reshape(2, rows) / features
        scale = lax.rsqrt(total[0] + 1e-05)
        shrink = scale * scale * total[1]
        grads.append(
            (scale[None, :, None] * (upstream - final * shrink[None, :, None])).astype(BF16)
        )

    full = [
        jnp.concatenate(
            [grads[m]] + [to_block(grads[m], step) for step in range(1, blocks)], axis=1
        )
        for m in range(micro)
    ]
    order = [[(t - step) % blocks for step in range(blocks)]] * micro

    outs = []
    for m in range(micro):
        by_group = after(leaving[m], grads[m]).reshape(2, outers, own_rows, width)
        row = jnp.zeros((own_rows, features), BF16)
        for step in range(outers):
            at = (outer + step) % outers
            piece = by_group[:, step]
            if step:
                piece = after(to_outer(piece, outers - step), full[-1])
            for slot in range(2):
                place = (2 * at + (core if slot == 0 else 1 - core)) * width
                row = lax.dynamic_update_slice_in_dim(row, piece[slot], place, 1)
        outs.append(row)
    section_out = jnp.stack(outs).reshape(1, micro, 1, own_rows, features)

    mix_rows = [
        jnp.concatenate(
            [pick(taken[m].reshape(blocks, rows, head_cols), at) for at in order[m]], axis=0
        )
        for m in range(micro)
    ]
    permuted_rows = [
        jnp.concatenate(
            [
                columns(half, m * tokens + at * own_rows, own_rows)
                for at in order[m]
                for half in permuted
            ],
            axis=1,
        )
        for m in range(micro)
    ]

    holder = (t * per_block) // 2
    mix_grads = []
    right_sum = 0.0
    left_sum = 0.0
    for m in range(micro):
        if per_block == 1:
            cols = pick(full[m], jnp.where(t % 2 == core, 0, 1))
        else:
            cols = jnp.concatenate(list(of_cores(full[m])), axis=1)
        left_sum = left_sum + dot(permuted_rows[m], cols, 1, 0)

        inner_grads = [
            dot(full[m][slot], left_slots[slot], 1, 1).astype(BF16) for slot in range(2)
        ]
        if per_block == 1:
            mine = jnp.concatenate(inner_grads, axis=1)
            right_here = jnp.concatenate(right_slots, axis=1)
        else:
            mine = (inner_grads[0].astype(F32) + inner_grads[1].astype(F32)).astype(BF16)
            right_here = right_slots[0]
        right_sum = right_sum + dot(mine, mix_rows[m], 0, 0)

        partial_mix = (
            dot(full[m][0], weights[0], 1, 1)
            + dot(full[m][1], weights[1], 1, 1)
            + dot(mine, right_here, 1, 1)
        ).reshape(blocks, outers, own_rows, head_cols)
        whole = partial_mix[:, 0]
        for step in range(1, outers):
            whole = whole + to_outer(partial_mix[:, step].astype(BF16), outers - step).astype(F32)
        whole = whole.astype(BF16)
        back = order[m]
        mix_grads.append(
            jnp.concatenate([pick(whole, at) for at in back], axis=0)
        )
    grad_mix = jnp.stack(mix_grads).reshape(1, micro, 1, tokens, head_cols)

    half = block_cols // 2
    half_sum = (
        columns(left_sum, core * half, half) + to_core(columns(left_sum, (1 - core) * half, half))
    ).astype(BF16)
    best = half_sum
    for step in range(1, outers):
        pairs = []
        for i in range(blocks):
            at = (i * per_block) // 2
            for c in range(2):
                pairs.append(
                    (i * parts + 2 * at + c, i * parts + 2 * ((at + step) % outers) + c)
                )
        arrived = lax.ppermute(half_sum, ("tensor", "dp"), pairs)
        best = jnp.where((outer - holder) % outers == step, arrived, best)
    there = to_core(best)
    grad_left = jnp.concatenate(list(of_cores(jnp.stack([best, there]))), axis=1).astype(F32)

    if per_block == 1:
        right_sum = of_cores(right_sum.reshape(2, sub, head_cols)).reshape(2 * sub, head_cols)
    right_sum = (right_sum + to_core(right_sum)).astype(BF16)
    wide = jnp.zeros((rank, head_cols), BF16)
    count = right_sum.shape[0]
    for step in range(outers):
        arrived = to_outer(right_sum, step) if step else right_sum
        wide = lax.dynamic_update_slice_in_dim(
            wide, arrived, ((outer - step) % outers) * count, 0
        )
    grad_right = wide.T.astype(F32)

    return (
        section_out,
        grad_mix,
        grad_right.reshape(1, 1, head_cols, rank),
        grad_left.reshape(1, 1, rank, block_cols),
    )


def solution(mesh):
    sizes = (mesh.shape["tensor"], mesh.shape["dp"], mesh.shape["pipe"])
    return jax.shard_map(
        on_device if sizes == (4, 4, 2) else on_device_general,
        mesh=mesh,
        in_specs=(
            P("pipe", None, "dp", None, "tensor"),
            P(None, "dp", "tensor", None),
            P(None, "dp", "tensor", None),
            P("pipe", "tensor", "dp"),
            P("pipe", "tensor", None, None),
            P("pipe", "tensor", None, None),
            P(),
        ),
        out_specs=(
            P("pipe", None, "dp", "tensor", None),
            P("pipe", None, "dp", None, "tensor"),
            P("pipe", "tensor", None, None),
            P("pipe", "tensor", None, None),
        ),
        check_vma=False,
    )
```

```python
import functools

import jax
import jax.numpy as jnp
from jax import lax
from jax.experimental import pallas as pl
from jax.experimental.pallas import tpu as pltpu
from jax.sharding import PartitionSpec as P

F32 = jnp.float32
BF16 = jnp.bfloat16
VMEM = 24 * 2**20
VMEM_ALL = 48 * 2**20
VMEM_SMALL = 10 * 2**20


def dot(left_side, right_side, left_dim, right_dim):
    return lax.dot_general(
        left_side,
        right_side,
        (((left_dim,), (right_dim,)), ((), ())),
        preferred_element_type=F32,
    )


def pick(value, index, dim=0):
    return lax.dynamic_index_in_dim(value, index, dim, keepdims=False)


def columns(value, start, size):
    return lax.dynamic_slice_in_dim(value, start, size, value.ndim - 1)


def after(value, *others):
    return lax.optimization_barrier((value, *others))[0]


NO_COST = pl.CostEstimate(flops=0, bytes_accessed=0, transcendentals=0)


def small(kernel, outs, scratch, place, *values, cost=NO_COST):
    vmem = pl.BlockSpec(memory_space=pltpu.VMEM)
    return pl.pallas_call(
        kernel,
        in_specs=[pl.BlockSpec(memory_space=pltpu.SMEM)] + [vmem] * len(values),
        out_specs=[vmem] * len(outs),
        out_shape=[jax.ShapeDtypeStruct(shape, dtype) for shape, dtype in outs],
        scratch_shapes=scratch,
        compiler_params=pltpu.CompilerParams(vmem_limit_bytes=VMEM_SMALL),
        cost_estimate=cost,
    )(place, *values)


def at_multiple(index, size):
    return pl.ds(pl.multiple_of(index * size, size), size)


def cut_kernel(place, hidden, cotangent, here, there):
    outer, core = place[1], place[2]
    width = here.shape[4]
    for out, target in ((here, outer), (there, 1 - outer)):
        for which, source in enumerate((hidden, cotangent)):
            for m in range(source.shape[0]):
                for slot in range(2):
                    out[which, m, slot] = source[m, :, at_multiple(2 * target + (core ^ slot), width)]


def ahead_kernel(place, two_away, passed, ahead):
    carried = ahead.shape[2] - two_away.shape[2]
    width = two_away.shape[2] - carried
    ahead[:, :, :width] = (
        two_away[:, :, :width].astype(F32) + passed[:, :, :width].astype(F32)
    ).astype(BF16)
    if carried:
        ahead[:, :, width : width + carried] = two_away[:, :, width:]
        ahead[:, :, width + carried :] = passed[:, :, width:]


def update_kernel(place, own, beside, *refs):
    micro, _, _, width = own.shape
    mids, crossings, (update, kept, sent) = refs[:micro], refs[micro : 2 * micro], refs[2 * micro :]
    for m in range(micro):
        total = (own[m].astype(F32) + beside[m, :, :, :width].astype(F32)) + (
            mids[m][:, :, :width].astype(F32) + crossings[m][:, :, :width].astype(F32)
        )
        update[m] = total
        (sent if m else kept)[...] = total.astype(BF16)


def state_kernel(place, here, arrived, gain, update, other, leaving, final, sums):
    outer, core, section = place[1], place[2], place[3]
    own_rows, width = here.shape[3:]
    for group, source in enumerate((here, arrived)):
        at = pl.ds(group * own_rows, own_rows)
        squares = jnp.zeros((own_rows, 1), F32)
        products = jnp.zeros((own_rows, 1), F32)
        for slot in range(2):
            mine = update[0, slot, at, :]
            others = other[slot, at, :].astype(F32)
            first_add = jnp.where(section == 0, mine, others)
            second_add = jnp.where(section == 0, others, mine)
            first = (source[0, section, slot].astype(F32) + first_add).astype(BF16)
            second = (first.astype(F32) + second_add).astype(BF16)
            leaving[slot, at, :] = jnp.where(section == 0, first, second)
            final[slot, at, :] = second
            value = second.astype(F32)
            upstream = source[1, section, slot].astype(F32) * gain[:, at_multiple(2 * outer + (core ^ slot), width)]
            squares += jnp.sum(value * value, axis=1, keepdims=True)
            products += jnp.sum(value * upstream, axis=1, keepdims=True)
        lane = lax.broadcasted_iota(jnp.int32, (own_rows, sums.shape[1]), 1)
        sums[at, :] = jnp.where(lane < sums.shape[1] // 2, squares, products)


def later_kernel(place, here, arrived, update, before, leaving, own, sent):
    section = place[3]
    own_rows = here.shape[3]
    for group, (source, out) in enumerate(((here, own), (arrived, sent))):
        at = pl.ds(group * own_rows, own_rows)
        for slot in range(2):
            start = source[0, 1 - section, slot].astype(F32)
            entering = (start + before[slot, at, :].astype(F32)).astype(BF16).astype(F32)
            entering = jnp.where(section == 0, start, entering)
            out[0, slot] = leaving[slot, at, :]
            out[1, slot] = (entering + update[1, slot, at, :]).astype(BF16)


def norm_kernel(place, here, arrived, gain, final, sums, other_sums, grad):
    outer, core, section = place[1], place[2], place[3]
    own_rows, width = here.shape[3:]
    lanes = sums.shape[1]
    for group, source in enumerate((here, arrived)):
        at = pl.ds(group * own_rows, own_rows)
        total = sums[at, :] + other_sums[pl.ds((1 - group) * own_rows, own_rows), :]
        total = total * (1.0 / (4 * width))
        scale = lax.rsqrt(total[:, :1] + 1e-05)
        shrink = scale * scale * total[:, lanes // 2 : lanes // 2 + 1]
        for slot in range(2):
            upstream = source[1, section, slot].astype(F32) * gain[:, at_multiple(2 * outer + (core ^ slot), width)]
            value = final[slot, at, :].astype(F32)
            grad[slot, at, :] = (scale * (upstream - value * shrink)).astype(BF16)


def join_kernel(place, mid, farthest, last):
    last[...] = mid[...] + farthest[...]


def layout_kernel(place, mixes, right, own_rows, right_here):
    t, section = place[0], place[3]
    micro, _, rows, _ = own_rows.shape
    for m in range(micro):
        for r in range(4):
            own_rows[m, r] = mixes[m ^ section, at_multiple(t ^ r, rows), :]
    right_here[...] = right[...]


def project_kernel(place, own_mix, other_mix, own_weight, other_weight, right, own_half, other_half, *refs):
    own, next_one, *sums, mix_rows, left_rows, piece, inner, turned = refs
    t, outer, core, section = place[0], place[1], place[2], place[3]
    micro, shards = mix_rows.shape[0], 4
    sub, half = own_half.shape[1:]
    step = pl.program_id(0)
    rows = own.shape[2]
    own_rows = rows // 2
    size = shards * rows
    tile = own_weight.shape[1]

    @pl.when(step == 0)
    def _():
        for m in range(micro):
            for r in range(shards):
                at = at_multiple(t ^ r, own_rows)
                mix_rows[m, pl.ds(r * rows, own_rows), :] = own_mix[m, r]
                mix_rows[m, pl.ds(r * rows + own_rows, own_rows), :] = other_mix[m ^ section, at, :]
        product = jnp.dot(
            mix_rows[...].reshape(micro * size, -1), right[...], preferred_element_type=F32
        )
        inner[...] = product.astype(BF16)
        width = left_rows.shape[2]
        for o in range(shards):
            lines = [
                product[m * size + (r ^ o) * rows :][:rows] for m in range(micro) for r in range(shards)
            ]
            turned[...] = jnp.concatenate(lines, axis=0).T
            cut = turned[at_multiple(t ^ o, sub), :].astype(BF16)
            for m in range(micro):
                beside = cut[:, m * size : (m + 1) * size]
                if o == 0:
                    piece[m] = beside
                elif o == 1:
                    next_one[0, m, :, pl.ds(width, size)] = beside
                    next_one[1, m, :, pl.ds(width, size)] = jnp.zeros_like(beside)
                else:
                    sums[(o - 2) * micro][m, :, pl.ds(width, size)] = beside
        left_rows[...] = jnp.zeros_like(left_rows)
        for slot in range(2):
            part = core ^ slot
            at = pl.ds(pl.multiple_of((2 * outer + part) * sub, sub), sub)
            left_rows[slot, at, pl.ds(pl.multiple_of(core * half, half), half)] = own_half[part]
            left_rows[slot, at, pl.ds(pl.multiple_of((1 - core) * half, half), half)] = other_half[part]

    at = pl.ds(pl.multiple_of(step * tile, tile), tile)
    lines = mix_rows[...].reshape(micro * size, -1)
    for slot, weight in enumerate((own_weight, other_weight)):
        product = jnp.dot(lines, weight[...], preferred_element_type=F32) + jnp.dot(
            inner[...], left_rows[slot, :, at], preferred_element_type=F32
        )
        for m in range(micro):
            for r in range(shards):
                at_row = m * size + r * rows
                value = product[at_row : at_row + rows].astype(BF16)
                if r == 0:
                    own[m, slot] = value
                elif r == 1:
                    next_one[m, slot, :, at] = value
                else:
                    sums[(r - 2) * micro + m][slot, :, at] = value


def weight_specs(head_cols, tile):
    return [pl.BlockSpec((head_cols, tile), lambda i: (0, i))] * 2


def whole(*shape):
    return pl.BlockSpec(shape, lambda i: (0,) * len(shape))


def project(place, own_mix, other_mix, weights, right, own_half, other_half):
    micro, tokens, head_cols = other_mix.shape
    width = weights[0].shape[1]
    rank = right.shape[1]
    tile = 1024
    tiles = width // tile
    rows = tokens // 2
    size = 4 * rows
    carrying = (2, rows, width + size)
    plain = (2, rows, width)
    shapes = [(micro, *carrying)] + [carrying, *[plain] * (micro - 1)] * 2
    shapes += [(micro, size, head_cols), (2, rank, width), (2, rank // 4, size)]
    return pl.pallas_call(
        project_kernel,
        grid=(tiles,),
        in_specs=[
            pl.BlockSpec(memory_space=pltpu.SMEM),
            whole(*own_mix.shape),
            whole(*other_mix.shape),
            *weight_specs(head_cols, tile),
            whole(*right.shape),
            whole(*own_half.shape),
            whole(*own_half.shape),
        ],
        out_specs=[pl.BlockSpec((micro, 2, rows, tile), lambda i: (0, 0, 0, i))]
        + [whole(*shape) for shape in shapes],
        out_shape=[jax.ShapeDtypeStruct((micro, 2, rows, width), BF16)]
        + [jax.ShapeDtypeStruct(shape, BF16) for shape in shapes],
        scratch_shapes=[
            pltpu.VMEM((micro * size, rank), BF16),
            pltpu.VMEM((rank, micro * size), F32),
        ],
        compiler_params=pltpu.CompilerParams(vmem_limit_bytes=VMEM_ALL),
        cost_estimate=NO_COST,
    )(place, own_mix, other_mix, *weights, right, own_half, other_half)


def back_kernel(micro, place, *refs):
    pieces, refs = refs[: 4 * micro], refs[4 * micro :]
    (own_weight, other_weight), refs = refs[:2], refs[2:]
    left_rows, right, mix_rows = refs[:3]
    (own_piece, beside_piece, crossed_piece, relayed_piece, mid_piece), refs = refs[3:8], refs[8:]
    mix_here, *mix_sent, kept_factors, sent_factors, total, inner_grad, permuted, right_all = refs
    factors = (kept_factors, sent_factors)
    rank = permuted.shape[0]
    t, outer, core, section = place[0], place[1], place[2], place[3]
    step = pl.program_id(0)
    rows = pieces[0].shape[1]
    own_rows = rows // 2
    tile = own_weight.shape[1]
    half = factors[0].shape[1]

    @pl.when(step == 0)
    def _():
        total[...] = jnp.zeros_like(total)
        inner_grad[...] = jnp.zeros_like(inner_grad)
        _, sub, size = own_piece.shape
        for m in range(micro):
            cut = pl.ds(m * size, size)
            last = mid_piece[m] + relayed_piece[m]
            for o, value in enumerate((own_piece[m], beside_piece[0, m], crossed_piece[m], last)):
                permuted[at_multiple(t ^ o, sub), cut] = value

    grads = []
    for slot in range(2):
        parts = []
        for m in range(micro):
            parts += [piece[slot] for piece in pieces[4 * m : 4 * m + 4]]
        grads.append(jnp.concatenate(parts, axis=0))
    over = (((1,), (1,)), ((), ()))
    total[...] += lax.dot_general(
        own_weight[...], grads[0], over, preferred_element_type=F32
    ) + lax.dot_general(other_weight[...], grads[1], over, preferred_element_type=F32)
    inner_grad[...] += lax.dot_general(
        grads[0], left_rows[0], over, preferred_element_type=F32
    ) + lax.dot_general(grads[1], left_rows[1], over, preferred_element_type=F32)

    at = step * tile
    cut = pl.ds(pl.multiple_of(at % half, tile), tile)
    block = jnp.where(((t & 1) ^ core) == 0, grads[0], grads[1])
    product = jnp.dot(permuted[...], block, preferred_element_type=F32)
    for i, factor in enumerate(factors):

        @pl.when((at // half) ^ core == i)
        def _():
            factor[:rank, cut] = product


    @pl.when(step == pl.num_programs(0) - 1)
    def _():
        mine = inner_grad[...].astype(BF16)
        everything = total[...].T + lax.dot_general(
            mine, right[...], over, preferred_element_type=F32
        )
        for m in range(micro):
            for r in range(4):
                at = at_multiple(t ^ r, own_rows)
                lines = everything[(4 * m + r) * rows :][:rows]
                mix_here[m, at, :] = lines[:own_rows]
                mix_sent[m][at, :] = lines[own_rows:].astype(BF16)
        right_all[...] = lax.dot_general(
            mine,
            mix_rows[...].reshape(mine.shape[0], -1),
            (((0,), (0,)), ((), ())),
            preferred_element_type=F32,
        )
        for i in range(2):
            factors[i][rank:, :] = right_all[at_multiple(outer, rank // 2), :]


def back(place, pieces, weights, left_rows, right, mix_rows, permuted):
    _, rows, width = pieces[0].shape
    head_cols, rank = right.shape
    micro, size, _ = mix_rows.shape
    half = width // 2
    tile = 1024
    tiles = width // tile
    shapes = [
        jax.ShapeDtypeStruct((micro, size // 2, head_cols), F32),
        *[jax.ShapeDtypeStruct((size // 2, head_cols), BF16)] * micro,
        jax.ShapeDtypeStruct((rank + rank // 2, half), F32),
        jax.ShapeDtypeStruct((rank + rank // 2, half), F32),
    ]
    return pl.pallas_call(
        functools.partial(back_kernel, micro),
        grid=(tiles,),
        in_specs=[pl.BlockSpec(memory_space=pltpu.SMEM)]
        + [pl.BlockSpec((2, rows, tile), lambda i: (0, 0, i))] * (4 * micro)
        + weight_specs(head_cols, tile)
        + [
            pl.BlockSpec((2, rank, tile), lambda i: (0, 0, i)),
            whole(*right.shape),
            whole(*mix_rows.shape),
        ]
        + [
            whole(*permuted[0].shape),
            pl.BlockSpec((1, 2, rows, size), lambda i: (0, 0, 0, width // size)),
            pl.BlockSpec((2, rows, size), lambda i: (0, 0, width // size)),
            pl.BlockSpec((2, rows, size), lambda i: (0, 0, width // size + 1)),
            pl.BlockSpec((2, rows, size), lambda i: (0, 0, width // size)),
        ],
        out_specs=[whole(*shape.shape) for shape in shapes],
        out_shape=shapes,
        scratch_shapes=[
            pltpu.VMEM((head_cols, micro * size), F32),
            pltpu.VMEM((micro * size, rank), F32),
            pltpu.VMEM((rank, micro * size), BF16),
            pltpu.VMEM((rank, head_cols), F32),
        ],
        compiler_params=pltpu.CompilerParams(vmem_limit_bytes=VMEM),
        cost_estimate=NO_COST,
    )(place, *pieces, *weights, left_rows, right, mix_rows, *permuted)


def gather_kernel(place, here, arrived, out):
    outer, core, section = place[1], place[2], place[3]
    width = arrived.shape[3]
    for m in range(here.shape[0]):
        for slot in range(2):
            part = core ^ slot
            at = pl.ds(pl.multiple_of((2 * outer + part) * width, width), width)
            out[m ^ section, :, at] = here[m, slot]
            at = pl.ds(pl.multiple_of((2 * (1 - outer) + part) * width, width), width)
            out[m ^ section, :, at] = arrived[m, slot]


def add_kernel(m, place, here, arrived, total):
    total[...] = (here[m] + arrived[...].astype(F32)).astype(BF16)


def place_kernel(place, first, here, arrived, total):
    section = place[3]
    total[section] = first[...]
    total[1 - section] = (here[1] + arrived[...].astype(F32)).astype(BF16)


def sum_kernel(place, kept, arrived, total):
    total[...] = (kept[...] + arrived[...]).astype(BF16)


def left_kernel(place, own_left, other_left, grad_left):
    core = place[2]
    half = own_left.shape[1]
    grad_left[:, pl.ds(pl.multiple_of(core * half, half), half)] = own_left[...].astype(F32)
    grad_left[:, pl.ds(pl.multiple_of((1 - core) * half, half), half)] = other_left[...].astype(F32)


def right_kernel(place, own_right, other_right, grad_right, wide):
    outer = place[1]
    rank = wide.shape[0]
    wide[at_multiple(outer, rank // 2), :] = own_right[rank:, :].astype(F32)
    wide[at_multiple(1 - outer, rank // 2), :] = other_right[rank:, :].astype(F32)
    grad_right[...] = wide[...].T


def on_device(mix, hidden_in, cotangent, frozen_weight, right_factor, left_factor, norm_gain):
    t = lax.axis_index("tensor")
    d = lax.axis_index("dp")
    section = lax.axis_index("pipe")
    outer = d // 2
    core = d % 2
    place = jnp.stack([t, outer, core, section]).astype(jnp.int32)

    def to_core(value):
        return lax.ppermute(value, "dp", [(i, i ^ 1) for i in range(4)])

    def to_outer(value):
        return lax.ppermute(value, "dp", [(i, i ^ 2) for i in range(4)])

    def along(value, *pairs):
        return lax.ppermute(value, "tensor", pairs)

    mixes = mix[0, :, 0]
    micro, tokens, head_cols = mixes.shape
    own_rows = tokens // 4
    rows = 2 * own_rows
    weight = frozen_weight[0]
    right = right_factor[0, 0]
    left = left_factor[0, 0]
    rank, width = left.shape
    sub = rank // 4
    half = width // 2
    features = 4 * width
    slots = (d, d ^ 1)

    other_mixes = to_outer(mixes)
    weights = (weight, to_core(weight))

    def swapped(values):
        return [values[0]] + [along(values[o], *[(i, i ^ o) for i in range(4)]) for o in (1, 2, 3)]

    def of_block(values, block):
        return lax.select_n(t ^ block, *values)

    cut = [
        lax.dynamic_slice(left, ((t ^ o) * sub, core * half), (sub, half)) for o in range(4)
    ]
    laid, right_here = small(
        layout_kernel,
        [((micro, 4, own_rows, head_cols), BF16), (right.shape, BF16)],
        [],
        place,
        mixes,
        right,
    )
    met = swapped(cut)
    met[2] = after(met[2], laid, right_here)
    own_half = jnp.stack([of_block(met, 2 * outer + i) for i in range(2)])
    other_half = to_core(own_half)

    own, next_one, *partial, mix_rows, left_rows, own_piece = project(
        place, laid, other_mixes, weights, right_here, own_half, other_half
    )

    swaps = [[(i, i ^ o) for i in range(4)] for o in range(4)]
    shape = (2, rows, width)
    passed, mids, crossings = [], [], []
    for m in range(micro):
        last = partial[micro + m]
        passed.append(along(last, (0, 1), (3, 2)))
        mids.append(along(last, (1, 2), (2, 1)))
    for m in range(micro):
        two_away = partial[m]
        carried = two_away.shape[2] - width
        (ahead,) = small(
            ahead_kernel,
            [((2, rows, width + 2 * carried), BF16)],
            [],
            place,
            two_away,
            after(passed[m], *mids, *passed),
        )
        crossings.append(along(ahead, *swaps[2]))
    beside = along(next_one, *swaps[1])
    permuted = (own_piece, beside, crossings[0], crossings[0], mids[0])

    layout = (2, micro, 2, own_rows, width)
    here, there = small(
        cut_kernel,
        [(layout, BF16)] * 2,
        [],
        place,
        after(hidden_in[:, 0], own),
        cotangent[:, 0],
    )
    arrived = to_outer(there)
    gain = norm_gain.astype(F32).reshape(1, features)

    update, kept, sent = small(
        update_kernel,
        [((micro, *shape), F32), (shape, BF16), (shape, BF16)],
        [],
        place,
        own,
        after(beside, arrived),
        *mids,
        *crossings,
    )

    def to_section(value):
        return lax.ppermute(value, "pipe", [(0, 1), (1, 0)])

    leaving, final, sums = small(
        state_kernel,
        [(shape, BF16)] * 2 + [((rows, 128), F32)],
        [],
        place,
        here,
        arrived,
        gain,
        update,
        to_section(sent),
    )
    (grad,) = small(
        norm_kernel, [(shape, BF16)], [], place, here, arrived, gain, final, sums, to_outer(sums)
    )

    opposite = along(grad, *swaps[2])
    beside = along(grad, *swaps[1])
    before = to_section(after(kept, final))
    own_there = to_section(after(grad, before))
    relay = after(opposite, own_there, beside)
    mid = along(after(grad, beside), (1, 2), (2, 1))
    farthest = along(relay, (1, 0), (2, 3))
    opposite_there = to_section(opposite)
    by_group, others = small(
        later_kernel,
        [((micro, 2, own_rows, width), BF16)] * 2,
        [],
        place,
        here,
        arrived,
        update,
        before,
        leaving,
    )
    others = to_outer(others)
    beside_there = to_section(after(beside, others))
    (section_out,) = small(
        gather_kernel, [((micro, own_rows, features), BF16)], [], place, by_group, others
    )
    (last,) = small(
        join_kernel, [(shape, BF16)], [], place, mid, after(farthest, beside_there)
    )
    pieces = [grad, beside, relay, last]
    pieces += [own_there, beside_there, opposite_there, to_section(after(last, opposite_there))]
    mix_here, first_sent, second_sent, kept_factors, sent_factors = back(
        place, pieces, weights, left_rows, right, mix_rows, permuted
    )
    (joined,) = small(
        sum_kernel, [(kept_factors.shape, BF16)], [], place, kept_factors, to_core(sent_factors)
    )
    other_joined = after(to_outer(joined), section_out)
    best = jnp.where(outer == t // 2, joined[:rank], other_joined[:rank])
    (grad_right,) = small(
        right_kernel,
        [((head_cols, rank), F32)],
        [pltpu.VMEM((rank, head_cols), F32)],
        place,
        joined,
        other_joined,
    )
    (grad_left,) = small(
        left_kernel,
        [((rank, width), F32)],
        [],
        place,
        best,
        after(to_core(best), grad_right),
        cost=pl.CostEstimate(flops=8 * 10**9, bytes_accessed=0, transcendentals=0),
    )
    (first_mix,) = small(
        functools.partial(add_kernel, 0),
        [(second_sent.shape, BF16)],
        [],
        place,
        mix_here,
        to_outer(first_sent),
        cost=pl.CostEstimate(flops=15 * 10**9, bytes_accessed=0, transcendentals=0),
    )
    (grad_mix,) = small(
        place_kernel,
        [((micro, tokens, head_cols), BF16)],
        [],
        place,
        first_mix,
        mix_here,
        after(to_outer(after(second_sent, joined)), grad_right),
        cost=pl.CostEstimate(flops=5 * 10**9, bytes_accessed=0, transcendentals=0),
    )
    grad_mix = grad_mix.reshape(1, micro, 1, tokens, head_cols)

    return (
        section_out.reshape(1, micro, 1, own_rows, features),
        grad_mix,
        grad_right.reshape(1, 1, head_cols, rank),
        grad_left.reshape(1, 1, rank, width),
    )


def on_device_general(mix, hidden_in, cotangent, frozen_weight, right_factor, left_factor, norm_gain):
    blocks = lax.axis_size("tensor")
    parts = lax.axis_size("dp")
    sections = lax.axis_size("pipe")
    t = lax.axis_index("tensor")
    d = lax.axis_index("dp")
    section = lax.axis_index("pipe")
    outers = parts // 2
    outer = d // 2
    core = d % 2

    def to_core(value):
        return lax.ppermute(value, "dp", [(i, i ^ 1) for i in range(parts)])

    def to_outer(value, step):
        return lax.ppermute(value, "dp", [(i, (i + 2 * step) % parts) for i in range(parts)])

    def to_block(value, step):
        return lax.ppermute(value, "tensor", [(i, (i + step) % blocks) for i in range(blocks)])

    def of_cores(value):
        return jnp.where(core == 0, value, value[::-1])

    mixes = mix[0, :, 0]
    micro, tokens, head_cols = mixes.shape
    own_rows = tokens // blocks
    weight = frozen_weight[0]
    right = right_factor[0, 0]
    left = left_factor[0, 0]
    rank, block_cols = left.shape
    sub = rank // blocks
    width = weight.shape[1]
    features = width * parts
    rows = outers * own_rows
    all_rows = blocks * rows
    per_block = parts // blocks
    slots = (d, d ^ 1)

    def block_of(part):
        return part // per_block

    weights = (weight, to_core(weight))
    own = mixes.reshape(micro, blocks, 1, own_rows, head_cols)
    taken = [
        jnp.concatenate(
            [own[m]] + [to_outer(own[m], step) for step in range(1, outers)], axis=1
        ).reshape(all_rows, head_cols)
        for m in range(micro)
    ]
    own_inner = dot(right, mixes.reshape(micro * tokens, head_cols), 0, 1).astype(BF16)
    pieces = lax.all_to_all(
        jnp.concatenate(
            [
                left.reshape(blocks, sub, block_cols),
                own_inner.reshape(blocks, sub, micro * tokens),
            ],
            axis=2,
        ),
        "tensor",
        split_axis=0,
        concat_axis=0,
        tiled=True,
    )
    left_slots = [
        columns(pick(pieces, block_of(part)), (part % per_block) * width, width) for part in slots
    ]
    right_slots = [columns(right, block_of(part) * sub, sub) for part in slots]
    own_permuted = pieces[:, :, block_cols:].reshape(rank, micro * tokens)
    own_permuted = after(own_permuted, *taken)
    permuted = [own_permuted] + [to_outer(own_permuted, step) for step in range(1, outers)]

    inners = [dot(taken[m], right, 1, 0).astype(BF16) for m in range(micro)]
    partial = [
        jnp.stack(
            [
                (
                    dot(taken[m], weights[slot], 1, 0)
                    + dot(
                        columns(inners[m], block_of(part) * sub, sub), left_slots[slot], 1, 0
                    )
                ).astype(BF16)
                for slot, part in enumerate(slots)
            ]
        ).reshape(2, blocks, rows, width)
        for m in range(micro)
    ]

    def shard(m, index):
        return pick(partial[m], index, 1)

    updates_here = []
    for m in range(micro):
        total = shard(m, t).astype(F32)
        for step in range(1, blocks):
            total = total + to_block(shard(m, (t + step) % blocks), step).astype(F32)
        updates_here.append(total)

    hidden_late = after(hidden_in, *taken)

    def by_column(step):
        target = (outer + step) % outers
        cuts = [2 * target + core, 2 * target + (1 - core)]
        return jnp.stack(
            [
                jnp.stack([columns(value[:, 0], part * width, width) for part in cuts])
                for value in (hidden_late, cotangent)
            ]
        )

    entering = jnp.concatenate(
        [by_column(0)] + [to_outer(by_column(step), step) for step in range(1, outers)], axis=3
    )
    gains = jnp.stack([columns(norm_gain, part * width, width) for part in slots]).astype(F32)

    grads = []
    leaving = []
    for m in range(micro):
        sent = updates_here[m].astype(BF16)
        updates = [updates_here[m]] + [
            lax.ppermute(
                sent, "pipe", [(i, (i + step) % sections) for i in range(sections)]
            ).astype(F32)
            for step in range(1, sections)
        ]
        state = entering[0, :, m]
        kept = state
        for s in range(sections):
            add = updates[0]
            for step in range(1, sections):
                add = jnp.where((section - step) % sections == s, updates[step], add)
            state = (state.astype(F32) + add).astype(BF16)
            kept = jnp.where(section == s, state, kept)
        leaving.append(kept)
        final = state.astype(F32)
        upstream = entering[1, :, m].astype(F32) * gains[:, None, :]
        sums = jnp.stack(
            [jnp.sum(final * final, axis=(0, 2)), jnp.sum(upstream * final, axis=(0, 2))]
        ).reshape(2, outers, own_rows)
        total = sums
        for step in range(1, outers):
            total = total + jnp.roll(to_outer(sums, step), step, axis=1)
        total = total.reshape(2, rows) / features
        scale = lax.rsqrt(total[0] + 1e-05)
        shrink = scale * scale * total[1]
        grads.append(
            (scale[None, :, None] * (upstream - final * shrink[None, :, None])).astype(BF16)
        )

    full = [
        jnp.concatenate(
            [grads[m]] + [to_block(grads[m], step) for step in range(1, blocks)], axis=1
        )
        for m in range(micro)
    ]
    order = [[(t - step) % blocks for step in range(blocks)]] * micro

    outs = []
    for m in range(micro):
        by_group = after(leaving[m], grads[m]).reshape(2, outers, own_rows, width)
        row = jnp.zeros((own_rows, features), BF16)
        for step in range(outers):
            at = (outer + step) % outers
            piece = by_group[:, step]
            if step:
                piece = after(to_outer(piece, outers - step), full[-1])
            for slot in range(2):
                place = (2 * at + (core if slot == 0 else 1 - core)) * width
                row = lax.dynamic_update_slice_in_dim(row, piece[slot], place, 1)
        outs.append(row)
    section_out = jnp.stack(outs).reshape(1, micro, 1, own_rows, features)

    mix_rows = [
        jnp.concatenate(
            [pick(taken[m].reshape(blocks, rows, head_cols), at) for at in order[m]], axis=0
        )
        for m in range(micro)
    ]
    permuted_rows = [
        jnp.concatenate(
            [
                columns(half, m * tokens + at * own_rows, own_rows)
                for at in order[m]
                for half in permuted
            ],
            axis=1,
        )
        for m in range(micro)
    ]

    holder = (t * per_block) // 2
    mix_grads = []
    right_sum = 0.0
    left_sum = 0.0
    for m in range(micro):
        if per_block == 1:
            cols = pick(full[m], jnp.where(t % 2 == core, 0, 1))
        else:
            cols = jnp.concatenate(list(of_cores(full[m])), axis=1)
        left_sum = left_sum + dot(permuted_rows[m], cols, 1, 0)

        inner_grads = [
            dot(full[m][slot], left_slots[slot], 1, 1).astype(BF16) for slot in range(2)
        ]
        if per_block == 1:
            mine = jnp.concatenate(inner_grads, axis=1)
            right_here = jnp.concatenate(right_slots, axis=1)
        else:
            mine = (inner_grads[0].astype(F32) + inner_grads[1].astype(F32)).astype(BF16)
            right_here = right_slots[0]
        right_sum = right_sum + dot(mine, mix_rows[m], 0, 0)

        partial_mix = (
            dot(full[m][0], weights[0], 1, 1)
            + dot(full[m][1], weights[1], 1, 1)
            + dot(mine, right_here, 1, 1)
        ).reshape(blocks, outers, own_rows, head_cols)
        whole = partial_mix[:, 0]
        for step in range(1, outers):
            whole = whole + to_outer(partial_mix[:, step].astype(BF16), outers - step).astype(F32)
        whole = whole.astype(BF16)
        back = order[m]
        mix_grads.append(
            jnp.concatenate([pick(whole, at) for at in back], axis=0)
        )
    grad_mix = jnp.stack(mix_grads).reshape(1, micro, 1, tokens, head_cols)

    half = block_cols // 2
    half_sum = (
        columns(left_sum, core * half, half) + to_core(columns(left_sum, (1 - core) * half, half))
    ).astype(BF16)
    best = half_sum
    for step in range(1, outers):
        pairs = []
        for i in range(blocks):
            at = (i * per_block) // 2
            for c in range(2):
                pairs.append(
                    (i * parts + 2 * at + c, i * parts + 2 * ((at + step) % outers) + c)
                )
        arrived = lax.ppermute(half_sum, ("tensor", "dp"), pairs)
        best = jnp.where((outer - holder) % outers == step, arrived, best)
    there = to_core(best)
    grad_left = jnp.concatenate(list(of_cores(jnp.stack([best, there]))), axis=1).astype(F32)

    if per_block == 1:
        right_sum = of_cores(right_sum.reshape(2, sub, head_cols)).reshape(2 * sub, head_cols)
    right_sum = (right_sum + to_core(right_sum)).astype(BF16)
    wide = jnp.zeros((rank, head_cols), BF16)
    count = right_sum.shape[0]
    for step in range(outers):
        arrived = to_outer(right_sum, step) if step else right_sum
        wide = lax.dynamic_update_slice_in_dim(
            wide, arrived, ((outer - step) % outers) * count, 0
        )
    grad_right = wide.T.astype(F32)

    return (
        section_out,
        grad_mix,
        grad_right.reshape(1, 1, head_cols, rank),
        grad_left.reshape(1, 1, rank, block_cols),
    )


def solution(mesh):
    sizes = (mesh.shape["tensor"], mesh.shape["dp"], mesh.shape["pipe"])
    return jax.shard_map(
        on_device if sizes == (4, 4, 2) else on_device_general,
        mesh=mesh,
        in_specs=(
            P("pipe", None, "dp", None, "tensor"),
            P(None, "dp", "tensor", None),
            P(None, "dp", "tensor", None),
            P("pipe", "tensor", "dp"),
            P("pipe", "tensor", None, None),
            P("pipe", "tensor", None, None),
            P(),
        ),
        out_specs=(
            P("pipe", None, "dp", "tensor", None),
            P("pipe", None, "dp", None, "tensor"),
            P("pipe", "tensor", None, None),
            P("pipe", "tensor", None, None),
        ),
        check_vma=False,
    )
```

```python
import functools

import jax
import jax.numpy as jnp
from jax import lax
from jax.experimental import pallas as pl
from jax.experimental.pallas import tpu as pltpu
from jax.sharding import PartitionSpec as P

F32 = jnp.float32
BF16 = jnp.bfloat16
VMEM = 24 * 2**20
VMEM_ALL = 48 * 2**20
VMEM_SMALL = 10 * 2**20


def dot(left_side, right_side, left_dim, right_dim):
    return lax.dot_general(
        left_side,
        right_side,
        (((left_dim,), (right_dim,)), ((), ())),
        preferred_element_type=F32,
    )


def pick(value, index, dim=0):
    return lax.dynamic_index_in_dim(value, index, dim, keepdims=False)


def columns(value, start, size):
    return lax.dynamic_slice_in_dim(value, start, size, value.ndim - 1)


def after(value, *others):
    return lax.optimization_barrier((value, *others))[0]


NO_COST = pl.CostEstimate(flops=0, bytes_accessed=0, transcendentals=0)


def small(kernel, outs, scratch, place, *values, cost=NO_COST):
    vmem = pl.BlockSpec(memory_space=pltpu.VMEM)
    return pl.pallas_call(
        kernel,
        in_specs=[pl.BlockSpec(memory_space=pltpu.SMEM)] + [vmem] * len(values),
        out_specs=[vmem] * len(outs),
        out_shape=[jax.ShapeDtypeStruct(shape, dtype) for shape, dtype in outs],
        scratch_shapes=scratch,
        compiler_params=pltpu.CompilerParams(vmem_limit_bytes=VMEM_SMALL),
        cost_estimate=cost,
    )(place, *values)


def at_multiple(index, size):
    return pl.ds(pl.multiple_of(index * size, size), size)


def cut_kernel(place, hidden, cotangent, here, there):
    outer, core = place[1], place[2]
    width = here.shape[4]
    for out, target in ((here, outer), (there, 1 - outer)):
        for which, source in enumerate((hidden, cotangent)):
            for m in range(source.shape[0]):
                for slot in range(2):
                    out[which, m, slot] = source[m, :, at_multiple(2 * target + (core ^ slot), width)]


def ahead_kernel(place, two_away, passed, ahead):
    carried = ahead.shape[2] - two_away.shape[2]
    width = two_away.shape[2] - carried
    ahead[:, :, :width] = (
        two_away[:, :, :width].astype(F32) + passed[:, :, :width].astype(F32)
    ).astype(BF16)
    if carried:
        ahead[:, :, width : width + carried] = two_away[:, :, width:]
        ahead[:, :, width + carried :] = passed[:, :, width:]


def update_kernel(place, own, beside, *refs):
    micro, _, _, width = own.shape
    mids, crossings, (update, kept, sent) = refs[:micro], refs[micro : 2 * micro], refs[2 * micro :]
    for m in range(micro):
        total = (own[m].astype(F32) + beside[m, :, :, :width].astype(F32)) + (
            mids[m][:, :, :width].astype(F32) + crossings[m][:, :, :width].astype(F32)
        )
        update[m] = total
        (sent if m else kept)[...] = total.astype(BF16)


def state_kernel(place, here, arrived, gain, update, other, leaving, final, sums):
    outer, core, section = place[1], place[2], place[3]
    own_rows, width = here.shape[3:]
    for group, source in enumerate((here, arrived)):
        at = pl.ds(group * own_rows, own_rows)
        squares = jnp.zeros((own_rows, 1), F32)
        products = jnp.zeros((own_rows, 1), F32)
        for slot in range(2):
            mine = update[0, slot, at, :]
            others = other[slot, at, :].astype(F32)
            first_add = jnp.where(section == 0, mine, others)
            second_add = jnp.where(section == 0, others, mine)
            first = (source[0, section, slot].astype(F32) + first_add).astype(BF16)
            second = (first.astype(F32) + second_add).astype(BF16)
            leaving[slot, at, :] = jnp.where(section == 0, first, second)
            final[slot, at, :] = second
            value = second.astype(F32)
            upstream = source[1, section, slot].astype(F32) * gain[:, at_multiple(2 * outer + (core ^ slot), width)]
            squares += jnp.sum(value * value, axis=1, keepdims=True)
            products += jnp.sum(value * upstream, axis=1, keepdims=True)
        lane = lax.broadcasted_iota(jnp.int32, (own_rows, sums.shape[1]), 1)
        sums[at, :] = jnp.where(lane < sums.shape[1] // 2, squares, products)


def later_kernel(place, here, arrived, update, before, leaving, own, sent):
    section = place[3]
    own_rows = here.shape[3]
    for group, (source, out) in enumerate(((here, own), (arrived, sent))):
        at = pl.ds(group * own_rows, own_rows)
        for slot in range(2):
            start = source[0, 1 - section, slot].astype(F32)
            entering = (start + before[slot, at, :].astype(F32)).astype(BF16).astype(F32)
            entering = jnp.where(section == 0, start, entering)
            out[0, slot] = leaving[slot, at, :]
            out[1, slot] = (entering + update[1, slot, at, :]).astype(BF16)


def norm_kernel(place, here, arrived, gain, final, sums, other_sums, grad):
    outer, core, section = place[1], place[2], place[3]
    own_rows, width = here.shape[3:]
    lanes = sums.shape[1]
    for group, source in enumerate((here, arrived)):
        at = pl.ds(group * own_rows, own_rows)
        total = sums[at, :] + other_sums[pl.ds((1 - group) * own_rows, own_rows), :]
        total = total * (1.0 / (4 * width))
        scale = lax.rsqrt(total[:, :1] + 1e-05)
        shrink = scale * scale * total[:, lanes // 2 : lanes // 2 + 1]
        for slot in range(2):
            upstream = source[1, section, slot].astype(F32) * gain[:, at_multiple(2 * outer + (core ^ slot), width)]
            value = final[slot, at, :].astype(F32)
            grad[slot, at, :] = (scale * (upstream - value * shrink)).astype(BF16)


def join_kernel(place, mid, farthest, last):
    last[...] = mid[...] + farthest[...]


def layout_kernel(place, mixes, right, own_rows, right_here):
    t, section = place[0], place[3]
    micro, _, rows, _ = own_rows.shape
    for m in range(micro):
        for r in range(4):
            own_rows[m, r] = mixes[m ^ section, at_multiple(t ^ r, rows), :]
    right_here[...] = right[...]


def project_kernel(place, own_mix, other_mix, own_weight, other_weight, right, own_half, other_half, *refs):
    own, next_one, *sums, mix_rows, left_rows, piece, inner, turned = refs
    t, outer, core, section = place[0], place[1], place[2], place[3]
    micro, shards = mix_rows.shape[0], 4
    sub, half = own_half.shape[1:]
    step = pl.program_id(0)
    rows = own.shape[2]
    own_rows = rows // 2
    size = shards * rows
    tile = own_weight.shape[1]

    @pl.when(step == 0)
    def _():
        for m in range(micro):
            for r in range(shards):
                at = at_multiple(t ^ r, own_rows)
                mix_rows[m, pl.ds(r * rows, own_rows), :] = own_mix[m, r]
                mix_rows[m, pl.ds(r * rows + own_rows, own_rows), :] = other_mix[m ^ section, at, :]
        product = jnp.dot(
            mix_rows[...].reshape(micro * size, -1), right[...], preferred_element_type=F32
        )
        inner[...] = product.astype(BF16)
        width = left_rows.shape[2]
        for o in range(shards):
            lines = [
                product[m * size + (r ^ o) * rows :][:rows] for m in range(micro) for r in range(shards)
            ]
            turned[...] = jnp.concatenate(lines, axis=0).T
            cut = turned[at_multiple(t ^ o, sub), :].astype(BF16)
            for m in range(micro):
                beside = cut[:, m * size : (m + 1) * size]
                if o == 0:
                    piece[m] = beside
                elif o == 1:
                    next_one[0, m, :, pl.ds(width, size)] = beside
                    next_one[1, m, :, pl.ds(width, size)] = jnp.zeros_like(beside)
                else:
                    sums[(o - 2) * micro][m, :, pl.ds(width, size)] = beside
        left_rows[...] = jnp.zeros_like(left_rows)
        for slot in range(2):
            part = core ^ slot
            at = pl.ds(pl.multiple_of((2 * outer + part) * sub, sub), sub)
            left_rows[slot, at, pl.ds(pl.multiple_of(core * half, half), half)] = own_half[part]
            left_rows[slot, at, pl.ds(pl.multiple_of((1 - core) * half, half), half)] = other_half[part]

    at = pl.ds(pl.multiple_of(step * tile, tile), tile)
    lines = mix_rows[...].reshape(micro * size, -1)
    for slot, weight in enumerate((own_weight, other_weight)):
        product = jnp.dot(lines, weight[...], preferred_element_type=F32) + jnp.dot(
            inner[...], left_rows[slot, :, at], preferred_element_type=F32
        )
        for m in range(micro):
            for r in range(shards):
                at_row = m * size + r * rows
                value = product[at_row : at_row + rows].astype(BF16)
                if r == 0:
                    own[m, slot] = value
                elif r == 1:
                    next_one[m, slot, :, at] = value
                else:
                    sums[(r - 2) * micro + m][slot, :, at] = value


def weight_specs(head_cols, tile):
    return [pl.BlockSpec((head_cols, tile), lambda i: (0, i))] * 2


def whole(*shape):
    return pl.BlockSpec(shape, lambda i: (0,) * len(shape))


def project(place, own_mix, other_mix, weights, right, own_half, other_half):
    micro, tokens, head_cols = other_mix.shape
    width = weights[0].shape[1]
    rank = right.shape[1]
    tile = 1024
    tiles = width // tile
    rows = tokens // 2
    size = 4 * rows
    carrying = (2, rows, width + size)
    plain = (2, rows, width)
    shapes = [(micro, *carrying)] + [carrying, *[plain] * (micro - 1)] * 2
    shapes += [(micro, size, head_cols), (2, rank, width), (2, rank // 4, size)]
    return pl.pallas_call(
        project_kernel,
        grid=(tiles,),
        in_specs=[
            pl.BlockSpec(memory_space=pltpu.SMEM),
            whole(*own_mix.shape),
            whole(*other_mix.shape),
            *weight_specs(head_cols, tile),
            whole(*right.shape),
            whole(*own_half.shape),
            whole(*own_half.shape),
        ],
        out_specs=[pl.BlockSpec((micro, 2, rows, tile), lambda i: (0, 0, 0, i))]
        + [whole(*shape) for shape in shapes],
        out_shape=[jax.ShapeDtypeStruct((micro, 2, rows, width), BF16)]
        + [jax.ShapeDtypeStruct(shape, BF16) for shape in shapes],
        scratch_shapes=[
            pltpu.VMEM((micro * size, rank), BF16),
            pltpu.VMEM((rank, micro * size), F32),
        ],
        compiler_params=pltpu.CompilerParams(vmem_limit_bytes=VMEM_ALL),
        cost_estimate=NO_COST,
    )(place, own_mix, other_mix, *weights, right, own_half, other_half)


def back_kernel(micro, place, *refs):
    pieces, refs = refs[: 4 * micro], refs[4 * micro :]
    (own_weight, other_weight), refs = refs[:2], refs[2:]
    left_rows, right, mix_rows = refs[:3]
    (own_piece, beside_piece, crossed_piece, relayed_piece, mid_piece), refs = refs[3:8], refs[8:]
    mix_here, *mix_sent, kept_factors, sent_factors, total, inner_grad, permuted, right_all = refs
    factors = (kept_factors, sent_factors)
    rank = permuted.shape[0]
    t, outer, core, section = place[0], place[1], place[2], place[3]
    step = pl.program_id(0)
    rows = pieces[0].shape[1]
    own_rows = rows // 2
    tile = own_weight.shape[1]
    half = factors[0].shape[1]

    @pl.when(step == 0)
    def _():
        total[...] = jnp.zeros_like(total)
        inner_grad[...] = jnp.zeros_like(inner_grad)
        _, sub, size = own_piece.shape
        for m in range(micro):
            cut = pl.ds(m * size, size)
            last = mid_piece[m] + relayed_piece[m]
            for o, value in enumerate((own_piece[m], beside_piece[0, m], crossed_piece[m], last)):
                permuted[at_multiple(t ^ o, sub), cut] = value

    grads = []
    for slot in range(2):
        parts = []
        for m in range(micro):
            parts += [piece[slot] for piece in pieces[4 * m : 4 * m + 4]]
        grads.append(jnp.concatenate(parts, axis=0))
    over = (((1,), (1,)), ((), ()))
    total[...] += lax.dot_general(
        own_weight[...], grads[0], over, preferred_element_type=F32
    ) + lax.dot_general(other_weight[...], grads[1], over, preferred_element_type=F32)
    inner_grad[...] += lax.dot_general(
        grads[0], left_rows[0], over, preferred_element_type=F32
    ) + lax.dot_general(grads[1], left_rows[1], over, preferred_element_type=F32)

    at = step * tile
    cut = pl.ds(pl.multiple_of(at % half, tile), tile)
    block = jnp.where(((t & 1) ^ core) == 0, grads[0], grads[1])
    product = jnp.dot(permuted[...], block, preferred_element_type=F32)
    for i, factor in enumerate(factors):

        @pl.when((at // half) ^ core == i)
        def _():
            factor[:rank, cut] = product


    @pl.when(step == pl.num_programs(0) - 1)
    def _():
        mine = inner_grad[...].astype(BF16)
        everything = total[...].T + lax.dot_general(
            mine, right[...], over, preferred_element_type=F32
        )
        for m in range(micro):
            for r in range(4):
                at = at_multiple(t ^ r, own_rows)
                lines = everything[(4 * m + r) * rows :][:rows]
                mix_here[m, at, :] = lines[:own_rows]
                mix_sent[m][at, :] = lines[own_rows:].astype(BF16)
        right_all[...] = lax.dot_general(
            mine,
            mix_rows[...].reshape(mine.shape[0], -1),
            (((0,), (0,)), ((), ())),
            preferred_element_type=F32,
        )
        for i in range(2):
            factors[i][rank:, :] = right_all[at_multiple(outer, rank // 2), :]


def back(place, pieces, weights, left_rows, right, mix_rows, permuted):
    _, rows, width = pieces[0].shape
    head_cols, rank = right.shape
    micro, size, _ = mix_rows.shape
    half = width // 2
    tile = 1024
    tiles = width // tile
    shapes = [
        jax.ShapeDtypeStruct((micro, size // 2, head_cols), F32),
        *[jax.ShapeDtypeStruct((size // 2, head_cols), BF16)] * micro,
        jax.ShapeDtypeStruct((rank + rank // 2, half), F32),
        jax.ShapeDtypeStruct((rank + rank // 2, half), F32),
    ]
    return pl.pallas_call(
        functools.partial(back_kernel, micro),
        grid=(tiles,),
        in_specs=[pl.BlockSpec(memory_space=pltpu.SMEM)]
        + [pl.BlockSpec((2, rows, tile), lambda i: (0, 0, i))] * (4 * micro)
        + weight_specs(head_cols, tile)
        + [
            pl.BlockSpec((2, rank, tile), lambda i: (0, 0, i)),
            whole(*right.shape),
            whole(*mix_rows.shape),
        ]
        + [
            whole(*permuted[0].shape),
            pl.BlockSpec((1, 2, rows, size), lambda i: (0, 0, 0, width // size)),
            pl.BlockSpec((2, rows, size), lambda i: (0, 0, width // size)),
            pl.BlockSpec((2, rows, size), lambda i: (0, 0, width // size + 1)),
            pl.BlockSpec((2, rows, size), lambda i: (0, 0, width // size)),
        ],
        out_specs=[whole(*shape.shape) for shape in shapes],
        out_shape=shapes,
        scratch_shapes=[
            pltpu.VMEM((head_cols, micro * size), F32),
            pltpu.VMEM((micro * size, rank), F32),
            pltpu.VMEM((rank, micro * size), BF16),
            pltpu.VMEM((rank, head_cols), F32),
        ],
        compiler_params=pltpu.CompilerParams(vmem_limit_bytes=VMEM),
        cost_estimate=NO_COST,
    )(place, *pieces, *weights, left_rows, right, mix_rows, *permuted)


def gather_kernel(place, here, arrived, out):
    outer, core, section = place[1], place[2], place[3]
    width = arrived.shape[3]
    for m in range(here.shape[0]):
        for slot in range(2):
            part = core ^ slot
            at = pl.ds(pl.multiple_of((2 * outer + part) * width, width), width)
            out[m ^ section, :, at] = here[m, slot]
            at = pl.ds(pl.multiple_of((2 * (1 - outer) + part) * width, width), width)
            out[m ^ section, :, at] = arrived[m, slot]


def add_kernel(m, place, here, arrived, total):
    total[...] = (here[m] + arrived[...].astype(F32)).astype(BF16)


def place_kernel(place, first, here, arrived, total):
    section = place[3]
    total[section] = first[...]
    total[1 - section] = (here[1] + arrived[...].astype(F32)).astype(BF16)


def sum_kernel(place, kept, arrived, total):
    total[...] = (kept[...] + arrived[...]).astype(BF16)


def left_kernel(place, own_left, other_left, grad_left):
    core = place[2]
    half = own_left.shape[1]
    grad_left[:, pl.ds(pl.multiple_of(core * half, half), half)] = own_left[...].astype(F32)
    grad_left[:, pl.ds(pl.multiple_of((1 - core) * half, half), half)] = other_left[...].astype(F32)


def right_kernel(place, own_right, other_right, grad_right, wide):
    outer = place[1]
    rank = wide.shape[0]
    wide[at_multiple(outer, rank // 2), :] = own_right[rank:, :].astype(F32)
    wide[at_multiple(1 - outer, rank // 2), :] = other_right[rank:, :].astype(F32)
    grad_right[...] = wide[...].T


def on_device(mix, hidden_in, cotangent, frozen_weight, right_factor, left_factor, norm_gain):
    t = lax.axis_index("tensor")
    d = lax.axis_index("dp")
    section = lax.axis_index("pipe")
    outer = d // 2
    core = d % 2
    place = jnp.stack([t, outer, core, section]).astype(jnp.int32)

    def to_core(value):
        return lax.ppermute(value, "dp", [(i, i ^ 1) for i in range(4)])

    def to_outer(value):
        return lax.ppermute(value, "dp", [(i, i ^ 2) for i in range(4)])

    def along(value, *pairs):
        return lax.ppermute(value, "tensor", pairs)

    mixes = mix[0, :, 0]
    micro, tokens, head_cols = mixes.shape
    own_rows = tokens // 4
    rows = 2 * own_rows
    weight = frozen_weight[0]
    right = right_factor[0, 0]
    left = left_factor[0, 0]
    rank, width = left.shape
    sub = rank // 4
    half = width // 2
    features = 4 * width
    slots = (d, d ^ 1)

    other_mixes = to_outer(mixes)
    weights = (weight, to_core(weight))

    def swapped(values):
        return [values[0]] + [along(values[o], *[(i, i ^ o) for i in range(4)]) for o in (1, 2, 3)]

    def of_block(values, block):
        return lax.select_n(t ^ block, *values)

    cut = [
        lax.dynamic_slice(left, ((t ^ o) * sub, core * half), (sub, half)) for o in range(4)
    ]
    laid, right_here = small(
        layout_kernel,
        [((micro, 4, own_rows, head_cols), BF16), (right.shape, BF16)],
        [],
        place,
        mixes,
        right,
    )
    met = swapped(cut)
    met[2] = after(met[2], laid, right_here)
    own_half = jnp.stack([of_block(met, 2 * outer + i) for i in range(2)])
    other_half = to_core(own_half)

    own, next_one, *partial, mix_rows, left_rows, own_piece = project(
        place, laid, other_mixes, weights, right_here, own_half, other_half
    )

    swaps = [[(i, i ^ o) for i in range(4)] for o in range(4)]
    shape = (2, rows, width)
    passed, mids, crossings = [], [], []
    for m in range(micro):
        last = partial[micro + m]
        passed.append(along(last, (0, 1), (3, 2)))
        mids.append(along(last, (1, 2), (2, 1)))
    for m in range(micro):
        two_away = partial[m]
        carried = two_away.shape[2] - width
        (ahead,) = small(
            ahead_kernel,
            [((2, rows, width + 2 * carried), BF16)],
            [],
            place,
            two_away,
            after(passed[m], *mids, *passed),
        )
        crossings.append(along(ahead, *swaps[2]))
    beside = along(next_one, *swaps[1])
    permuted = (own_piece, beside, crossings[0], crossings[0], mids[0])

    layout = (2, micro, 2, own_rows, width)
    here, there = small(
        cut_kernel,
        [(layout, BF16)] * 2,
        [],
        place,
        after(hidden_in[:, 0], own),
        cotangent[:, 0],
    )
    arrived = to_outer(there)
    gain = norm_gain.astype(F32).reshape(1, features)

    update, kept, sent = small(
        update_kernel,
        [((micro, *shape), F32), (shape, BF16), (shape, BF16)],
        [],
        place,
        own,
        after(beside, arrived),
        *mids,
        *crossings,
    )

    def to_section(value):
        return lax.ppermute(value, "pipe", [(0, 1), (1, 0)])

    leaving, final, sums = small(
        state_kernel,
        [(shape, BF16)] * 2 + [((rows, 128), F32)],
        [],
        place,
        here,
        arrived,
        gain,
        update,
        to_section(sent),
    )
    (grad,) = small(
        norm_kernel, [(shape, BF16)], [], place, here, arrived, gain, final, sums, to_outer(sums)
    )

    opposite = along(grad, *swaps[2])
    beside = along(grad, *swaps[1])
    own_there = to_section(grad)
    before = to_section(after(kept, grad))
    relay = after(opposite, beside)
    mid = along(after(grad, beside), (1, 2), (2, 1))
    farthest = along(relay, (1, 0), (2, 3))
    opposite_there = to_section(after(opposite, own_there))
    by_group, others = small(
        later_kernel,
        [((micro, 2, own_rows, width), BF16)] * 2,
        [],
        place,
        here,
        arrived,
        update,
        before,
        leaving,
    )
    others = to_outer(others)
    beside_there = to_section(beside)
    (section_out,) = small(
        gather_kernel,
        [((micro, own_rows, features), BF16)],
        [],
        place,
        by_group,
        others,
        cost=pl.CostEstimate(flops=3 * 10**9, bytes_accessed=0, transcendentals=0),
    )
    (last,) = small(
        join_kernel, [(shape, BF16)], [], place, mid, after(farthest, beside_there, opposite_there),
        cost=pl.CostEstimate(flops=5 * 10**9, bytes_accessed=0, transcendentals=0),
    )
    pieces = [grad, beside, relay, last]
    pieces += [own_there, beside_there, opposite_there, to_section(after(last, section_out))]
    mix_here, first_sent, second_sent, kept_factors, sent_factors = back(
        place, pieces, weights, left_rows, right, mix_rows, permuted
    )
    (joined,) = small(
        sum_kernel, [(kept_factors.shape, BF16)], [], place, kept_factors, to_core(sent_factors)
    )
    other_joined = to_outer(joined)
    best = jnp.where(outer == t // 2, joined[:rank], other_joined[:rank])
    (grad_right,) = small(
        right_kernel,
        [((head_cols, rank), F32)],
        [pltpu.VMEM((rank, head_cols), F32)],
        place,
        joined,
        other_joined,
    )
    (grad_left,) = small(
        left_kernel,
        [((rank, width), F32)],
        [],
        place,
        best,
        after(to_core(best), grad_right),
        cost=pl.CostEstimate(flops=8 * 10**9, bytes_accessed=0, transcendentals=0),
    )
    (first_mix,) = small(
        functools.partial(add_kernel, 0),
        [(second_sent.shape, BF16)],
        [],
        place,
        mix_here,
        to_outer(first_sent),
        cost=pl.CostEstimate(flops=15 * 10**9, bytes_accessed=0, transcendentals=0),
    )
    (grad_mix,) = small(
        place_kernel,
        [((micro, tokens, head_cols), BF16)],
        [],
        place,
        first_mix,
        mix_here,
        after(to_outer(after(second_sent, joined)), grad_right),
        cost=pl.CostEstimate(flops=5 * 10**9, bytes_accessed=0, transcendentals=0),
    )
    grad_mix = grad_mix.reshape(1, micro, 1, tokens, head_cols)

    return (
        section_out.reshape(1, micro, 1, own_rows, features),
        grad_mix,
        grad_right.reshape(1, 1, head_cols, rank),
        grad_left.reshape(1, 1, rank, width),
    )


def on_device_general(mix, hidden_in, cotangent, frozen_weight, right_factor, left_factor, norm_gain):
    blocks = lax.axis_size("tensor")
    parts = lax.axis_size("dp")
    sections = lax.axis_size("pipe")
    t = lax.axis_index("tensor")
    d = lax.axis_index("dp")
    section = lax.axis_index("pipe")
    outers = parts // 2
    outer = d // 2
    core = d % 2

    def to_core(value):
        return lax.ppermute(value, "dp", [(i, i ^ 1) for i in range(parts)])

    def to_outer(value, step):
        return lax.ppermute(value, "dp", [(i, (i + 2 * step) % parts) for i in range(parts)])

    def to_block(value, step):
        return lax.ppermute(value, "tensor", [(i, (i + step) % blocks) for i in range(blocks)])

    def of_cores(value):
        return jnp.where(core == 0, value, value[::-1])

    mixes = mix[0, :, 0]
    micro, tokens, head_cols = mixes.shape
    own_rows = tokens // blocks
    weight = frozen_weight[0]
    right = right_factor[0, 0]
    left = left_factor[0, 0]
    rank, block_cols = left.shape
    sub = rank // blocks
    width = weight.shape[1]
    features = width * parts
    rows = outers * own_rows
    all_rows = blocks * rows
    per_block = parts // blocks
    slots = (d, d ^ 1)

    def block_of(part):
        return part // per_block

    weights = (weight, to_core(weight))
    own = mixes.reshape(micro, blocks, 1, own_rows, head_cols)
    taken = [
        jnp.concatenate(
            [own[m]] + [to_outer(own[m], step) for step in range(1, outers)], axis=1
        ).reshape(all_rows, head_cols)
        for m in range(micro)
    ]
    own_inner = dot(right, mixes.reshape(micro * tokens, head_cols), 0, 1).astype(BF16)
    pieces = lax.all_to_all(
        jnp.concatenate(
            [
                left.reshape(blocks, sub, block_cols),
                own_inner.reshape(blocks, sub, micro * tokens),
            ],
            axis=2,
        ),
        "tensor",
        split_axis=0,
        concat_axis=0,
        tiled=True,
    )
    left_slots = [
        columns(pick(pieces, block_of(part)), (part % per_block) * width, width) for part in slots
    ]
    right_slots = [columns(right, block_of(part) * sub, sub) for part in slots]
    own_permuted = pieces[:, :, block_cols:].reshape(rank, micro * tokens)
    own_permuted = after(own_permuted, *taken)
    permuted = [own_permuted] + [to_outer(own_permuted, step) for step in range(1, outers)]

    inners = [dot(taken[m], right, 1, 0).astype(BF16) for m in range(micro)]
    partial = [
        jnp.stack(
            [
                (
                    dot(taken[m], weights[slot], 1, 0)
                    + dot(
                        columns(inners[m], block_of(part) * sub, sub), left_slots[slot], 1, 0
                    )
                ).astype(BF16)
                for slot, part in enumerate(slots)
            ]
        ).reshape(2, blocks, rows, width)
        for m in range(micro)
    ]

    def shard(m, index):
        return pick(partial[m], index, 1)

    updates_here = []
    for m in range(micro):
        total = shard(m, t).astype(F32)
        for step in range(1, blocks):
            total = total + to_block(shard(m, (t + step) % blocks), step).astype(F32)
        updates_here.append(total)

    hidden_late = after(hidden_in, *taken)

    def by_column(step):
        target = (outer + step) % outers
        cuts = [2 * target + core, 2 * target + (1 - core)]
        return jnp.stack(
            [
                jnp.stack([columns(value[:, 0], part * width, width) for part in cuts])
                for value in (hidden_late, cotangent)
            ]
        )

    entering = jnp.concatenate(
        [by_column(0)] + [to_outer(by_column(step), step) for step in range(1, outers)], axis=3
    )
    gains = jnp.stack([columns(norm_gain, part * width, width) for part in slots]).astype(F32)

    grads = []
    leaving = []
    for m in range(micro):
        sent = updates_here[m].astype(BF16)
        updates = [updates_here[m]] + [
            lax.ppermute(
                sent, "pipe", [(i, (i + step) % sections) for i in range(sections)]
            ).astype(F32)
            for step in range(1, sections)
        ]
        state = entering[0, :, m]
        kept = state
        for s in range(sections):
            add = updates[0]
            for step in range(1, sections):
                add = jnp.where((section - step) % sections == s, updates[step], add)
            state = (state.astype(F32) + add).astype(BF16)
            kept = jnp.where(section == s, state, kept)
        leaving.append(kept)
        final = state.astype(F32)
        upstream = entering[1, :, m].astype(F32) * gains[:, None, :]
        sums = jnp.stack(
            [jnp.sum(final * final, axis=(0, 2)), jnp.sum(upstream * final, axis=(0, 2))]
        ).reshape(2, outers, own_rows)
        total = sums
        for step in range(1, outers):
            total = total + jnp.roll(to_outer(sums, step), step, axis=1)
        total = total.reshape(2, rows) / features
        scale = lax.rsqrt(total[0] + 1e-05)
        shrink = scale * scale * total[1]
        grads.append(
            (scale[None, :, None] * (upstream - final * shrink[None, :, None])).astype(BF16)
        )

    full = [
        jnp.concatenate(
            [grads[m]] + [to_block(grads[m], step) for step in range(1, blocks)], axis=1
        )
        for m in range(micro)
    ]
    order = [[(t - step) % blocks for step in range(blocks)]] * micro

    outs = []
    for m in range(micro):
        by_group = after(leaving[m], grads[m]).reshape(2, outers, own_rows, width)
        row = jnp.zeros((own_rows, features), BF16)
        for step in range(outers):
            at = (outer + step) % outers
            piece = by_group[:, step]
            if step:
                piece = after(to_outer(piece, outers - step), full[-1])
            for slot in range(2):
                place = (2 * at + (core if slot == 0 else 1 - core)) * width
                row = lax.dynamic_update_slice_in_dim(row, piece[slot], place, 1)
        outs.append(row)
    section_out = jnp.stack(outs).reshape(1, micro, 1, own_rows, features)

    mix_rows = [
        jnp.concatenate(
            [pick(taken[m].reshape(blocks, rows, head_cols), at) for at in order[m]], axis=0
        )
        for m in range(micro)
    ]
    permuted_rows = [
        jnp.concatenate(
            [
                columns(half, m * tokens + at * own_rows, own_rows)
                for at in order[m]
                for half in permuted
            ],
            axis=1,
        )
        for m in range(micro)
    ]

    holder = (t * per_block) // 2
    mix_grads = []
    right_sum = 0.0
    left_sum = 0.0
    for m in range(micro):
        if per_block == 1:
            cols = pick(full[m], jnp.where(t % 2 == core, 0, 1))
        else:
            cols = jnp.concatenate(list(of_cores(full[m])), axis=1)
        left_sum = left_sum + dot(permuted_rows[m], cols, 1, 0)

        inner_grads = [
            dot(full[m][slot], left_slots[slot], 1, 1).astype(BF16) for slot in range(2)
        ]
        if per_block == 1:
            mine = jnp.concatenate(inner_grads, axis=1)
            right_here = jnp.concatenate(right_slots, axis=1)
        else:
            mine = (inner_grads[0].astype(F32) + inner_grads[1].astype(F32)).astype(BF16)
            right_here = right_slots[0]
        right_sum = right_sum + dot(mine, mix_rows[m], 0, 0)

        partial_mix = (
            dot(full[m][0], weights[0], 1, 1)
            + dot(full[m][1], weights[1], 1, 1)
            + dot(mine, right_here, 1, 1)
        ).reshape(blocks, outers, own_rows, head_cols)
        whole = partial_mix[:, 0]
        for step in range(1, outers):
            whole = whole + to_outer(partial_mix[:, step].astype(BF16), outers - step).astype(F32)
        whole = whole.astype(BF16)
        back = order[m]
        mix_grads.append(
            jnp.concatenate([pick(whole, at) for at in back], axis=0)
        )
    grad_mix = jnp.stack(mix_grads).reshape(1, micro, 1, tokens, head_cols)

    half = block_cols // 2
    half_sum = (
        columns(left_sum, core * half, half) + to_core(columns(left_sum, (1 - core) * half, half))
    ).astype(BF16)
    best = half_sum
    for step in range(1, outers):
        pairs = []
        for i in range(blocks):
            at = (i * per_block) // 2
            for c in range(2):
                pairs.append(
                    (i * parts + 2 * at + c, i * parts + 2 * ((at + step) % outers) + c)
                )
        arrived = lax.ppermute(half_sum, ("tensor", "dp"), pairs)
        best = jnp.where((outer - holder) % outers == step, arrived, best)
    there = to_core(best)
    grad_left = jnp.concatenate(list(of_cores(jnp.stack([best, there]))), axis=1).astype(F32)

    if per_block == 1:
        right_sum = of_cores(right_sum.reshape(2, sub, head_cols)).reshape(2 * sub, head_cols)
    right_sum = (right_sum + to_core(right_sum)).astype(BF16)
    wide = jnp.zeros((rank, head_cols), BF16)
    count = right_sum.shape[0]
    for step in range(outers):
        arrived = to_outer(right_sum, step) if step else right_sum
        wide = lax.dynamic_update_slice_in_dim(
            wide, arrived, ((outer - step) % outers) * count, 0
        )
    grad_right = wide.T.astype(F32)

    return (
        section_out,
        grad_mix,
        grad_right.reshape(1, 1, head_cols, rank),
        grad_left.reshape(1, 1, rank, block_cols),
    )


def solution(mesh):
    sizes = (mesh.shape["tensor"], mesh.shape["dp"], mesh.shape["pipe"])
    return jax.shard_map(
        on_device if sizes == (4, 4, 2) else on_device_general,
        mesh=mesh,
        in_specs=(
            P("pipe", None, "dp", None, "tensor"),
            P(None, "dp", "tensor", None),
            P(None, "dp", "tensor", None),
            P("pipe", "tensor", "dp"),
            P("pipe", "tensor", None, None),
            P("pipe", "tensor", None, None),
            P(),
        ),
        out_specs=(
            P("pipe", None, "dp", "tensor", None),
            P("pipe", None, "dp", None, "tensor"),
            P("pipe", "tensor", None, None),
            P("pipe", "tensor", None, None),
        ),
        check_vma=False,
    )
```

```python
import functools

import jax
import jax.numpy as jnp
from jax import lax
from jax.experimental import pallas as pl
from jax.experimental.pallas import tpu as pltpu
from jax.sharding import PartitionSpec as P

F32 = jnp.float32
BF16 = jnp.bfloat16
VMEM = 24 * 2**20
VMEM_ALL = 48 * 2**20
VMEM_SMALL = 10 * 2**20


def dot(left_side, right_side, left_dim, right_dim):
    return lax.dot_general(
        left_side,
        right_side,
        (((left_dim,), (right_dim,)), ((), ())),
        preferred_element_type=F32,
    )


def pick(value, index, dim=0):
    return lax.dynamic_index_in_dim(value, index, dim, keepdims=False)


def columns(value, start, size):
    return lax.dynamic_slice_in_dim(value, start, size, value.ndim - 1)


def after(value, *others):
    return lax.optimization_barrier((value, *others))[0]


NO_COST = pl.CostEstimate(flops=0, bytes_accessed=0, transcendentals=0)


def small(kernel, outs, scratch, place, *values, cost=NO_COST):
    vmem = pl.BlockSpec(memory_space=pltpu.VMEM)
    return pl.pallas_call(
        kernel,
        in_specs=[pl.BlockSpec(memory_space=pltpu.SMEM)] + [vmem] * len(values),
        out_specs=[vmem] * len(outs),
        out_shape=[jax.ShapeDtypeStruct(shape, dtype) for shape, dtype in outs],
        scratch_shapes=scratch,
        compiler_params=pltpu.CompilerParams(vmem_limit_bytes=VMEM_SMALL),
        cost_estimate=cost,
    )(place, *values)


def at_multiple(index, size):
    return pl.ds(pl.multiple_of(index * size, size), size)


def cut_kernel(place, hidden, cotangent, here, there):
    outer, core = place[1], place[2]
    width = here.shape[4]
    for out, target in ((here, outer), (there, 1 - outer)):
        for which, source in enumerate((hidden, cotangent)):
            for m in range(source.shape[0]):
                for slot in range(2):
                    out[which, m, slot] = source[m, :, at_multiple(2 * target + (core ^ slot), width)]


def ahead_kernel(place, two_away, passed, ahead):
    carried = ahead.shape[2] - two_away.shape[2]
    width = two_away.shape[2] - carried
    ahead[:, :, :width] = (
        two_away[:, :, :width].astype(F32) + passed[:, :, :width].astype(F32)
    ).astype(BF16)
    if carried:
        ahead[:, :, width : width + carried] = two_away[:, :, width:]
        ahead[:, :, width + carried :] = passed[:, :, width:]


def update_kernel(place, own, beside, *refs):
    micro, _, _, width = own.shape
    mids, crossings, (update, kept, sent) = refs[:micro], refs[micro : 2 * micro], refs[2 * micro :]
    for m in range(micro):
        total = (own[m].astype(F32) + beside[m, :, :, :width].astype(F32)) + (
            mids[m][:, :, :width].astype(F32) + crossings[m][:, :, :width].astype(F32)
        )
        update[m] = total
        (sent if m else kept)[...] = total.astype(BF16)


def state_kernel(place, here, arrived, gain, update, other, leaving, final, sums):
    outer, core, section = place[1], place[2], place[3]
    own_rows, width = here.shape[3:]
    for group, source in enumerate((here, arrived)):
        at = pl.ds(group * own_rows, own_rows)
        squares = jnp.zeros((own_rows, 1), F32)
        products = jnp.zeros((own_rows, 1), F32)
        for slot in range(2):
            mine = update[0, slot, at, :]
            others = other[slot, at, :].astype(F32)
            first_add = jnp.where(section == 0, mine, others)
            second_add = jnp.where(section == 0, others, mine)
            first = (source[0, section, slot].astype(F32) + first_add).astype(BF16)
            second = (first.astype(F32) + second_add).astype(BF16)
            leaving[slot, at, :] = jnp.where(section == 0, first, second)
            final[slot, at, :] = second
            value = second.astype(F32)
            upstream = source[1, section, slot].astype(F32) * gain[:, at_multiple(2 * outer + (core ^ slot), width)]
            squares += jnp.sum(value * value, axis=1, keepdims=True)
            products += jnp.sum(value * upstream, axis=1, keepdims=True)
        lane = lax.broadcasted_iota(jnp.int32, (own_rows, sums.shape[1]), 1)
        sums[at, :] = jnp.where(lane < sums.shape[1] // 2, squares, products)


def later_kernel(place, here, arrived, update, before, leaving, own, sent):
    section = place[3]
    own_rows = here.shape[3]
    for group, (source, out) in enumerate(((here, own), (arrived, sent))):
        at = pl.ds(group * own_rows, own_rows)
        for slot in range(2):
            start = source[0, 1 - section, slot].astype(F32)
            entering = (start + before[slot, at, :].astype(F32)).astype(BF16).astype(F32)
            entering = jnp.where(section == 0, start, entering)
            out[0, slot] = leaving[slot, at, :]
            out[1, slot] = (entering + update[1, slot, at, :]).astype(BF16)


def norm_kernel(place, here, arrived, gain, final, sums, other_sums, grad):
    outer, core, section = place[1], place[2], place[3]
    own_rows, width = here.shape[3:]
    lanes = sums.shape[1]
    for group, source in enumerate((here, arrived)):
        at = pl.ds(group * own_rows, own_rows)
        total = sums[at, :] + other_sums[pl.ds((1 - group) * own_rows, own_rows), :]
        total = total * (1.0 / (4 * width))
        scale = lax.rsqrt(total[:, :1] + 1e-05)
        shrink = scale * scale * total[:, lanes // 2 : lanes // 2 + 1]
        for slot in range(2):
            upstream = source[1, section, slot].astype(F32) * gain[:, at_multiple(2 * outer + (core ^ slot), width)]
            value = final[slot, at, :].astype(F32)
            grad[slot, at, :] = (scale * (upstream - value * shrink)).astype(BF16)


def join_kernel(place, mid, farthest, last):
    last[...] = mid[...] + farthest[...]


def layout_kernel(place, mixes, right, own_rows, right_here):
    t, section = place[0], place[3]
    micro, _, rows, _ = own_rows.shape
    for m in range(micro):
        for r in range(4):
            own_rows[m, r] = mixes[m ^ section, at_multiple(t ^ r, rows), :]
    right_here[...] = right[...]


def project_kernel(place, own_mix, other_mix, own_weight, other_weight, right, own_half, other_half, *refs):
    own, next_one, *sums, mix_rows, left_rows, piece, inner, turned = refs
    t, outer, core, section = place[0], place[1], place[2], place[3]
    micro, shards = mix_rows.shape[0], 4
    sub, half = own_half.shape[1:]
    step = pl.program_id(0)
    rows = own.shape[2]
    own_rows = rows // 2
    size = shards * rows
    tile = own_weight.shape[1]

    @pl.when(step == 0)
    def _():
        for m in range(micro):
            for r in range(shards):
                at = at_multiple(t ^ r, own_rows)
                mix_rows[m, pl.ds(r * rows, own_rows), :] = own_mix[m, r]
                mix_rows[m, pl.ds(r * rows + own_rows, own_rows), :] = other_mix[m ^ section, at, :]
        product = jnp.dot(
            mix_rows[...].reshape(micro * size, -1), right[...], preferred_element_type=F32
        )
        inner[...] = product.astype(BF16)
        width = left_rows.shape[2]
        for o in range(shards):
            lines = [
                product[m * size + (r ^ o) * rows :][:rows] for m in range(micro) for r in range(shards)
            ]
            turned[...] = jnp.concatenate(lines, axis=0).T
            cut = turned[at_multiple(t ^ o, sub), :].astype(BF16)
            for m in range(micro):
                beside = cut[:, m * size : (m + 1) * size]
                if o == 0:
                    piece[m] = beside
                elif o == 1:
                    next_one[0, m, :, pl.ds(width, size)] = beside
                    next_one[1, m, :, pl.ds(width, size)] = jnp.zeros_like(beside)
                else:
                    sums[(o - 2) * micro][m, :, pl.ds(width, size)] = beside
        left_rows[...] = jnp.zeros_like(left_rows)
        for slot in range(2):
            part = core ^ slot
            at = pl.ds(pl.multiple_of((2 * outer + part) * sub, sub), sub)
            left_rows[slot, at, pl.ds(pl.multiple_of(core * half, half), half)] = own_half[part]
            left_rows[slot, at, pl.ds(pl.multiple_of((1 - core) * half, half), half)] = other_half[part]

    at = pl.ds(pl.multiple_of(step * tile, tile), tile)
    lines = mix_rows[...].reshape(micro * size, -1)
    for slot, weight in enumerate((own_weight, other_weight)):
        product = jnp.dot(lines, weight[...], preferred_element_type=F32) + jnp.dot(
            inner[...], left_rows[slot, :, at], preferred_element_type=F32
        )
        for m in range(micro):
            for r in range(shards):
                at_row = m * size + r * rows
                value = product[at_row : at_row + rows].astype(BF16)
                if r == 0:
                    own[m, slot] = value
                elif r == 1:
                    next_one[m, slot, :, at] = value
                else:
                    sums[(r - 2) * micro + m][slot, :, at] = value


def weight_specs(head_cols, tile):
    return [pl.BlockSpec((head_cols, tile), lambda i: (0, i))] * 2


def whole(*shape):
    return pl.BlockSpec(shape, lambda i: (0,) * len(shape))


def project(place, own_mix, other_mix, weights, right, own_half, other_half):
    micro, tokens, head_cols = other_mix.shape
    width = weights[0].shape[1]
    rank = right.shape[1]
    tile = 1024
    tiles = width // tile
    rows = tokens // 2
    size = 4 * rows
    carrying = (2, rows, width + size)
    plain = (2, rows, width)
    shapes = [(micro, *carrying)] + [carrying, *[plain] * (micro - 1)] * 2
    shapes += [(micro, size, head_cols), (2, rank, width), (2, rank // 4, size)]
    return pl.pallas_call(
        project_kernel,
        grid=(tiles,),
        in_specs=[
            pl.BlockSpec(memory_space=pltpu.SMEM),
            whole(*own_mix.shape),
            whole(*other_mix.shape),
            *weight_specs(head_cols, tile),
            whole(*right.shape),
            whole(*own_half.shape),
            whole(*own_half.shape),
        ],
        out_specs=[pl.BlockSpec((micro, 2, rows, tile), lambda i: (0, 0, 0, i))]
        + [whole(*shape) for shape in shapes],
        out_shape=[jax.ShapeDtypeStruct((micro, 2, rows, width), BF16)]
        + [jax.ShapeDtypeStruct(shape, BF16) for shape in shapes],
        scratch_shapes=[
            pltpu.VMEM((micro * size, rank), BF16),
            pltpu.VMEM((rank, micro * size), F32),
        ],
        compiler_params=pltpu.CompilerParams(vmem_limit_bytes=VMEM_ALL),
        cost_estimate=NO_COST,
    )(place, own_mix, other_mix, *weights, right, own_half, other_half)


def back_kernel(micro, place, *refs):
    pieces, refs = refs[: 4 * micro], refs[4 * micro :]
    (own_weight, other_weight), refs = refs[:2], refs[2:]
    left_rows, right, mix_rows = refs[:3]
    (own_piece, beside_piece, crossed_piece, relayed_piece, mid_piece), refs = refs[3:8], refs[8:]
    mix_here, *mix_sent, kept_factors, sent_factors, total, inner_grad, permuted, right_all = refs
    factors = (kept_factors, sent_factors)
    rank = permuted.shape[0]
    t, outer, core, section = place[0], place[1], place[2], place[3]
    step = pl.program_id(0)
    rows = pieces[0].shape[1]
    own_rows = rows // 2
    tile = own_weight.shape[1]
    half = factors[0].shape[1]

    @pl.when(step == 0)
    def _():
        total[...] = jnp.zeros_like(total)
        inner_grad[...] = jnp.zeros_like(inner_grad)
        _, sub, size = own_piece.shape
        for m in range(micro):
            cut = pl.ds(m * size, size)
            last = mid_piece[m] + relayed_piece[m]
            for o, value in enumerate((own_piece[m], beside_piece[0, m], crossed_piece[m], last)):
                permuted[at_multiple(t ^ o, sub), cut] = value

    grads = []
    for slot in range(2):
        parts = []
        for m in range(micro):
            parts += [piece[slot] for piece in pieces[4 * m : 4 * m + 4]]
        grads.append(jnp.concatenate(parts, axis=0))
    over = (((1,), (1,)), ((), ()))
    total[...] += lax.dot_general(
        own_weight[...], grads[0], over, preferred_element_type=F32
    ) + lax.dot_general(other_weight[...], grads[1], over, preferred_element_type=F32)
    inner_grad[...] += lax.dot_general(
        grads[0], left_rows[0], over, preferred_element_type=F32
    ) + lax.dot_general(grads[1], left_rows[1], over, preferred_element_type=F32)

    at = step * tile
    cut = pl.ds(pl.multiple_of(at % half, tile), tile)
    block = jnp.where(((t & 1) ^ core) == 0, grads[0], grads[1])
    product = jnp.dot(permuted[...], block, preferred_element_type=F32)
    for i, factor in enumerate(factors):

        @pl.when((at // half) ^ core == i)
        def _():
            factor[:rank, cut] = product


    @pl.when(step == pl.num_programs(0) - 1)
    def _():
        mine = inner_grad[...].astype(BF16)
        everything = total[...].T + lax.dot_general(
            mine, right[...], over, preferred_element_type=F32
        )
        for m in range(micro):
            for r in range(4):
                at = at_multiple(t ^ r, own_rows)
                lines = everything[(4 * m + r) * rows :][:rows]
                mix_here[m, at, :] = lines[:own_rows]
                mix_sent[m][at, :] = lines[own_rows:].astype(BF16)
        right_all[...] = lax.dot_general(
            mine,
            mix_rows[...].reshape(mine.shape[0], -1),
            (((0,), (0,)), ((), ())),
            preferred_element_type=F32,
        )
        for i in range(2):
            factors[i][rank:, :] = right_all[at_multiple(outer, rank // 2), :]


def back(place, pieces, weights, left_rows, right, mix_rows, permuted):
    _, rows, width = pieces[0].shape
    head_cols, rank = right.shape
    micro, size, _ = mix_rows.shape
    half = width // 2
    tile = 1024
    tiles = width // tile
    shapes = [
        jax.ShapeDtypeStruct((micro, size // 2, head_cols), F32),
        *[jax.ShapeDtypeStruct((size // 2, head_cols), BF16)] * micro,
        jax.ShapeDtypeStruct((rank + rank // 2, half), F32),
        jax.ShapeDtypeStruct((rank + rank // 2, half), F32),
    ]
    return pl.pallas_call(
        functools.partial(back_kernel, micro),
        grid=(tiles,),
        in_specs=[pl.BlockSpec(memory_space=pltpu.SMEM)]
        + [pl.BlockSpec((2, rows, tile), lambda i: (0, 0, i))] * (4 * micro)
        + weight_specs(head_cols, tile)
        + [
            pl.BlockSpec((2, rank, tile), lambda i: (0, 0, i)),
            whole(*right.shape),
            whole(*mix_rows.shape),
        ]
        + [
            whole(*permuted[0].shape),
            pl.BlockSpec((1, 2, rows, size), lambda i: (0, 0, 0, width // size)),
            pl.BlockSpec((2, rows, size), lambda i: (0, 0, width // size)),
            pl.BlockSpec((2, rows, size), lambda i: (0, 0, width // size + 1)),
            pl.BlockSpec((2, rows, size), lambda i: (0, 0, width // size)),
        ],
        out_specs=[whole(*shape.shape) for shape in shapes],
        out_shape=shapes,
        scratch_shapes=[
            pltpu.VMEM((head_cols, micro * size), F32),
            pltpu.VMEM((micro * size, rank), F32),
            pltpu.VMEM((rank, micro * size), BF16),
            pltpu.VMEM((rank, head_cols), F32),
        ],
        compiler_params=pltpu.CompilerParams(vmem_limit_bytes=VMEM),
        cost_estimate=NO_COST,
    )(place, *pieces, *weights, left_rows, right, mix_rows, *permuted)


def gather_kernel(place, here, arrived, out):
    outer, core, section = place[1], place[2], place[3]
    width = arrived.shape[3]
    for m in range(here.shape[0]):
        for slot in range(2):
            part = core ^ slot
            at = pl.ds(pl.multiple_of((2 * outer + part) * width, width), width)
            out[m ^ section, :, at] = here[m, slot]
            at = pl.ds(pl.multiple_of((2 * (1 - outer) + part) * width, width), width)
            out[m ^ section, :, at] = arrived[m, slot]


def add_kernel(m, place, here, arrived, total):
    total[...] = (here[m] + arrived[...].astype(F32)).astype(BF16)


def place_kernel(place, first, here, arrived, total):
    section = place[3]
    total[section] = first[...]
    total[1 - section] = (here[1] + arrived[...].astype(F32)).astype(BF16)


def sum_kernel(place, kept, arrived, total):
    total[...] = (kept[...] + arrived[...]).astype(BF16)


def right_kernel(place, own_right, other_right, grad_right, wide):
    outer = place[1]
    rank = wide.shape[0]
    wide[at_multiple(outer, rank // 2), :] = own_right[rank:, :].astype(F32)
    wide[at_multiple(1 - outer, rank // 2), :] = other_right[rank:, :].astype(F32)
    grad_right[...] = wide[...].T


def on_device(mix, hidden_in, cotangent, frozen_weight, right_factor, left_factor, norm_gain):
    t = lax.axis_index("tensor")
    d = lax.axis_index("dp")
    section = lax.axis_index("pipe")
    outer = d // 2
    core = d % 2
    place = jnp.stack([t, outer, core, section]).astype(jnp.int32)

    def to_core(value):
        return lax.ppermute(value, "dp", [(i, i ^ 1) for i in range(4)])

    def to_outer(value):
        return lax.ppermute(value, "dp", [(i, i ^ 2) for i in range(4)])

    def along(value, *pairs):
        return lax.ppermute(value, "tensor", pairs)

    mixes = mix[0, :, 0]
    micro, tokens, head_cols = mixes.shape
    own_rows = tokens // 4
    rows = 2 * own_rows
    weight = frozen_weight[0]
    right = right_factor[0, 0]
    left = left_factor[0, 0]
    rank, width = left.shape
    sub = rank // 4
    half = width // 2
    features = 4 * width
    slots = (d, d ^ 1)

    other_mixes = to_outer(mixes)
    weights = (weight, to_core(weight))

    def swapped(values):
        return [values[0]] + [along(values[o], *[(i, i ^ o) for i in range(4)]) for o in (1, 2, 3)]

    def of_block(values, block):
        return lax.select_n(t ^ block, *values)

    cut = [
        lax.dynamic_slice(left, ((t ^ o) * sub, core * half), (sub, half)) for o in range(4)
    ]
    laid, right_here = small(
        layout_kernel,
        [((micro, 4, own_rows, head_cols), BF16), (right.shape, BF16)],
        [],
        place,
        mixes,
        right,
    )
    met = swapped(cut)
    met[2] = after(met[2], laid, right_here)
    own_half = jnp.stack([of_block(met, 2 * outer + i) for i in range(2)])
    other_half = to_core(own_half)

    own, next_one, *partial, mix_rows, left_rows, own_piece = project(
        place, laid, other_mixes, weights, right_here, own_half, other_half
    )

    swaps = [[(i, i ^ o) for i in range(4)] for o in range(4)]
    shape = (2, rows, width)
    passed, mids, crossings = [], [], []
    for m in range(micro):
        last = partial[micro + m]
        passed.append(along(last, (0, 1), (3, 2)))
        mids.append(along(last, (1, 2), (2, 1)))
    for m in range(micro):
        two_away = partial[m]
        carried = two_away.shape[2] - width
        (ahead,) = small(
            ahead_kernel,
            [((2, rows, width + 2 * carried), BF16)],
            [],
            place,
            two_away,
            after(passed[m], *mids, *passed),
        )
        crossings.append(along(ahead, *swaps[2]))
    beside = along(next_one, *swaps[1])
    permuted = (own_piece, beside, crossings[0], crossings[0], mids[0])

    layout = (2, micro, 2, own_rows, width)
    here, there = small(
        cut_kernel,
        [(layout, BF16)] * 2,
        [],
        place,
        after(hidden_in[:, 0], own),
        cotangent[:, 0],
    )
    arrived = to_outer(there)
    gain = norm_gain.astype(F32).reshape(1, features)

    update, kept, sent = small(
        update_kernel,
        [((micro, *shape), F32), (shape, BF16), (shape, BF16)],
        [],
        place,
        own,
        after(beside, arrived),
        *mids,
        *crossings,
    )

    def to_section(value):
        return lax.ppermute(value, "pipe", [(0, 1), (1, 0)])

    leaving, final, sums = small(
        state_kernel,
        [(shape, BF16)] * 2 + [((rows, 128), F32)],
        [],
        place,
        here,
        arrived,
        gain,
        update,
        to_section(sent),
    )
    (grad,) = small(
        norm_kernel, [(shape, BF16)], [], place, here, arrived, gain, final, sums, to_outer(sums)
    )

    opposite = along(grad, *swaps[2])
    beside = along(grad, *swaps[1])
    own_there = to_section(grad)
    before = to_section(after(kept, grad))
    relay = after(opposite, beside)
    mid = along(after(grad, beside), (1, 2), (2, 1))
    farthest = along(relay, (1, 0), (2, 3))
    opposite_there = to_section(after(opposite, own_there))
    by_group, others = small(
        later_kernel,
        [((micro, 2, own_rows, width), BF16)] * 2,
        [],
        place,
        here,
        arrived,
        update,
        before,
        leaving,
    )
    others = to_outer(others)
    beside_there = to_section(beside)
    (section_out,) = small(
        gather_kernel,
        [((micro, own_rows, features), BF16)],
        [],
        place,
        by_group,
        others,
        cost=pl.CostEstimate(flops=3 * 10**9, bytes_accessed=0, transcendentals=0),
    )
    (last,) = small(
        join_kernel, [(shape, BF16)], [], place, mid, after(farthest, beside_there, opposite_there),
        cost=pl.CostEstimate(flops=5 * 10**9, bytes_accessed=0, transcendentals=0),
    )
    pieces = [grad, beside, relay, last]
    pieces += [own_there, beside_there, opposite_there, to_section(after(last, section_out))]
    mix_here, first_sent, second_sent, kept_factors, sent_factors = back(
        place, pieces, weights, left_rows, right, mix_rows, permuted
    )
    (joined,) = small(
        sum_kernel, [(kept_factors.shape, BF16)], [], place, kept_factors, to_core(sent_factors)
    )
    other_joined = to_outer(joined)
    best = jnp.where(outer == t // 2, joined[:rank], other_joined[:rank])
    (grad_right,) = small(
        right_kernel,
        [((head_cols, rank), F32)],
        [pltpu.VMEM((rank, head_cols), F32)],
        place,
        joined,
        other_joined,
    )
    there = after(to_core(best), grad_right)
    grad_left = jnp.where(
        core == 0,
        jnp.concatenate([best, there], axis=1),
        jnp.concatenate([there, best], axis=1),
    ).astype(F32)
    (first_mix,) = small(
        functools.partial(add_kernel, 0),
        [(second_sent.shape, BF16)],
        [],
        place,
        mix_here,
        to_outer(first_sent),
        cost=pl.CostEstimate(flops=15 * 10**9, bytes_accessed=0, transcendentals=0),
    )
    (grad_mix,) = small(
        place_kernel,
        [((micro, tokens, head_cols), BF16)],
        [],
        place,
        first_mix,
        mix_here,
        after(to_outer(after(second_sent, joined)), grad_right),
        cost=pl.CostEstimate(flops=5 * 10**9, bytes_accessed=0, transcendentals=0),
    )
    grad_mix = grad_mix.reshape(1, micro, 1, tokens, head_cols)

    return (
        section_out.reshape(1, micro, 1, own_rows, features),
        grad_mix,
        grad_right.reshape(1, 1, head_cols, rank),
        grad_left.reshape(1, 1, rank, width),
    )


def on_device_general(mix, hidden_in, cotangent, frozen_weight, right_factor, left_factor, norm_gain):
    blocks = lax.axis_size("tensor")
    parts = lax.axis_size("dp")
    sections = lax.axis_size("pipe")
    t = lax.axis_index("tensor")
    d = lax.axis_index("dp")
    section = lax.axis_index("pipe")
    outers = parts // 2
    outer = d // 2
    core = d % 2

    def to_core(value):
        return lax.ppermute(value, "dp", [(i, i ^ 1) for i in range(parts)])

    def to_outer(value, step):
        return lax.ppermute(value, "dp", [(i, (i + 2 * step) % parts) for i in range(parts)])

    def to_block(value, step):
        return lax.ppermute(value, "tensor", [(i, (i + step) % blocks) for i in range(blocks)])

    def of_cores(value):
        return jnp.where(core == 0, value, value[::-1])

    mixes = mix[0, :, 0]
    micro, tokens, head_cols = mixes.shape
    own_rows = tokens // blocks
    weight = frozen_weight[0]
    right = right_factor[0, 0]
    left = left_factor[0, 0]
    rank, block_cols = left.shape
    sub = rank // blocks
    width = weight.shape[1]
    features = width * parts
    rows = outers * own_rows
    all_rows = blocks * rows
    per_block = parts // blocks
    slots = (d, d ^ 1)

    def block_of(part):
        return part // per_block

    weights = (weight, to_core(weight))
    own = mixes.reshape(micro, blocks, 1, own_rows, head_cols)
    taken = [
        jnp.concatenate(
            [own[m]] + [to_outer(own[m], step) for step in range(1, outers)], axis=1
        ).reshape(all_rows, head_cols)
        for m in range(micro)
    ]
    own_inner = dot(right, mixes.reshape(micro * tokens, head_cols), 0, 1).astype(BF16)
    pieces = lax.all_to_all(
        jnp.concatenate(
            [
                left.reshape(blocks, sub, block_cols),
                own_inner.reshape(blocks, sub, micro * tokens),
            ],
            axis=2,
        ),
        "tensor",
        split_axis=0,
        concat_axis=0,
        tiled=True,
    )
    left_slots = [
        columns(pick(pieces, block_of(part)), (part % per_block) * width, width) for part in slots
    ]
    right_slots = [columns(right, block_of(part) * sub, sub) for part in slots]
    own_permuted = pieces[:, :, block_cols:].reshape(rank, micro * tokens)
    own_permuted = after(own_permuted, *taken)
    permuted = [own_permuted] + [to_outer(own_permuted, step) for step in range(1, outers)]

    inners = [dot(taken[m], right, 1, 0).astype(BF16) for m in range(micro)]
    partial = [
        jnp.stack(
            [
                (
                    dot(taken[m], weights[slot], 1, 0)
                    + dot(
                        columns(inners[m], block_of(part) * sub, sub), left_slots[slot], 1, 0
                    )
                ).astype(BF16)
                for slot, part in enumerate(slots)
            ]
        ).reshape(2, blocks, rows, width)
        for m in range(micro)
    ]

    def shard(m, index):
        return pick(partial[m], index, 1)

    updates_here = []
    for m in range(micro):
        total = shard(m, t).astype(F32)
        for step in range(1, blocks):
            total = total + to_block(shard(m, (t + step) % blocks), step).astype(F32)
        updates_here.append(total)

    hidden_late = after(hidden_in, *taken)

    def by_column(step):
        target = (outer + step) % outers
        cuts = [2 * target + core, 2 * target + (1 - core)]
        return jnp.stack(
            [
                jnp.stack([columns(value[:, 0], part * width, width) for part in cuts])
                for value in (hidden_late, cotangent)
            ]
        )

    entering = jnp.concatenate(
        [by_column(0)] + [to_outer(by_column(step), step) for step in range(1, outers)], axis=3
    )
    gains = jnp.stack([columns(norm_gain, part * width, width) for part in slots]).astype(F32)

    grads = []
    leaving = []
    for m in range(micro):
        sent = updates_here[m].astype(BF16)
        updates = [updates_here[m]] + [
            lax.ppermute(
                sent, "pipe", [(i, (i + step) % sections) for i in range(sections)]
            ).astype(F32)
            for step in range(1, sections)
        ]
        state = entering[0, :, m]
        kept = state
        for s in range(sections):
            add = updates[0]
            for step in range(1, sections):
                add = jnp.where((section - step) % sections == s, updates[step], add)
            state = (state.astype(F32) + add).astype(BF16)
            kept = jnp.where(section == s, state, kept)
        leaving.append(kept)
        final = state.astype(F32)
        upstream = entering[1, :, m].astype(F32) * gains[:, None, :]
        sums = jnp.stack(
            [jnp.sum(final * final, axis=(0, 2)), jnp.sum(upstream * final, axis=(0, 2))]
        ).reshape(2, outers, own_rows)
        total = sums
        for step in range(1, outers):
            total = total + jnp.roll(to_outer(sums, step), step, axis=1)
        total = total.reshape(2, rows) / features
        scale = lax.rsqrt(total[0] + 1e-05)
        shrink = scale * scale * total[1]
        grads.append(
            (scale[None, :, None] * (upstream - final * shrink[None, :, None])).astype(BF16)
        )

    full = [
        jnp.concatenate(
            [grads[m]] + [to_block(grads[m], step) for step in range(1, blocks)], axis=1
        )
        for m in range(micro)
    ]
    order = [[(t - step) % blocks for step in range(blocks)]] * micro

    outs = []
    for m in range(micro):
        by_group = after(leaving[m], grads[m]).reshape(2, outers, own_rows, width)
        row = jnp.zeros((own_rows, features), BF16)
        for step in range(outers):
            at = (outer + step) % outers
            piece = by_group[:, step]
            if step:
                piece = after(to_outer(piece, outers - step), full[-1])
            for slot in range(2):
                place = (2 * at + (core if slot == 0 else 1 - core)) * width
                row = lax.dynamic_update_slice_in_dim(row, piece[slot], place, 1)
        outs.append(row)
    section_out = jnp.stack(outs).reshape(1, micro, 1, own_rows, features)

    mix_rows = [
        jnp.concatenate(
            [pick(taken[m].reshape(blocks, rows, head_cols), at) for at in order[m]], axis=0
        )
        for m in range(micro)
    ]
    permuted_rows = [
        jnp.concatenate(
            [
                columns(half, m * tokens + at * own_rows, own_rows)
                for at in order[m]
                for half in permuted
            ],
            axis=1,
        )
        for m in range(micro)
    ]

    holder = (t * per_block) // 2
    mix_grads = []
    right_sum = 0.0
    left_sum = 0.0
    for m in range(micro):
        if per_block == 1:
            cols = pick(full[m], jnp.where(t % 2 == core, 0, 1))
        else:
            cols = jnp.concatenate(list(of_cores(full[m])), axis=1)
        left_sum = left_sum + dot(permuted_rows[m], cols, 1, 0)

        inner_grads = [
            dot(full[m][slot], left_slots[slot], 1, 1).astype(BF16) for slot in range(2)
        ]
        if per_block == 1:
            mine = jnp.concatenate(inner_grads, axis=1)
            right_here = jnp.concatenate(right_slots, axis=1)
        else:
            mine = (inner_grads[0].astype(F32) + inner_grads[1].astype(F32)).astype(BF16)
            right_here = right_slots[0]
        right_sum = right_sum + dot(mine, mix_rows[m], 0, 0)

        partial_mix = (
            dot(full[m][0], weights[0], 1, 1)
            + dot(full[m][1], weights[1], 1, 1)
            + dot(mine, right_here, 1, 1)
        ).reshape(blocks, outers, own_rows, head_cols)
        whole = partial_mix[:, 0]
        for step in range(1, outers):
            whole = whole + to_outer(partial_mix[:, step].astype(BF16), outers - step).astype(F32)
        whole = whole.astype(BF16)
        back = order[m]
        mix_grads.append(
            jnp.concatenate([pick(whole, at) for at in back], axis=0)
        )
    grad_mix = jnp.stack(mix_grads).reshape(1, micro, 1, tokens, head_cols)

    half = block_cols // 2
    half_sum = (
        columns(left_sum, core * half, half) + to_core(columns(left_sum, (1 - core) * half, half))
    ).astype(BF16)
    best = half_sum
    for step in range(1, outers):
        pairs = []
        for i in range(blocks):
            at = (i * per_block) // 2
            for c in range(2):
                pairs.append(
                    (i * parts + 2 * at + c, i * parts + 2 * ((at + step) % outers) + c)
                )
        arrived = lax.ppermute(half_sum, ("tensor", "dp"), pairs)
        best = jnp.where((outer - holder) % outers == step, arrived, best)
    there = to_core(best)
    grad_left = jnp.concatenate(list(of_cores(jnp.stack([best, there]))), axis=1).astype(F32)

    if per_block == 1:
        right_sum = of_cores(right_sum.reshape(2, sub, head_cols)).reshape(2 * sub, head_cols)
    right_sum = (right_sum + to_core(right_sum)).astype(BF16)
    wide = jnp.zeros((rank, head_cols), BF16)
    count = right_sum.shape[0]
    for step in range(outers):
        arrived = to_outer(right_sum, step) if step else right_sum
        wide = lax.dynamic_update_slice_in_dim(
            wide, arrived, ((outer - step) % outers) * count, 0
        )
    grad_right = wide.T.astype(F32)

    return (
        section_out,
        grad_mix,
        grad_right.reshape(1, 1, head_cols, rank),
        grad_left.reshape(1, 1, rank, block_cols),
    )


def solution(mesh):
    sizes = (mesh.shape["tensor"], mesh.shape["dp"], mesh.shape["pipe"])
    return jax.shard_map(
        on_device if sizes == (4, 4, 2) else on_device_general,
        mesh=mesh,
        in_specs=(
            P("pipe", None, "dp", None, "tensor"),
            P(None, "dp", "tensor", None),
            P(None, "dp", "tensor", None),
            P("pipe", "tensor", "dp"),
            P("pipe", "tensor", None, None),
            P("pipe", "tensor", None, None),
            P(),
        ),
        out_specs=(
            P("pipe", None, "dp", "tensor", None),
            P("pipe", None, "dp", None, "tensor"),
            P("pipe", "tensor", None, None),
            P("pipe", "tensor", None, None),
        ),
        check_vma=False,
    )
```
